32 devices in a mesh: groups: 2 (over y), serve: 4 (over z), tensor: 4 (over x, core).
Axes of the slice: x: 2, y: 2, z: 4, core: 2. Of those that a mesh axis runs over, the one named last changes fastest.
Arguments:
- tokens: bfloat16 [12288, 4096], P(('groups', 'serve'), 'tensor'), parts along dimension 0, as said below
- norm_gain: bfloat16 [4096], P('tensor'), may hold values from 0.099609375 to 1.8984375
- kv_weight: bfloat16 [4096, 2048], P('tensor'), may hold values from -0.09375 to 0.09375
- live_blocks: int32 [8], P('groups'), parts along dimension 0, may hold values from 1 to 24, 48 in all
- span_offset: int32 [8], P('groups'), parts along dimension 0, may hold values from 0 to 2
Outputs:
- kv_cache: bfloat16 [12288, 2048], P(('groups', 'serve'), 'tensor'), parts along dimension 0
The draws below stay inside these ranges and needn't reach their ends.
There are 2 independent parts, one for each index of `groups`. The reference program is written for one: setup_inputs(seed, part) draws one part's arguments, and reference() takes and returns one part's arrays. A program takes and returns all parts, laid end to end along the dimension named above; an argument that names none is the same for every part. Nothing has to cross between parts.
Inputs may be any that keep to these rules, and one draw needn't show every extreme that they name: `live_blocks`: the 4 lengths sum to exactly 48 row blocks; the longest is exactly 24. `span_offset`: every position stays below 2048. `tokens`: finite hidden states.
All inputs are finite; a program needn't handle non-finite values.
Results may differ from the reference program's by a relative error of at most 0.012.
Values may be sent and summed in bfloat16 or wider, within the bound.
No kernel may reach another device: no remote copies, remote signals or barrier semaphores. Data moves between devices by JAX's collectives and lax.ppermute only.
A program may use at most 64 MiB of HBM per device.

```python
import math
import jax
import jax.numpy as jnp
import numpy as np
from jax import lax

D = 4096
HD = 128
PAGE = 256
SESSION = 2048
BLOCK = 64
UNITS = 24
HELP = 12
OWNERS = 4
KVCOLS = 2048
N_TENSOR = 4


def draw_tokens(key, part):
    key = jax.random.fold_in(key, 11)
    row_key, column_key, value_key = jax.random.split(key, 3)
    rows_all = OWNERS * UNITS * BLOCK
    values = jnp.clip(jax.random.normal(value_key, (rows_all, D), jnp.float32), -4.0, 4.0)
    row_scale = jnp.exp(jax.random.uniform(row_key, (rows_all, 1), jnp.float32, 0.0, math.log(10.0)))
    rising = jnp.exp(math.log(3.0) * jnp.arange(D, dtype=jnp.float32) / D)[None, :]
    column_scale = rising * jnp.exp(jax.random.uniform(column_key, (1, D), jnp.float32, -0.35, 0.35))
    return (values * row_scale * column_scale).astype(jnp.bfloat16)


def touch_ends(result, key, smallest, high):
    longest = result.shape.index(max(result.shape))
    spots = []
    for shift in (0, 1):
        where = [jax.random.randint(jax.random.fold_in(key, axis), (), 0, length) for axis, length in enumerate(result.shape)]
        where[longest] = (where[longest] + shift) % result.shape[longest]
        spots.append(tuple(where))
    return result.at[spots[0]].set(smallest).at[spots[1]].set(high)


def shard_levels(stream_key, extent, cuts, smallest, top_value):
    level = 1.0
    for dim, shards_of in cuts:
        heights = jax.random.uniform(jax.random.fold_in(jax.random.fold_in(stream_key, 6), dim), (shards_of,), jnp.float32, smallest / len(cuts), top_value / len(cuts))
        level = level * jnp.repeat(jnp.exp(heights), extent[dim] // shards_of).reshape((-1,) + (1,) * (len(extent) - 1 - dim))
    return level


def profile(count, total, reach, skew):
    portions = [(1 << 20) // math.isqrt(rank ** skew) + 1 for rank in range(2, count + 1)]
    surplus, given = total - reach - (count - 1), [1] * (count - 1)
    while surplus > 0:
        candidates = [i for i in range(count - 1) if given[i] < reach]
        mass, budget = sum([portions[i] for i in candidates]), surplus
        for i in candidates:
            addition = min(reach - given[i], max(1, budget * portions[i] // mass), surplus)
            given[i] = given[i] + addition
            surplus = surplus - addition
    return np.array([reach] + given)


def ragged(stream_key, amount, total, limit, slope):
    if amount == 2:
        one = jax.random.randint(stream_key, (), max(1, total - limit), min(limit, total - 1) + 1)
        return jnp.stack([one, total - one])
    tallies = jnp.asarray(profile(amount, total, limit, slope), jnp.int32)
    pairs = (amount - 1) // 2
    donor, sink = tallies[1:1 + 2 * pairs:2], tallies[2:2 + 2 * pairs:2]
    slack = jnp.minimum(donor - 1, limit - sink)
    moved = jax.random.randint(jax.random.fold_in(stream_key, 1), (pairs,), 0, 1 << 20) % (slack + 1)
    tallies = tallies.at[1:1 + 2 * pairs:2].set(donor - moved).at[2:2 + 2 * pairs:2].set(sink + moved)
    return tallies[jax.random.permutation(jax.random.fold_in(stream_key, 2), amount)]


def noise(own_key, dims, spread, reach, cuts=(), kind=jnp.bfloat16):
    drawn = spread * jax.random.normal(own_key, dims, jnp.float32)
    if cuts:
        drawn = drawn * shard_levels(own_key, dims, cuts, -0.22, 0.18)
    return jnp.clip(drawn, -reach, reach).astype(kind)


def setup_inputs(seed: int = 0, part: int = 0) -> dict:
    seeds = jax.random.split(jax.random.key(seed), 6)
    part_splits = jax.random.split(jax.random.fold_in(seeds[5], part), 6)
    tokens = draw_tokens(jax.random.fold_in(jax.random.fold_in(seeds[5], part), 71), part)
    norm_gain = jnp.clip(1.0 + 0.18 * jax.random.normal(seeds[1], (D,), jnp.float32), 0.099609375, 1.8984375).astype(jnp.bfloat16)
    kv_weight = noise(seeds[2], (D, KVCOLS), D ** -0.5, 0.09375, ((0, 4),))
    live_blocks = ragged(part_splits[3], OWNERS, HELP * OWNERS, UNITS, 2).astype(jnp.int32)
    span_offset = touch_ends(jax.random.randint(part_splits[4], (OWNERS,), 0, SESSION // PAGE - (UNITS * BLOCK + PAGE - 1) // PAGE + 1), jax.random.fold_in(part_splits[4], 1), 0, (SESSION // PAGE - (UNITS * BLOCK + PAGE - 1) // PAGE + 1) - 1).astype(jnp.int32)
    return dict(tokens=tokens, norm_gain=norm_gain, kv_weight=kv_weight, live_blocks=live_blocks, span_offset=span_offset)


rope_base = 500000.0
norm_eps = 1e-05

def rotate_pairs(values, positions):
    half_dim = values.shape[-1] // 2
    inv_freq = rope_base ** (-(jnp.arange(half_dim, dtype=jnp.float32) * 2.0) / values.shape[-1])
    angles = positions.astype(jnp.float32)[:, None] * inv_freq[None, :]
    cosine = jnp.cos(angles)[:, None, :]
    sine_part = jnp.sin(angles)[:, None, :]
    key_part = values[:, :, 0, :]
    first_half = key_part[..., :half_dim]
    second = key_part[..., half_dim:]
    rotated = jnp.concatenate([first_half * cosine - second * sine_part, second * cosine + first_half * sine_part], axis=-1)
    return jnp.stack([rotated, values[:, :, 1, :]], axis=2)

def reference(tokens, norm_gain, kv_weight, live_blocks, span_offset):
    owner_count = live_blocks.shape[0]
    slot_rows = tokens.shape[0] // owner_count
    column_count = kv_weight.shape[1]
    feature_part = D // N_TENSOR
    live_blocks = live_blocks.astype(jnp.int32)
    starts = (jnp.cumsum(live_blocks) - live_blocks).astype(jnp.int32)
    block_ends = (starts + live_blocks).astype(jnp.int32)
    global_ids = jnp.arange(HELP * owner_count, dtype=jnp.int32)
    owner_ids = lax.optimization_barrier(jnp.sum((block_ends[None, :] <= global_ids[:, None]).astype(jnp.int32), axis=1)).astype(jnp.int32)
    block_ids = (global_ids - starts[owner_ids]).astype(jnp.int32)
    inner = jnp.arange(BLOCK, dtype=jnp.int32)
    row_index = ((owner_ids * slot_rows + block_ids * BLOCK)[:, None] + inner[None, :]).astype(jnp.int32)
    positions = ((span_offset.astype(jnp.int32)[owner_ids] * PAGE + block_ids * BLOCK)[:, None] + inner[None, :]).astype(jnp.int32)
    gain_wide = norm_gain.astype(jnp.float32)

    def one_group(operands):
        group_rows, group_positions = operands
        row_block = tokens[group_rows]
        wide_rows = row_block.astype(jnp.float32)
        squares = lax.optimization_barrier(jnp.sum(wide_rows * wide_rows, axis=1))
        inv_rms = 1.0 / jnp.sqrt(squares / D + norm_eps)
        scaled = (wide_rows * gain_wide[None, :]).astype(jnp.bfloat16)
        summed = jnp.zeros((row_block.shape[0], column_count), jnp.float32)
        for part_index in range(N_TENSOR):
            lower = part_index * feature_part
            partial_value = jnp.dot(scaled[:, lower:lower + feature_part], kv_weight[lower:lower + feature_part], preferred_element_type=jnp.float32)
            partial_value = lax.optimization_barrier(partial_value.astype(jnp.bfloat16))
            summed = summed + partial_value.astype(jnp.float32)
        values = (summed * inv_rms[:, None]).reshape(row_block.shape[0], column_count // (2 * HD), 2, HD)
        return rotate_pairs(values, group_positions).reshape(row_block.shape[0], column_count).astype(jnp.bfloat16)
    results = lax.map(one_group, (row_index.reshape(owner_count, HELP * BLOCK), positions.reshape(owner_count, HELP * BLOCK)))
    kv_cache = jnp.zeros((tokens.shape[0], column_count), jnp.bfloat16)
    return kv_cache.at[row_index.reshape(-1)].set(results.reshape(-1, column_count))
```

```python
import functools

import jax
import jax.numpy as jnp
from jax import lax
from jax.experimental import pallas as pl
from jax.experimental.pallas import tpu as pltpu
from jax.sharding import PartitionSpec as P

HD = 128
PAGE = 256
BLOCK = 64
LANES = 128

rope_base = 500000.0
norm_eps = 1e-05

TILE = 128
CHUNKS = (1, 2, 3, 3, 2, 1)
PIECES = (3, 9)


def scaled_rows(rows_ref, gain_ref):
    wide = rows_ref[...].astype(jnp.float32) * gain_ref[...].astype(jnp.float32)
    return wide.astype(jnp.bfloat16)


def pair_product(near_ref, far_ref, near_gain, far_gain, near_weight, far_weight):
    total = jnp.dot(
        scaled_rows(near_ref, near_gain), near_weight[...], preferred_element_type=jnp.float32
    )
    return total + jnp.dot(
        scaled_rows(far_ref, far_gain), far_weight[...], preferred_element_type=jnp.float32
    )


def partial_kernel(place, near, far, near_gain, far_gain, near_weight, far_weight, out):
    out[...] = pair_product(near, far, near_gain, far_gain, near_weight, far_weight).astype(out.dtype)


def squares_kernel(rows_ref, out):
    total = jnp.zeros((LANES, LANES), jnp.float32)
    for part in range(rows_ref.shape[1] // LANES):
        wide = rows_ref[:, part * LANES : (part + 1) * LANES].astype(jnp.float32)
        total += wide * wide
    out[0] = jnp.sum(jnp.transpose(total), axis=0, keepdims=True)


def finish_kernel(first_tile, model_dim, place, live, *refs):
    (near, far, near_gain, far_gain, near_weight, far_weight, squares, cosine, sine) = refs[:9]
    arrived, out = refs[9:-2], refs[-1]
    values = pair_product(near, far, near_gain, far_gain, near_weight, far_weight)
    for part in arrived:
        values += part[...].astype(jnp.float32)
    square_row = jnp.sum(squares[...], axis=0)
    on_diagonal = lax.broadcasted_iota(jnp.int32, (TILE, TILE), 0) == lax.broadcasted_iota(
        jnp.int32, (TILE, TILE), 1
    )
    totals = jnp.sum(jnp.where(on_diagonal, square_row, 0.0), axis=1, keepdims=True)
    scales = 1.0 / jnp.sqrt(totals / model_dim + norm_eps)
    row = (first_tile + pl.program_id(0)) * TILE + lax.broadcasted_iota(jnp.int32, (TILE, 1), 0)
    alive = row < live[place[2]] * BLOCK
    for start in range(0, out.shape[1], 2 * HD):
        key = values[:, start : start + HD] * scales
        turned = key * cosine[...] + pltpu.roll(key, HD // 2, 1) * sine[...]
        out[:, start : start + HD] = jnp.where(alive, turned, 0.0).astype(out.dtype)
        value = values[:, start + HD : start + 2 * HD] * scales
        out[:, start + HD : start + 2 * HD] = jnp.where(alive, value, 0.0).astype(out.dtype)


def shards(tokens, norm_gain, kv_weight, live_blocks, span_offset):
    tensor_count = lax.axis_size("tensor")
    chip_count = tensor_count // 2
    me = lax.axis_index("tensor")
    own_index = lax.axis_index("serve")
    slot_rows, depth = tokens.shape
    columns = kv_weight.shape[1] // tensor_count
    tiles = slot_rows // TILE
    model_dim = depth * tensor_count

    swap = [(i, i ^ 1) for i in range(tensor_count)]

    def shift(step):
        return [(i, (i + 2 * step) % tensor_count) for i in range(tensor_count)]

    def block_of(step):
        return (me + 2 * step) % tensor_count

    far_gain = lax.ppermute(norm_gain, "tensor", swap)
    far_weight = [None] * chip_count
    far_tokens = []
    for step in list(range(1, chip_count)) + [0]:
        sent = lax.dynamic_slice_in_dim(kv_weight, (block_of(step) ^ 1) * columns, columns, axis=1)
        far_weight[step] = lax.ppermute(sent, "tensor", swap)
    tile_at = 0
    for piece in PIECES:
        sent = tokens[tile_at * TILE : (tile_at + piece) * TILE]
        far_tokens.append((tile_at, lax.ppermute(sent, "tensor", swap)))
        tile_at += piece

    near_gain = norm_gain.reshape(1, depth)
    far_gain = far_gain.reshape(1, depth)

    own_squares = pl.pallas_call(
        squares_kernel,
        grid=(tiles,),
        in_specs=[pl.BlockSpec((TILE, depth), lambda i: (i, 0))],
        out_specs=pl.BlockSpec((1, 1, TILE), lambda i: (i, 0, 0)),
        out_shape=jax.ShapeDtypeStruct((tiles, 1, TILE), jnp.float32),
    )(tokens)
    flat = own_squares.reshape(tiles, TILE)
    pair_squares = flat + lax.ppermute(flat, "tensor", swap)
    squares = jnp.stack(
        [pair_squares] + [lax.ppermute(pair_squares, "tensor", shift(s)) for s in range(1, chip_count)]
    ).reshape(chip_count, tiles, 1, TILE)

    half = HD // 2
    inv_freq = rope_base ** (-(jnp.arange(half, dtype=jnp.float32) * 2.0) / HD)
    positions = span_offset[own_index] * PAGE + jnp.arange(slot_rows, dtype=jnp.int32)
    angles = positions.astype(jnp.float32)[:, None] * inv_freq[None, :]
    cosine, sine = jnp.cos(angles), jnp.sin(angles)
    cosine = jnp.concatenate([cosine, cosine], axis=1)
    sine = jnp.concatenate([-sine, sine], axis=1)

    def piece_at(tile):
        found = [p for p in far_tokens if p[0] <= tile]
        return found[-1]

    def operand_specs(first, piece_first):
        return [
            pl.BlockSpec((TILE, depth), lambda i, *_: (first + i, 0)),
            pl.BlockSpec((TILE, depth), lambda i, *_: (first - piece_first + i, 0)),
            pl.BlockSpec((1, depth), lambda i, *_: (0, 0)),
            pl.BlockSpec((1, depth), lambda i, *_: (0, 0)),
        ]

    def weight_specs(slot):
        return [
            pl.BlockSpec((depth, columns), lambda i, place, *_: (0, place[slot])),
            pl.BlockSpec((depth, columns), lambda i, *_: (0, 0)),
        ]

    params = pltpu.CompilerParams(vmem_limit_bytes=32 * 1024 * 1024)

    def product_cost(rows):
        return pl.CostEstimate(
            flops=4 * rows * depth * columns,
            bytes_accessed=4 * rows * depth + 4 * depth * columns + 2 * rows * columns,
            transcendentals=0,
        )

    def make_partial(first, count, step):
        piece_first, piece_rows = piece_at(first)
        place = jnp.stack([block_of(step), block_of(0), own_index]).astype(jnp.int32)
        return pl.pallas_call(
            partial_kernel,
            grid_spec=pltpu.PrefetchScalarGridSpec(
                num_scalar_prefetch=1,
                grid=(count,),
                in_specs=operand_specs(first, piece_first) + weight_specs(0),
                out_specs=pl.BlockSpec((TILE, columns), lambda i, *_: (i, 0)),
            ),
            out_shape=jax.ShapeDtypeStruct((count * TILE, columns), jnp.bfloat16),
            compiler_params=params,
            cost_estimate=product_cost(count * TILE),
        )(place, tokens, piece_rows, near_gain, far_gain, kv_weight, far_weight[step])

    def finish(first, count, arrived, result):
        piece_first, piece_rows = piece_at(first)
        place = jnp.stack([block_of(1), block_of(0), own_index]).astype(jnp.int32)
        operands = [tokens, piece_rows, near_gain, far_gain, kv_weight, far_weight[0], squares, cosine, sine]
        specs = (
            operand_specs(first, piece_first)
            + weight_specs(1)
            + [pl.BlockSpec((chip_count, None, 1, TILE), lambda i, *_: (0, first + i, 0, 0))]
            + [pl.BlockSpec((TILE, HD), lambda i, *_: (first + i, 0))] * 2
            + [pl.BlockSpec((TILE, columns), lambda i, *_: (i, 0))] * len(arrived)
        )
        operands += arrived
        if result is None:
            result = jnp.zeros((8, LANES), jnp.bfloat16)
            aliases = {}
        else:
            aliases = {2 + len(operands): 0}
        return pl.pallas_call(
            functools.partial(finish_kernel, first, model_dim),
            grid_spec=pltpu.PrefetchScalarGridSpec(
                num_scalar_prefetch=2,
                grid=(count,),
                in_specs=specs + [pl.BlockSpec(memory_space=pl.ANY)],
                out_specs=pl.BlockSpec((TILE, columns), lambda i, *_: (first + i, 0)),
            ),
            out_shape=jax.ShapeDtypeStruct((slot_rows, columns), jnp.bfloat16),
            input_output_aliases=aliases,
            compiler_params=params,
            cost_estimate=product_cost(count * TILE),
        )(place, live_blocks, *operands, result)

    arrivals = []
    first = 0
    for count in CHUNKS:
        arrived = []
        for step in range(1, chip_count):
            sent = make_partial(first, count, step)
            arrived.append(lax.ppermute(sent, "tensor", shift(step)))
        arrivals.append((first, count, arrived))
        first += count

    result = None
    for first, count, arrived in arrivals:
        result = finish(first, count, arrived, result)
    return result


def solution(mesh):
    in_specs = (
        P(("groups", "serve"), "tensor"),
        P("tensor"),
        P("tensor", None),
        P("groups"),
        P("groups"),
    )
    out_specs = P(("groups", "serve"), "tensor")
    return jax.shard_map(shards, mesh=mesh, in_specs=in_specs, out_specs=out_specs, check_vma=False)
```

```python
import functools

import jax
import jax.numpy as jnp
from jax import lax
from jax.experimental import pallas as pl
from jax.experimental.pallas import tpu as pltpu
from jax.sharding import PartitionSpec as P

HD = 128
PAGE = 256
BLOCK = 64
LANES = 128

rope_base = 500000.0
norm_eps = 1e-05

TILE = 256
CHUNKS = (1, 2, 2, 1)

PARAMS = pltpu.CompilerParams(vmem_limit_bytes=24 * 1024 * 1024)


def square_sums(rows):
    total = jnp.zeros((rows.shape[0], LANES), jnp.float32)
    for part in range(rows.shape[1] // LANES):
        wide = rows[:, part * LANES : (part + 1) * LANES].astype(jnp.float32)
        total += wide * wide
    return total


def product_kernel(with_squares, place, rows_ref, gain_ref, keep_weight, send_weight, keep, send, *squares):
    scaled = rows_ref[...] * gain_ref[...]
    send[...] = jnp.dot(scaled, send_weight[...], preferred_element_type=jnp.float32).astype(send.dtype)
    keep[...] = jnp.dot(scaled, keep_weight[...], preferred_element_type=jnp.float32).astype(keep.dtype)
    if with_squares:
        total = square_sums(rows_ref[...])
        for part in range(TILE // LANES):
            turned = jnp.transpose(total[part * LANES : (part + 1) * LANES])
            squares[0][part] = jnp.sum(turned, axis=0, keepdims=True)


def finish_kernel(first_tile, model_dim, place, live, *refs):
    keep, received, squares, far_cos, far_sin, near_cos, near_sin = refs[:7]
    arrived, out = refs[7:-2], refs[-1]
    values = keep[...].astype(jnp.float32) + received[...].astype(jnp.float32)
    for part in arrived:
        values += part[...].astype(jnp.float32)
    on_diagonal = lax.broadcasted_iota(jnp.int32, (LANES, LANES), 0) == lax.broadcasted_iota(
        jnp.int32, (LANES, LANES), 1
    )
    square_rows = jnp.sum(squares[...], axis=0)
    totals = jnp.concatenate(
        [
            jnp.sum(jnp.where(on_diagonal, square_rows[part], 0.0), axis=1, keepdims=True)
            for part in range(TILE // LANES)
        ],
        axis=0,
    )
    scales = 1.0 / jnp.sqrt(totals / model_dim + norm_eps)
    tile = first_tile + pl.program_id(0)
    row = tile * TILE + lax.broadcasted_iota(jnp.int32, (TILE, 1), 0)
    alive = row < live[place[2]] * BLOCK
    sign = jnp.where(lax.broadcasted_iota(jnp.int32, (1, HD), 1) < HD // 2, -1.0, 1.0)
    cosines, sines = [], []
    for part in range(TILE // BLOCK):
        block_cos = far_cos[part]
        block_sin = far_sin[part]
        cosines.append(block_cos * near_cos[...] - block_sin * near_sin[...])
        sines.append((sign * block_sin) * near_cos[...] + (sign * block_cos) * near_sin[...])
    cosine = jnp.concatenate(cosines, axis=0)
    sine = jnp.concatenate(sines, axis=0)
    for start in range(0, out.shape[1], 2 * HD):
        key = values[:, start : start + HD] * scales
        turned = key * cosine + pltpu.roll(key, HD // 2, 1) * sine
        out[:, start : start + HD] = jnp.where(alive, turned, 0.0).astype(out.dtype)
        value = values[:, start + HD : start + 2 * HD] * scales
        out[:, start + HD : start + 2 * HD] = jnp.where(alive, value, 0.0).astype(out.dtype)


def shards(tokens, norm_gain, kv_weight, live_blocks, span_offset):
    tensor_count = lax.axis_size("tensor")
    chip_count = tensor_count // 2
    me = lax.axis_index("tensor")
    own_index = lax.axis_index("serve")
    slot_rows, depth = tokens.shape
    columns = kv_weight.shape[1] // tensor_count
    tiles = slot_rows // TILE
    model_dim = depth * tensor_count
    gain = norm_gain.reshape(1, depth)

    swap = [(i, i ^ 1) for i in range(tensor_count)]

    def shift(step):
        return [(i, (i + 2 * step) % tensor_count) for i in range(tensor_count)]

    def place_of(step):
        keep = (me + 2 * step) % tensor_count
        return jnp.stack([keep, keep ^ 1, own_index]).astype(jnp.int32)

    def product(place, first, count, with_squares):
        rows = count * TILE
        groups = TILE // LANES
        out_shape = [jax.ShapeDtypeStruct((rows, columns), jnp.bfloat16)] * 2
        out_specs = [pl.BlockSpec((TILE, columns), lambda i, *_: (i, 0))] * 2
        if with_squares:
            out_shape.append(jax.ShapeDtypeStruct((rows // LANES, 1, LANES), jnp.float32))
            out_specs.append(pl.BlockSpec((groups, 1, LANES), lambda i, *_: (i, 0, 0)))
        return pl.pallas_call(
            functools.partial(product_kernel, with_squares),
            grid_spec=pltpu.PrefetchScalarGridSpec(
                num_scalar_prefetch=1,
                grid=(count,),
                in_specs=[
                    pl.BlockSpec((TILE, depth), lambda i, *_: (first + i, 0)),
                    pl.BlockSpec((1, depth), lambda i, *_: (0, 0)),
                    pl.BlockSpec((depth, columns), lambda i, where: (0, where[0])),
                    pl.BlockSpec((depth, columns), lambda i, where: (0, where[1])),
                ],
                out_specs=out_specs,
            ),
            out_shape=out_shape,
            compiler_params=PARAMS,
            cost_estimate=pl.CostEstimate(
                flops=4 * rows * depth * columns,
                bytes_accessed=2 * rows * depth + 4 * depth * columns + 4 * rows * columns,
                transcendentals=0,
            ),
        )(place, tokens, gain, kv_weight, kv_weight)

    def tables(offset):
        half = HD // 2
        inv_freq = rope_base ** (-(jnp.arange(half, dtype=jnp.float32) * 2.0) / HD)
        inv_freq = jnp.concatenate([inv_freq, inv_freq])
        starts = offset * PAGE + BLOCK * jnp.arange(slot_rows // BLOCK, dtype=jnp.int32)
        far = starts.astype(jnp.float32)[:, None, None] * inv_freq
        near = jnp.arange(BLOCK, dtype=jnp.float32)[:, None] * inv_freq
        return [jnp.cos(far), jnp.sin(far), jnp.cos(near), jnp.sin(near)]

    def finish(first, count, keep, received, squares, table, arrived, result):
        blocks = TILE // BLOCK
        operands = [keep, received, squares] + table + arrived
        specs = (
            [pl.BlockSpec((TILE, columns), lambda i, *_: (first + i, 0))] * 2
            + [pl.BlockSpec((chip_count, TILE // LANES, 1, LANES), lambda i, *_: (0, first + i, 0, 0))]
            + [pl.BlockSpec((blocks, 1, HD), lambda i, *_: (first + i, 0, 0))] * 2
            + [pl.BlockSpec((BLOCK, HD), lambda i, *_: (0, 0))] * 2
            + [pl.BlockSpec((TILE, columns), lambda i, *_: (i, 0))] * len(arrived)
        )
        if result is None:
            result = keep
            aliases = {}
        else:
            aliases = {2 + len(operands): 0}
        return pl.pallas_call(
            functools.partial(finish_kernel, first, model_dim),
            grid_spec=pltpu.PrefetchScalarGridSpec(
                num_scalar_prefetch=2,
                grid=(count,),
                in_specs=specs + [pl.BlockSpec(memory_space=pl.ANY)],
                out_specs=pl.BlockSpec((TILE, columns), lambda i, *_: (first + i, 0)),
            ),
            out_shape=jax.ShapeDtypeStruct((slot_rows, columns), jnp.bfloat16),
            input_output_aliases=aliases,
            compiler_params=PARAMS,
            cost_estimate=pl.CostEstimate(
                flops=20 * count * TILE * columns, bytes_accessed=8 * count * TILE * columns, transcendentals=0
            ),
        )(place_of(0), live_blocks, *operands, result)

    others = range(1, chip_count)
    firsts = [sum(CHUNKS[:index]) for index in range(len(CHUNKS))]
    places = {step: place_of(step) for step in range(chip_count)}
    offset = span_offset[own_index]

    def start_chunk(index):
        made, sums = [], None
        for step in others:
            result = product(places[step], firsts[index], CHUNKS[index], step == 1)
            if step == 1:
                sums = result[2]
            made.append((result[0], lax.ppermute(result[1], "tensor", swap)))
        return made, sums

    def cross(made):
        sums = [
            (keep.astype(jnp.float32) + got.astype(jnp.float32)).astype(jnp.bfloat16) for keep, got in made
        ]
        sums, held = lax.optimization_barrier((sums, (places, offset)))
        return [lax.ppermute(part, "tensor", shift(step)) for step, part in zip(others, sums)], held

    chunk_count = len(CHUNKS)
    arrivals, square_parts = [], []
    pending = []
    for index in range(chunk_count):
        made, sums = start_chunk(index)
        square_parts.append(sums)
        pending.append(made)
        if len(pending) > 1:
            arrived, (places, offset) = cross(pending.pop(0))
            arrivals.append(arrived)
    keep, send = product(places[0], 0, tiles, False)
    received = lax.ppermute(send, "tensor", swap)
    arrived, (places, offset) = cross(pending.pop(0))
    arrivals.append(arrived)

    flat = jnp.concatenate(square_parts, axis=0).reshape(slot_rows // LANES, LANES)
    pair_squares = flat + lax.ppermute(flat, "tensor", swap)
    squares = jnp.stack(
        [pair_squares] + [lax.ppermute(pair_squares, "tensor", shift(step)) for step in others]
    ).reshape(chip_count, slot_rows // LANES, 1, LANES)
    table = tables(offset)

    result = None
    for first, count, arrived in zip(firsts, CHUNKS, arrivals):
        result = finish(first, count, keep, received, squares, table, arrived, result)
    return result


def solution(mesh):
    in_specs = (
        P(("groups", "serve"), "tensor"),
        P("tensor"),
        P("tensor", None),
        P("groups"),
        P("groups"),
    )
    out_specs = P(("groups", "serve"), "tensor")
    return jax.shard_map(shards, mesh=mesh, in_specs=in_specs, out_specs=out_specs, check_vma=False)
```

```python
import functools

import jax
import jax.numpy as jnp
from jax import lax
from jax.experimental import pallas as pl
from jax.experimental.pallas import tpu as pltpu
from jax.sharding import PartitionSpec as P

HD = 128
PAGE = 256
BLOCK = 64
LANES = 128

rope_base = 500000.0
norm_eps = 1e-05

TILE = 256
CHUNKS = (1, 2, 2, 1)

WIDE = pltpu.CompilerParams(vmem_limit_bytes=60 * 1024 * 1024)
PARAMS = pltpu.CompilerParams(vmem_limit_bytes=16 * 1024 * 1024)
COST = pl.CostEstimate(flops=1, bytes_accessed=1, transcendentals=0)


def square_sums(rows):
    total = jnp.zeros((rows.shape[0], LANES), jnp.float32)
    for part in range(rows.shape[1] // LANES):
        wide = rows[:, part * LANES : (part + 1) * LANES].astype(jnp.float32)
        total += wide * wide
    return total


def product_kernel(with_squares, place, rows_ref, gain_ref, keep_weight, send_weight, keep, send, *squares):
    scaled = rows_ref[...] * gain_ref[...].reshape(1, gain_ref.shape[0])
    send[...] = jnp.dot(scaled, send_weight[...], preferred_element_type=jnp.float32).astype(send.dtype)
    keep[...] = jnp.dot(scaled, keep_weight[...], preferred_element_type=jnp.float32).astype(keep.dtype)
    if with_squares:
        total = square_sums(rows_ref[...])
        for part in range(TILE // LANES):
            turned = jnp.transpose(total[part * LANES : (part + 1) * LANES])
            row = pl.program_id(0) * (TILE // LANES) + part
            squares[0][pl.ds(row, 1), :] = jnp.sum(turned, axis=0, keepdims=True)


def add_kernel(keep, received, out):
    out[...] = (keep[...].astype(jnp.float32) + received[...].astype(jnp.float32)).astype(out.dtype)


def finish_kernel(first_tile, chip_count, model_dim, place, live, *refs):
    keep, received, far_cos, far_sin, near_cos, near_sin = refs[:6]
    squares, arrived, out = refs[6 : 6 + chip_count], refs[6 + chip_count : -2], refs[-1]
    values = keep[...].astype(jnp.float32) + received[...].astype(jnp.float32)
    for part in arrived:
        values += part[...].astype(jnp.float32)
    on_diagonal = lax.broadcasted_iota(jnp.int32, (LANES, LANES), 0) == lax.broadcasted_iota(
        jnp.int32, (LANES, LANES), 1
    )
    tile = first_tile + pl.program_id(0)
    columns = []
    for part in range(TILE // LANES):
        row = pl.ds(tile * (TILE // LANES) + part, 1)
        totals = functools.reduce(jnp.add, [ref[row, :] for ref in squares])
        columns.append(jnp.sum(jnp.where(on_diagonal, totals, 0.0), axis=1, keepdims=True))
    scales = 1.0 / jnp.sqrt(jnp.concatenate(columns, axis=0) / model_dim + norm_eps)
    row = tile * TILE + lax.broadcasted_iota(jnp.int32, (TILE, 1), 0)
    alive = row < live[place[2]] * BLOCK
    sign = jnp.where(lax.broadcasted_iota(jnp.int32, (1, HD), 1) < HD // 2, -1.0, 1.0)
    cosines, sines = [], []
    for part in range(TILE // BLOCK):
        block_cos = far_cos[part]
        block_sin = far_sin[part]
        cosines.append(block_cos * near_cos[...] - block_sin * near_sin[...])
        sines.append((sign * block_sin) * near_cos[...] + (sign * block_cos) * near_sin[...])
    cosine = jnp.concatenate(cosines, axis=0)
    sine = jnp.concatenate(sines, axis=0)
    for start in range(0, out.shape[1], 2 * HD):
        key = values[:, start : start + HD] * scales
        turned = key * cosine + pltpu.roll(key, HD // 2, 1) * sine
        out[:, start : start + HD] = jnp.where(alive, turned, 0.0).astype(out.dtype)
        value = values[:, start + HD : start + 2 * HD] * scales
        out[:, start + HD : start + 2 * HD] = jnp.where(alive, value, 0.0).astype(out.dtype)


def shards(tokens, norm_gain, kv_weight, live_blocks, span_offset):
    tensor_count = lax.axis_size("tensor")
    chip_count = tensor_count // 2
    me = lax.axis_index("tensor")
    own_index = lax.axis_index("serve")
    slot_rows, depth = tokens.shape
    columns = kv_weight.shape[1] // tensor_count
    tiles = slot_rows // TILE
    model_dim = depth * tensor_count

    swap = [(i, i ^ 1) for i in range(tensor_count)]

    def shift(step):
        return [(i, (i + 2 * step) % tensor_count) for i in range(tensor_count)]

    def place_of(step):
        keep = (me + 2 * step) % tensor_count
        return jnp.stack([keep, keep ^ 1, own_index]).astype(jnp.int32)

    def product(place, first, count, with_squares):
        rows = count * TILE
        out_shape = [jax.ShapeDtypeStruct((rows, columns), jnp.bfloat16)] * 2
        out_specs = [pl.BlockSpec((TILE, columns), lambda i, *_: (i, 0))] * 2
        if with_squares:
            out_shape.append(jax.ShapeDtypeStruct((rows // LANES, LANES), jnp.float32))
            out_specs.append(pl.BlockSpec((rows // LANES, LANES), lambda i, *_: (0, 0)))
        return pl.pallas_call(
            functools.partial(product_kernel, with_squares),
            grid_spec=pltpu.PrefetchScalarGridSpec(
                num_scalar_prefetch=1,
                grid=(count,),
                in_specs=[
                    pl.BlockSpec((TILE, depth), lambda i, *_: (first + i, 0)),
                    pl.BlockSpec((depth,), lambda i, *_: (0,)),
                    pl.BlockSpec((depth, columns), lambda i, where: (0, where[0])),
                    pl.BlockSpec((depth, columns), lambda i, where: (0, where[1])),
                ],
                out_specs=out_specs,
            ),
            out_shape=out_shape,
            compiler_params=WIDE,
            cost_estimate=COST,
        )(place, tokens, norm_gain, kv_weight, kv_weight)

    def tables(offset):
        half = HD // 2
        inv_freq = rope_base ** (-(jnp.arange(half, dtype=jnp.float32) * 2.0) / HD)
        inv_freq = jnp.concatenate([inv_freq, inv_freq])
        starts = offset * PAGE + BLOCK * jnp.arange(slot_rows // BLOCK, dtype=jnp.int32)
        far = starts.astype(jnp.float32)[:, None, None] * inv_freq
        near = jnp.arange(BLOCK, dtype=jnp.float32)[:, None] * inv_freq
        return [jnp.cos(far), jnp.sin(far), jnp.cos(near), jnp.sin(near)]

    def finish(first, count, keep, received, table, squares, arrived, result):
        blocks = TILE // BLOCK
        operands = [keep, received] + table + squares + arrived
        specs = (
            [pl.BlockSpec((TILE, columns), lambda i, *_: (first + i, 0))] * 2
            + [pl.BlockSpec((blocks, 1, HD), lambda i, *_: (first + i, 0, 0))] * 2
            + [pl.BlockSpec((BLOCK, HD), lambda i, *_: (0, 0))] * 2
            + [pl.BlockSpec((slot_rows // LANES, LANES), lambda i, *_: (0, 0))] * chip_count
            + [pl.BlockSpec((TILE, columns), lambda i, *_: (i, 0))] * len(arrived)
        )
        if result is None:
            result = keep
            aliases = {}
        else:
            aliases = {2 + len(operands): 0}
        return pl.pallas_call(
            functools.partial(finish_kernel, first, chip_count, model_dim),
            grid_spec=pltpu.PrefetchScalarGridSpec(
                num_scalar_prefetch=2,
                grid=(count,),
                in_specs=specs + [pl.BlockSpec(memory_space=pl.ANY)],
                out_specs=pl.BlockSpec((TILE, columns), lambda i, *_: (first + i, 0)),
            ),
            out_shape=jax.ShapeDtypeStruct((slot_rows, columns), jnp.bfloat16),
            input_output_aliases=aliases,
            compiler_params=PARAMS,
            cost_estimate=COST,
        )(place_of(0), live_blocks, *operands, result)

    others = range(1, chip_count)
    firsts = [sum(CHUNKS[:index]) for index in range(len(CHUNKS))]
    chunk_count = len(CHUNKS)
    places = {step: place_of(step) for step in range(chip_count)}

    def start_chunk(index):
        return [product(places[step], firsts[index], CHUNKS[index], False) for step in others]

    def add_halves(made):
        return [
            pl.pallas_call(
                add_kernel,
                out_shape=jax.ShapeDtypeStruct(keep.shape, keep.dtype),
                compiler_params=PARAMS,
                cost_estimate=COST,
            )(keep, lax.ppermute(send, "tensor", swap))
            for keep, send in made
        ]

    def cross(sums):
        return [lax.ppermute(part, "tensor", shift(step)) for step, part in zip(others, sums)]

    def own_inputs(own, table):
        keep, send, own_squares = own
        received = lax.ppermute(send, "tensor", swap)
        pair_squares = own_squares + lax.ppermute(own_squares, "tensor", swap)
        squares = [pair_squares] + [lax.ppermute(pair_squares, "tensor", shift(step)) for step in others]
        return [keep, received, table, squares]

    hold = lax.optimization_barrier
    arrivals = []
    own, inputs, result, finished = None, None, None, 0
    made = start_chunk(0)
    made, places = hold((made, places))
    sums = add_halves(made)
    made = start_chunk(1)
    sums, made, places, span_offset = hold((sums, made, places, span_offset))
    for stage in range(1, chunk_count + 1):
        arrived = cross(sums)
        if stage < chunk_count:
            sums = add_halves(made)
        if stage + 1 < chunk_count:
            made = start_chunk(stage + 1)
        if stage == 2:
            own = product(places[0], 0, tiles, True), tables(span_offset[own_index])
        if stage == 3:
            inputs = own_inputs(*own)
        if stage >= 3:
            for index in range(finished, stage - 1):
                result = finish(firsts[index], CHUNKS[index], *inputs, arrivals[index], result)
            finished = stage - 1
        arrived, sums, made, places, span_offset, own, inputs, result = hold(
            (arrived, sums, made, places, span_offset, own, inputs, result)
        )
        arrivals.append(arrived)
    for index in range(finished, chunk_count):
        result = finish(firsts[index], CHUNKS[index], *inputs, arrivals[index], result)
    return result


def solution(mesh):
    in_specs = (
        P(("groups", "serve"), "tensor"),
        P("tensor"),
        P("tensor", None),
        P("groups"),
        P("groups"),
    )
    out_specs = P(("groups", "serve"), "tensor")
    return jax.shard_map(shards, mesh=mesh, in_specs=in_specs, out_specs=out_specs, check_vma=False)
```

```python
import functools

import jax
import jax.numpy as jnp
from jax import lax
from jax.experimental import pallas as pl
from jax.experimental.pallas import tpu as pltpu
from jax.sharding import PartitionSpec as P

HD = 128
PAGE = 256
BLOCK = 64
LANES = 128

rope_base = 500000.0
norm_eps = 1e-05

TILE = 256
CHUNKS = (1, 2, 2, 1)

WIDE = pltpu.CompilerParams(vmem_limit_bytes=60 * 1024 * 1024)
PARAMS = pltpu.CompilerParams(vmem_limit_bytes=16 * 1024 * 1024)
COST = pl.CostEstimate(flops=1, bytes_accessed=1, transcendentals=0)


def square_sums(rows):
    total = jnp.zeros((rows.shape[0], LANES), jnp.float32)
    for part in range(rows.shape[1] // LANES):
        wide = rows[:, part * LANES : (part + 1) * LANES].astype(jnp.float32)
        total += wide * wide
    return total


def product_kernel(step, chip_count, chunks, with_squares, tokens, gain, weight, *refs):
    outs = refs[: 2 * len(chunks)]
    squares = refs[2 * len(chunks)] if with_squares else None
    rows_buf, weight_buf, gain_buf, weight_sems, row_sems, gain_sem = refs[-6:]
    depth, width = weight_buf.shape
    me = lax.axis_index("tensor")
    chip = lax.rem(lax.div(me, 2) + step, chip_count)
    core = lax.rem(me, 2)
    place = pl.ds(pl.multiple_of(chip * width, width), width)
    cuts = weight_sems.shape[0]
    cut = depth // cuts

    copies = [pltpu.make_async_copy(gain, gain_buf, gain_sem)]
    weight_copies = [
        pltpu.make_async_copy(
            weight.at[pl.ds(index * cut, cut), place],
            weight_buf.at[pl.ds(index * cut, cut), :],
            weight_sems.at[index],
        )
        for index in range(cuts)
    ]
    row_copies, at = [], 0
    for index, (first, count) in enumerate(chunks):
        row_copies.append(
            pltpu.make_async_copy(
                tokens.at[pl.ds(first * TILE, count * TILE), :],
                rows_buf.at[pl.ds(at, count * TILE), :],
                row_sems.at[index],
            )
        )
        at += count * TILE
    for copy in copies + row_copies[:1] + weight_copies + row_copies[1:]:
        copy.start()

    copies[0].wait()
    gains = gain_buf[...].reshape(1, depth)
    at = 0
    for index, (first, count) in enumerate(chunks):
        row_copies[index].wait()
        for tile in range(count):
            rows = rows_buf[pl.ds(at, TILE), :]
            scaled = rows * gains
            if index == 0 and tile == 0:
                product = jnp.zeros((TILE, width), jnp.float32)
                for part in range(cuts):
                    weight_copies[part].wait()
                    span = slice(part * cut, (part + 1) * cut)
                    product += jnp.dot(
                        scaled[:, span], weight_buf[span, :], preferred_element_type=jnp.float32
                    )
            else:
                product = jnp.dot(scaled, weight_buf[...], preferred_element_type=jnp.float32)
            left = product[:, : width // 2].astype(jnp.bfloat16)
            right = product[:, width // 2 :].astype(jnp.bfloat16)
            inside = pl.ds(tile * TILE, TILE)
            outs[2 * index][inside, :] = jnp.where(core == 0, left, right)
            outs[2 * index + 1][inside, :] = jnp.where(core == 0, right, left)
            if with_squares:
                total = square_sums(rows)
                for part in range(TILE // LANES):
                    turned = jnp.transpose(total[part * LANES : (part + 1) * LANES])
                    squares[pl.ds(at // LANES + part, 1), :] = jnp.sum(turned, axis=0, keepdims=True)
            at += TILE


def add_kernel(keep, received, out):
    out[...] = (keep[...].astype(jnp.float32) + received[...].astype(jnp.float32)).astype(out.dtype)


def finish_kernel(first_tile, chip_count, model_dim, live, *refs):
    keep, received, far_cos, far_sin, near_cos, near_sin = refs[:6]
    squares, arrived, out = refs[6 : 6 + chip_count], refs[6 + chip_count : -2], refs[-1]
    values = keep[...].astype(jnp.float32) + received[...].astype(jnp.float32)
    for part in arrived:
        values += part[...].astype(jnp.float32)
    on_diagonal = lax.broadcasted_iota(jnp.int32, (LANES, LANES), 0) == lax.broadcasted_iota(
        jnp.int32, (LANES, LANES), 1
    )
    tile = first_tile + pl.program_id(0)
    columns = []
    for part in range(TILE // LANES):
        row = pl.ds(tile * (TILE // LANES) + part, 1)
        totals = functools.reduce(jnp.add, [ref[row, :] for ref in squares])
        columns.append(jnp.sum(jnp.where(on_diagonal, totals, 0.0), axis=1, keepdims=True))
    scales = 1.0 / jnp.sqrt(jnp.concatenate(columns, axis=0) / model_dim + norm_eps)
    row = tile * TILE + lax.broadcasted_iota(jnp.int32, (TILE, 1), 0)
    alive = row < live[lax.axis_index("serve")] * BLOCK
    sign = jnp.where(lax.broadcasted_iota(jnp.int32, (1, HD), 1) < HD // 2, -1.0, 1.0)
    cosines, sines = [], []
    for part in range(TILE // BLOCK):
        block_cos = far_cos[part]
        block_sin = far_sin[part]
        cosines.append(block_cos * near_cos[...] - block_sin * near_sin[...])
        sines.append((sign * block_sin) * near_cos[...] + (sign * block_cos) * near_sin[...])
    cosine = jnp.concatenate(cosines, axis=0)
    sine = jnp.concatenate(sines, axis=0)
    for start in range(0, out.shape[1], 2 * HD):
        key = values[:, start : start + HD] * scales
        turned = key * cosine + pltpu.roll(key, HD // 2, 1) * sine
        out[:, start : start + HD] = jnp.where(alive, turned, 0.0).astype(out.dtype)
        value = values[:, start + HD : start + 2 * HD] * scales
        out[:, start + HD : start + 2 * HD] = jnp.where(alive, value, 0.0).astype(out.dtype)


def shards(tokens, norm_gain, kv_weight, live_blocks, span_offset):
    tensor_count = lax.axis_size("tensor")
    chip_count = tensor_count // 2
    me = lax.axis_index("tensor")
    own_index = lax.axis_index("serve")
    slot_rows, depth = tokens.shape
    columns = kv_weight.shape[1] // tensor_count
    tiles = slot_rows // TILE
    model_dim = depth * tensor_count

    swap = [(i, i ^ 1) for i in range(tensor_count)]

    def shift(step):
        return [(i, (i + 2 * step) % tensor_count) for i in range(tensor_count)]

    def product(gain, step, chunks, with_squares):
        rows = [count * TILE for _, count in chunks]
        out_shape = [
            jax.ShapeDtypeStruct((size, columns), jnp.bfloat16) for size in rows for _ in range(2)
        ]
        if with_squares:
            out_shape.append(jax.ShapeDtypeStruct((sum(rows) // LANES, LANES), jnp.float32))
        made = pl.pallas_call(
            functools.partial(product_kernel, step, chip_count, chunks, with_squares),
            in_specs=[pl.BlockSpec(memory_space=pl.ANY)] * 3,
            out_shape=out_shape,
            scratch_shapes=[
                pltpu.VMEM((sum(rows), depth), jnp.bfloat16),
                pltpu.VMEM((depth, 2 * columns), jnp.bfloat16),
                pltpu.VMEM((depth,), jnp.bfloat16),
                pltpu.SemaphoreType.DMA((4,)),
                pltpu.SemaphoreType.DMA((len(chunks),)),
                pltpu.SemaphoreType.DMA,
            ],
            compiler_params=WIDE,
            cost_estimate=COST,
        )(tokens, gain, kv_weight)
        pairs = [(made[2 * index], made[2 * index + 1]) for index in range(len(chunks))]
        return (pairs, made[-1]) if with_squares else pairs

    def tables(offset):
        half = HD // 2
        inv_freq = rope_base ** (-(jnp.arange(half, dtype=jnp.float32) * 2.0) / HD)
        inv_freq = jnp.concatenate([inv_freq, inv_freq])
        starts = offset * PAGE + BLOCK * jnp.arange(slot_rows // BLOCK, dtype=jnp.int32)
        far = starts.astype(jnp.float32)[:, None, None] * inv_freq
        near = jnp.arange(BLOCK, dtype=jnp.float32)[:, None] * inv_freq
        return [jnp.cos(far), jnp.sin(far), jnp.cos(near), jnp.sin(near)]

    def finish(first, count, keep, received, table, squares, arrived, result):
        blocks = TILE // BLOCK
        operands = [keep, received] + table + squares + arrived
        specs = (
            [pl.BlockSpec((TILE, columns), lambda i, *_: (first + i, 0))] * 2
            + [pl.BlockSpec((blocks, 1, HD), lambda i, *_: (first + i, 0, 0))] * 2
            + [pl.BlockSpec((BLOCK, HD), lambda i, *_: (0, 0))] * 2
            + [pl.BlockSpec((slot_rows // LANES, LANES), lambda i, *_: (0, 0))] * chip_count
            + [pl.BlockSpec((TILE, columns), lambda i, *_: (i, 0))] * len(arrived)
        )
        if result is None:
            result = keep
            aliases = {}
        else:
            aliases = {1 + len(operands): 0}
        return pl.pallas_call(
            functools.partial(finish_kernel, first, chip_count, model_dim),
            grid_spec=pltpu.PrefetchScalarGridSpec(
                num_scalar_prefetch=1,
                grid=(count,),
                in_specs=specs + [pl.BlockSpec(memory_space=pl.ANY)],
                out_specs=pl.BlockSpec((TILE, columns), lambda i, *_: (first + i, 0)),
            ),
            out_shape=jax.ShapeDtypeStruct((slot_rows, columns), jnp.bfloat16),
            input_output_aliases=aliases,
            compiler_params=PARAMS,
            cost_estimate=COST,
        )(live_blocks, *operands, result)

    others = range(1, chip_count)
    firsts = [sum(CHUNKS[:index]) for index in range(len(CHUNKS))]
    chunk_count = len(CHUNKS)

    def start_chunks(gain, wanted):
        chunks = [(firsts[index], CHUNKS[index]) for index in wanted]
        made = [product(gain, step, chunks, False) for step in others]
        return [[per_step[index] for per_step in made] for index in range(len(wanted))]

    def add_halves(made):
        return [
            pl.pallas_call(
                add_kernel,
                out_shape=jax.ShapeDtypeStruct(keep.shape, keep.dtype),
                compiler_params=PARAMS,
                cost_estimate=COST,
            )(keep, lax.ppermute(send, "tensor", swap))
            for keep, send in made
        ]

    def cross(sums):
        return [lax.ppermute(part, "tensor", shift(step)) for step, part in zip(others, sums)]

    hold = lax.optimization_barrier
    gain, arrivals = norm_gain, []
    own, inputs, result, finished = None, None, None, 0
    (made,) = start_chunks(gain, [0])
    made, gain = hold((made, gain))
    sums = add_halves(made)
    waiting = start_chunks(gain, [1])
    sums, waiting, gain, span_offset = hold((sums, waiting, gain, span_offset))
    for stage in range(1, chunk_count + 1):
        arrived = cross(sums)
        if stage < chunk_count:
            sums = add_halves(waiting.pop(0))
        if stage == 1:
            waiting += start_chunks(gain, list(range(2, chunk_count)))
        if stage == 2:
            ((keep, send),), squares = product(gain, 0, [(0, tiles)], True)
            squares += lax.ppermute(squares, "tensor", swap)
            own = keep, send, squares, tables(span_offset[own_index])
        if stage == 3:
            keep, send, squares, table = own
            received = lax.ppermute(send, "tensor", swap)
            squares = [squares] + [lax.ppermute(squares, "tensor", shift(step)) for step in others]
            inputs = keep, received, table, squares
        if stage >= 4:
            for index in range(finished, stage - 1):
                result = finish(firsts[index], CHUNKS[index], *inputs, arrivals[index], result)
            finished = stage - 1
        arrived, sums, waiting, gain, span_offset, own, inputs, result = hold(
            (arrived, sums, waiting, gain, span_offset, own, inputs, result)
        )
        arrivals.append(arrived)
    for index in range(finished, chunk_count):
        result = finish(firsts[index], CHUNKS[index], *inputs, arrivals[index], result)
    return result


def solution(mesh):
    in_specs = (
        P(("groups", "serve"), "tensor"),
        P("tensor"),
        P("tensor", None),
        P("groups"),
        P("groups"),
    )
    out_specs = P(("groups", "serve"), "tensor")
    return jax.shard_map(shards, mesh=mesh, in_specs=in_specs, out_specs=out_specs, check_vma=False)
```

```python
import functools

import jax
import jax.numpy as jnp
from jax import lax
from jax.experimental import pallas as pl
from jax.experimental.pallas import tpu as pltpu
from jax.sharding import PartitionSpec as P

HD = 128
PAGE = 256
BLOCK = 64
LANES = 128

rope_base = 500000.0
norm_eps = 1e-05

TILE = 256
CHUNKS = (1, 2, 2, 1)

PARAMS = pltpu.CompilerParams(vmem_limit_bytes=16 * 1024 * 1024)
FIRST = pltpu.CompilerParams(vmem_limit_bytes=48 * 1024 * 1024)
COST = pl.CostEstimate(flops=1, bytes_accessed=1, transcendentals=0)


def square_sums(rows):
    total = jnp.zeros((rows.shape[0], LANES), jnp.float32)
    for part in range(rows.shape[1] // LANES):
        wide = rows[:, part * LANES : (part + 1) * LANES].astype(jnp.float32)
        total += wide * wide
    return total


def product_kernel(step, chip_count, chunks, with_squares, load_weight, load_rows, tokens, gain, weight, *refs):
    outs = list(refs[: 2 * len(chunks)])
    refs = list(refs[2 * len(chunks) :])
    squares = refs.pop(0) if with_squares else None
    weight_buf = refs.pop(0) if load_weight else weight
    rows_buf = refs.pop(0) if load_rows else tokens
    gain_buf, weight_sems, row_sems, gain_sem = refs
    depth, width = weight_buf.shape
    me = lax.axis_index("tensor")
    core = lax.rem(me, 2)
    cuts = weight_sems.shape[0] if load_weight else 1
    cut = depth // cuts

    gain_copy = pltpu.make_async_copy(gain, gain_buf, gain_sem)
    weight_copies = []
    if load_weight:
        chip = lax.rem(lax.div(me, 2) + step, chip_count)
        place = pl.ds(pl.multiple_of(chip * width, width), width)
        weight_copies = [
            pltpu.make_async_copy(
                weight.at[pl.ds(index * cut, cut), place],
                weight_buf.at[pl.ds(index * cut, cut), :],
                weight_sems.at[index],
            )
            for index in range(cuts)
        ]
    row_copies = []
    if load_rows:
        first, count = chunks[0]
        edges = [0, first * TILE, (first + count) * TILE, tokens.shape[0]]
        row_copies = [
            pltpu.make_async_copy(
                tokens.at[pl.ds(low, high - low), :], rows_buf.at[pl.ds(low, high - low), :], row_sems.at[index]
            )
            for index, (low, high) in enumerate(zip(edges, edges[1:]))
            if low < high
        ]
        if first:
            row_copies[:2] = row_copies[1::-1]
    for copy in [gain_copy] + row_copies[:1] + weight_copies + row_copies[1:]:
        copy.start()

    gain_copy.wait()
    gains = gain_buf[...].reshape(1, depth)
    for index, (first, count) in enumerate(chunks):
        for copy in row_copies if index == 1 else row_copies[:1] if index == 0 else []:
            copy.wait()
        row_copies = row_copies[1:] if index == 0 else []
        for tile in range(count):
            at = (first + tile) * TILE
            rows = rows_buf[pl.ds(at, TILE), :]
            scaled = rows * gains
            if weight_copies:
                product = jnp.zeros((TILE, width), jnp.float32)
                for part, copy in enumerate(weight_copies):
                    copy.wait()
                    span = slice(part * cut, (part + 1) * cut)
                    product += jnp.dot(
                        scaled[:, span], weight_buf[span, :], preferred_element_type=jnp.float32
                    )
                weight_copies = []
            else:
                product = jnp.dot(scaled, weight_buf[...], preferred_element_type=jnp.float32)
            left = product[:, : width // 2].astype(jnp.bfloat16)
            right = product[:, width // 2 :].astype(jnp.bfloat16)
            inside = pl.ds(tile * TILE, TILE)
            outs[2 * index][inside, :] = jnp.where(core == 0, left, right)
            outs[2 * index + 1][inside, :] = jnp.where(core == 0, right, left)
            if with_squares:
                total = square_sums(rows)
                for part in range(TILE // LANES):
                    turned = jnp.transpose(total[part * LANES : (part + 1) * LANES])
                    squares[at // LANES + part : at // LANES + part + 1, :] = jnp.sum(turned, axis=0, keepdims=True)
    for copy in row_copies:
        copy.wait()


def add_kernel(keep, received, out):
    out[...] = (keep[...].astype(jnp.float32) + received[...].astype(jnp.float32)).astype(out.dtype)


def finish_kernel(first_tile, chip_count, model_dim, live, *refs):
    keep, received, far_cos, far_sin, near_cos, near_sin = refs[:6]
    squares, arrived, out = refs[6 : 6 + chip_count], refs[6 + chip_count : -2], refs[-1]
    values = keep[...].astype(jnp.float32) + received[...].astype(jnp.float32)
    for part in arrived:
        values += part[...].astype(jnp.float32)
    on_diagonal = lax.broadcasted_iota(jnp.int32, (LANES, LANES), 0) == lax.broadcasted_iota(
        jnp.int32, (LANES, LANES), 1
    )
    tile = first_tile + pl.program_id(0)
    columns = []
    for part in range(TILE // LANES):
        row = pl.ds(tile * (TILE // LANES) + part, 1)
        totals = functools.reduce(jnp.add, [ref[row, :] for ref in squares])
        columns.append(jnp.sum(jnp.where(on_diagonal, totals, 0.0), axis=1, keepdims=True))
    scales = 1.0 / jnp.sqrt(jnp.concatenate(columns, axis=0) / model_dim + norm_eps)
    row = tile * TILE + lax.broadcasted_iota(jnp.int32, (TILE, 1), 0)
    alive = row < live[lax.axis_index("serve")] * BLOCK
    sign = jnp.where(lax.broadcasted_iota(jnp.int32, (1, HD), 1) < HD // 2, -1.0, 1.0)
    cosines, sines = [], []
    for part in range(TILE // BLOCK):
        block_cos = far_cos[part]
        block_sin = far_sin[part]
        cosines.append(block_cos * near_cos[...] - block_sin * near_sin[...])
        sines.append((sign * block_sin) * near_cos[...] + (sign * block_cos) * near_sin[...])
    cosine = jnp.concatenate(cosines, axis=0)
    sine = jnp.concatenate(sines, axis=0)
    for start in range(0, out.shape[1], 2 * HD):
        key = values[:, start : start + HD] * scales
        turned = key * cosine + pltpu.roll(key, HD // 2, 1) * sine
        out[:, start : start + HD] = jnp.where(alive, turned, 0.0).astype(out.dtype)
        value = values[:, start + HD : start + 2 * HD] * scales
        out[:, start + HD : start + 2 * HD] = jnp.where(alive, value, 0.0).astype(out.dtype)


def shards(tokens, norm_gain, kv_weight, live_blocks, span_offset):
    tensor_count = lax.axis_size("tensor")
    chip_count = tensor_count // 2
    me = lax.axis_index("tensor")
    own_index = lax.axis_index("serve")
    slot_rows, depth = tokens.shape
    columns = kv_weight.shape[1] // tensor_count
    tiles = slot_rows // TILE
    model_dim = depth * tensor_count

    swap = [(i, i ^ 1) for i in range(tensor_count)]

    def shift(step):
        return [(i, (i + 2 * step) % tensor_count) for i in range(tensor_count)]

    def product(gain, step, chunks, with_squares=False, weight=None, rows=None):
        vmem = pl.BlockSpec(memory_space=pltpu.VMEM)
        hbm = pl.BlockSpec(memory_space=pltpu.HBM)
        out_shape = [
            jax.ShapeDtypeStruct((count * TILE, columns), jnp.bfloat16) for _, count in chunks for _ in range(2)
        ]
        if with_squares:
            out_shape.append(jax.ShapeDtypeStruct((slot_rows // LANES, LANES), jnp.float32))
        if weight is None:
            out_shape.append(jax.ShapeDtypeStruct((depth, 2 * columns), jnp.bfloat16))
        if rows is None:
            out_shape.append(jax.ShapeDtypeStruct(tokens.shape, tokens.dtype))
        made = pl.pallas_call(
            functools.partial(product_kernel, step, chip_count, chunks, with_squares, weight is None, rows is None),
            in_specs=[hbm if rows is None else vmem, hbm, hbm if weight is None else vmem],
            out_shape=out_shape,
            out_specs=[vmem] * len(out_shape),
            scratch_shapes=[
                pltpu.VMEM((depth,), jnp.bfloat16),
                pltpu.SemaphoreType.DMA((4,)),
                pltpu.SemaphoreType.DMA((3,)),
                pltpu.SemaphoreType.DMA,
            ],
            compiler_params=FIRST if rows is None else PARAMS,
            cost_estimate=COST,
        )(tokens if rows is None else rows, gain, kv_weight if weight is None else weight)
        pairs = [(made[2 * index], made[2 * index + 1]) for index in range(len(chunks))]
        return [pairs] + list(made[2 * len(chunks) :])

    def tables(offset):
        half = HD // 2
        inv_freq = rope_base ** (-(jnp.arange(half, dtype=jnp.float32) * 2.0) / HD)
        inv_freq = jnp.concatenate([inv_freq, inv_freq])
        starts = offset * PAGE + BLOCK * jnp.arange(slot_rows // BLOCK, dtype=jnp.int32)
        far = starts.astype(jnp.float32)[:, None, None] * inv_freq
        near = jnp.arange(BLOCK, dtype=jnp.float32)[:, None] * inv_freq
        return [jnp.cos(far), jnp.sin(far), jnp.cos(near), jnp.sin(near)]

    def finish(first, count, keep, received, table, squares, arrived, result):
        blocks = TILE // BLOCK
        operands = [keep, received] + table + squares + arrived
        specs = (
            [pl.BlockSpec((TILE, columns), lambda i, *_: (first + i, 0))] * 2
            + [pl.BlockSpec((blocks, 1, HD), lambda i, *_: (first + i, 0, 0))] * 2
            + [pl.BlockSpec((BLOCK, HD), lambda i, *_: (0, 0))] * 2
            + [pl.BlockSpec((slot_rows // LANES, LANES), lambda i, *_: (0, 0))] * chip_count
            + [pl.BlockSpec((TILE, columns), lambda i, *_: (i, 0))] * len(arrived)
        )
        if result is None:
            result = keep
            aliases = {}
        else:
            aliases = {1 + len(operands): 0}
        return pl.pallas_call(
            functools.partial(finish_kernel, first, chip_count, model_dim),
            grid_spec=pltpu.PrefetchScalarGridSpec(
                num_scalar_prefetch=1,
                grid=(count,),
                in_specs=specs + [pl.BlockSpec(memory_space=pl.ANY)],
                out_specs=pl.BlockSpec((TILE, columns), lambda i, *_: (first + i, 0)),
            ),
            out_shape=jax.ShapeDtypeStruct((slot_rows, columns), jnp.bfloat16),
            input_output_aliases=aliases,
            compiler_params=PARAMS,
            cost_estimate=COST,
        )(live_blocks, *operands, result)

    others = range(1, chip_count)
    firsts = [sum(CHUNKS[:index]) for index in range(len(CHUNKS))]
    chunk_count = len(CHUNKS)

    def start_chunks(gain, wanted, kept):
        chunks = [(firsts[index], CHUNKS[index]) for index in wanted]
        made = []
        for step in others:
            results = product(gain, step, chunks, weight=kept.get(step), rows=kept.get("rows"))
            made.append(results[0])
            if step not in kept:
                kept[step] = results[1]
            if "rows" not in kept:
                kept["rows"] = results[2]
        return [[pairs[index] for pairs in made] for index in range(len(wanted))]

    def add_halves(made):
        return [
            pl.pallas_call(
                add_kernel,
                out_shape=jax.ShapeDtypeStruct(keep.shape, keep.dtype),
                compiler_params=PARAMS,
                cost_estimate=COST,
            )(keep, lax.ppermute(send, "tensor", swap))
            for keep, send in made
        ]

    def cross(sums):
        return [lax.ppermute(part, "tensor", shift(step)) for step, part in zip(others, sums)]

    hold = lax.optimization_barrier
    gain, kept, arrivals = norm_gain, {}, []
    own, inputs, result, finished, arrived = None, None, None, 0, None
    (made,) = start_chunks(gain, [0], kept)
    made, gain = hold((made, gain))
    sums = add_halves(made)
    waiting = start_chunks(gain, [1], kept)
    sums, waiting, gain, span_offset = hold((sums, waiting, gain, span_offset))
    for stage in range(1, chunk_count + 2):
        before, arrived = arrived, None
        if stage <= chunk_count:
            arrived = cross(sums)
        if stage < chunk_count:
            sums = add_halves(waiting.pop(0))
        if stage == 1:
            waiting += start_chunks(gain, list(range(2, chunk_count)), kept)
        if stage == 2:
            ((keep, send),), squares, _ = product(gain, 0, [(0, tiles)], True, rows=kept["rows"])
            squares += lax.ppermute(squares, "tensor", swap)
            own = keep, send, squares, tables(span_offset[own_index])
        if stage == 3:
            keep, send, squares, table = own
            received = lax.ppermute(send, "tensor", swap)
            squares = [squares] + [lax.ppermute(squares, "tensor", shift(step)) for step in others]
            inputs = keep, received, table, squares
        if stage >= 4:
            for index in range(finished, stage - 2):
                result = finish(firsts[index], CHUNKS[index], *inputs, arrivals[index], result)
            finished = stage - 2
        before, sums, waiting, gain, span_offset, own, inputs, result = hold(
            (before, sums, waiting, gain, span_offset, own, inputs, result)
        )
        if before is not None:
            arrivals.append(before)
    for index in range(finished, chunk_count):
        result = finish(firsts[index], CHUNKS[index], *inputs, arrivals[index], result)
    return result


def solution(mesh):
    in_specs = (
        P(("groups", "serve"), "tensor"),
        P("tensor"),
        P("tensor", None),
        P("groups"),
        P("groups"),
    )
    out_specs = P(("groups", "serve"), "tensor")
    return jax.shard_map(shards, mesh=mesh, in_specs=in_specs, out_specs=out_specs, check_vma=False)
```

```python
import functools

import jax
import jax.numpy as jnp
from jax import lax
from jax.experimental import pallas as pl
from jax.experimental.pallas import tpu as pltpu
from jax.sharding import PartitionSpec as P

HD = 128
PAGE = 256
BLOCK = 64
LANES = 128

rope_base = 500000.0
norm_eps = 1e-05

TILE = 256
CHUNKS = (2, 2, 2)

PARAMS = pltpu.CompilerParams(vmem_limit_bytes=16 * 1024 * 1024)
FIRST = pltpu.CompilerParams(vmem_limit_bytes=48 * 1024 * 1024)
COST = pl.CostEstimate(flops=1, bytes_accessed=1, transcendentals=0)


def square_sums(rows):
    total = jnp.zeros((rows.shape[0], LANES), jnp.float32)
    for part in range(rows.shape[1] // LANES):
        wide = rows[:, part * LANES : (part + 1) * LANES].astype(jnp.float32)
        total += wide * wide
    return total


def product_kernel(step, chip_count, chunks, loaded, load, with_squares, load_weight, tokens, gain, weight, *refs):
    refs = list(refs)
    sources = [(first, count, refs.pop(0)) for first, count in loaded]
    outs = [refs.pop(0) for _ in range(2 * len(chunks))]
    squares = refs.pop(0) if with_squares else None
    weight_buf = refs.pop(0) if load_weight else weight
    if load:
        sources.append((*load, refs.pop(0)))
    gain_buf, weight_sems, row_sems, gain_sem = refs
    depth, width = weight_buf.shape
    me = lax.axis_index("tensor")
    core = lax.rem(me, 2)
    cuts = weight_sems.shape[0] if load_weight else 1
    cut = depth // cuts

    gain_copy = pltpu.make_async_copy(gain, gain_buf, gain_sem)
    weight_copies = []
    if load_weight:
        chip = lax.rem(lax.div(me, 2) + step, chip_count)
        place = pl.ds(pl.multiple_of(chip * width, width), width)
        weight_copies = [
            pltpu.make_async_copy(
                weight.at[pl.ds(index * cut, cut), place],
                weight_buf.at[pl.ds(index * cut, cut), :],
                weight_sems.at[index],
            )
            for index in range(cuts)
        ]
    row_copies = {}
    if load:
        first, count = load
        for index in range(count):
            row_copies[first + index] = pltpu.make_async_copy(
                tokens.at[pl.ds((first + index) * TILE, TILE), :],
                sources[-1][2].at[pl.ds(index * TILE, TILE), :],
                row_sems.at[index],
            )
    in_order = list(row_copies.values())
    for copy in [gain_copy] + in_order[:1] + weight_copies + in_order[1:]:
        copy.start()

    gain_copy.wait()
    gains = gain_buf[...].reshape(1, depth)
    for index, (first, count) in enumerate(chunks):
        for tile in range(first, first + count):
            if tile in row_copies:
                row_copies.pop(tile).wait()
            low, _, source = [entry for entry in sources if entry[0] <= tile < entry[0] + entry[1]][0]
            rows = source[pl.ds((tile - low) * TILE, TILE), :]
            scaled = rows * gains
            if weight_copies:
                product = jnp.zeros((TILE, width), jnp.float32)
                for part, copy in enumerate(weight_copies):
                    copy.wait()
                    span = slice(part * cut, (part + 1) * cut)
                    product += jnp.dot(
                        scaled[:, span], weight_buf[span, :], preferred_element_type=jnp.float32
                    )
                weight_copies = []
            else:
                product = jnp.dot(scaled, weight_buf[...], preferred_element_type=jnp.float32)
            left = product[:, : width // 2].astype(jnp.bfloat16)
            right = product[:, width // 2 :].astype(jnp.bfloat16)
            inside = pl.ds((tile - first) * TILE, TILE)
            outs[2 * index][inside, :] = jnp.where(core == 0, left, right)
            outs[2 * index + 1][inside, :] = jnp.where(core == 0, right, left)
            if with_squares:
                total = square_sums(rows)
                for part in range(TILE // LANES):
                    turned = jnp.transpose(total[part * LANES : (part + 1) * LANES])
                    row = tile * (TILE // LANES) + part
                    squares[row : row + 1, :] = jnp.sum(turned, axis=0, keepdims=True)
    for copy in row_copies.values():
        copy.wait()


def add_kernel(keep, received, out):
    out[...] = (keep[...].astype(jnp.float32) + received[...].astype(jnp.float32)).astype(out.dtype)


def finish_kernel(first_tile, tensor_count, model_dim, live, *refs):
    keep, received, far_cos, far_sin, near_cos, near_sin = refs[:6]
    squares, arrived, out = refs[6 : 6 + tensor_count], refs[6 + tensor_count : -2], refs[-1]
    values = keep[...].astype(jnp.float32) + received[...].astype(jnp.float32)
    for part in arrived:
        values += part[...].astype(jnp.float32)
    on_diagonal = lax.broadcasted_iota(jnp.int32, (LANES, LANES), 0) == lax.broadcasted_iota(
        jnp.int32, (LANES, LANES), 1
    )
    tile = first_tile + pl.program_id(0)
    columns = []
    for part in range(TILE // LANES):
        row = pl.ds(tile * (TILE // LANES) + part, 1)
        totals = functools.reduce(jnp.add, [ref[row, :] for ref in squares])
        columns.append(jnp.sum(jnp.where(on_diagonal, totals, 0.0), axis=1, keepdims=True))
    scales = 1.0 / jnp.sqrt(jnp.concatenate(columns, axis=0) / model_dim + norm_eps)
    row = tile * TILE + lax.broadcasted_iota(jnp.int32, (TILE, 1), 0)
    alive = row < live[lax.axis_index("serve")] * BLOCK
    sign = jnp.where(lax.broadcasted_iota(jnp.int32, (1, HD), 1) < HD // 2, -1.0, 1.0)
    cosines, sines = [], []
    for part in range(TILE // BLOCK):
        block_cos = far_cos[part]
        block_sin = far_sin[part]
        cosines.append(block_cos * near_cos[...] - block_sin * near_sin[...])
        sines.append((sign * block_sin) * near_cos[...] + (sign * block_cos) * near_sin[...])
    cosine = jnp.concatenate(cosines, axis=0)
    sine = jnp.concatenate(sines, axis=0)
    for start in range(0, out.shape[1], 2 * HD):
        key = values[:, start : start + HD] * scales
        turned = key * cosine + pltpu.roll(key, HD // 2, 1) * sine
        out[:, start : start + HD] = jnp.where(alive, turned, 0.0).astype(out.dtype)
        value = values[:, start + HD : start + 2 * HD] * scales
        out[:, start + HD : start + 2 * HD] = jnp.where(alive, value, 0.0).astype(out.dtype)


def shards(tokens, norm_gain, kv_weight, live_blocks, span_offset):
    tensor_count = lax.axis_size("tensor")
    chip_count = tensor_count // 2
    me = lax.axis_index("tensor")
    own_index = lax.axis_index("serve")
    slot_rows, depth = tokens.shape
    columns = kv_weight.shape[1] // tensor_count
    tiles = slot_rows // TILE
    model_dim = depth * tensor_count

    swap = [(i, i ^ 1) for i in range(tensor_count)]

    def shift(step):
        return [(i, (i + 2 * step) % tensor_count) for i in range(tensor_count)]

    def product(gain, step, chunks, kept, load=None, with_squares=False):
        vmem = pl.BlockSpec(memory_space=pltpu.VMEM)
        hbm = pl.BlockSpec(memory_space=pltpu.HBM)
        weight = kept.get(step)
        loaded = kept["rows"]
        out_shape = [
            jax.ShapeDtypeStruct((count * TILE, columns), jnp.bfloat16) for _, count in chunks for _ in range(2)
        ]
        if with_squares:
            out_shape.append(jax.ShapeDtypeStruct((slot_rows // LANES, LANES), jnp.float32))
        if weight is None:
            out_shape.append(jax.ShapeDtypeStruct((depth, 2 * columns), jnp.bfloat16))
        if load:
            out_shape.append(jax.ShapeDtypeStruct((load[1] * TILE, depth), jnp.bfloat16))
        made = pl.pallas_call(
            functools.partial(
                product_kernel,
                step,
                chip_count,
                chunks,
                [entry[:2] for entry in loaded],
                load,
                with_squares,
                weight is None,
            ),
            in_specs=[hbm, hbm, hbm if weight is None else vmem] + [vmem] * len(loaded),
            out_shape=out_shape,
            out_specs=[vmem] * len(out_shape),
            scratch_shapes=[
                pltpu.VMEM((depth,), jnp.bfloat16),
                pltpu.SemaphoreType.DMA((4,)),
                pltpu.SemaphoreType.DMA((tiles,)),
                pltpu.SemaphoreType.DMA,
            ],
            compiler_params=PARAMS if loaded else FIRST,
            cost_estimate=COST,
        )(tokens, gain, kv_weight if weight is None else weight, *[entry[2] for entry in loaded])
        made = list(made)
        if load:
            kept["rows"] = loaded + [(*load, made.pop())]
        if weight is None:
            kept[step] = made.pop()
        squares = made.pop() if with_squares else None
        return list(zip(made[::2], made[1::2])), squares

    def tables(offset):
        half = HD // 2
        inv_freq = rope_base ** (-(jnp.arange(half, dtype=jnp.float32) * 2.0) / HD)
        inv_freq = jnp.concatenate([inv_freq, inv_freq])
        starts = offset * PAGE + BLOCK * jnp.arange(slot_rows // BLOCK, dtype=jnp.int32)
        far = starts.astype(jnp.float32)[:, None, None] * inv_freq
        near = jnp.arange(BLOCK, dtype=jnp.float32)[:, None] * inv_freq
        return [jnp.cos(far), jnp.sin(far), jnp.cos(near), jnp.sin(near)]

    def finish(first, count, keep, received, table, squares, arrived, result):
        blocks = TILE // BLOCK
        operands = [keep, received] + table + squares + arrived
        specs = (
            [pl.BlockSpec((TILE, columns), lambda i, *_: (first + i, 0))] * 2
            + [pl.BlockSpec((blocks, 1, HD), lambda i, *_: (first + i, 0, 0))] * 2
            + [pl.BlockSpec((BLOCK, HD), lambda i, *_: (0, 0))] * 2
            + [pl.BlockSpec((slot_rows // LANES, LANES), lambda i, *_: (0, 0))] * tensor_count
            + [pl.BlockSpec((TILE, columns), lambda i, *_: (i, 0))] * len(arrived)
        )
        if result is None:
            result = keep
            aliases = {}
        else:
            aliases = {1 + len(operands): 0}
        return pl.pallas_call(
            functools.partial(finish_kernel, first, tensor_count, model_dim),
            grid_spec=pltpu.PrefetchScalarGridSpec(
                num_scalar_prefetch=1,
                grid=(count,),
                in_specs=specs + [pl.BlockSpec(memory_space=pl.ANY)],
                out_specs=pl.BlockSpec((TILE, columns), lambda i, *_: (first + i, 0)),
            ),
            out_shape=jax.ShapeDtypeStruct((slot_rows, columns), jnp.bfloat16),
            input_output_aliases=aliases,
            compiler_params=PARAMS,
            cost_estimate=COST,
        )(live_blocks, *operands, result)

    others = range(1, chip_count)
    firsts = [sum(CHUNKS[:index]) for index in range(len(CHUNKS))]
    chunk_count = len(CHUNKS)

    def start_chunk(gain, index, kept, load=None):
        made = []
        for step in others:
            made += product(gain, step, [(firsts[index], CHUNKS[index])], kept, load if step == 1 else None)[0]
        return made

    def add_halves(made):
        return [
            pl.pallas_call(
                add_kernel,
                out_shape=jax.ShapeDtypeStruct(keep.shape, keep.dtype),
                compiler_params=PARAMS,
                cost_estimate=COST,
            )(keep, lax.ppermute(send, "tensor", swap))
            for keep, send in made
        ]

    def cross(sums):
        return [lax.ppermute(part, "tensor", shift(step)) for step, part in zip(others, sums)]

    hold = lax.optimization_barrier
    gain, kept = norm_gain, {"rows": []}
    made = start_chunk(gain, 0, kept, (0, CHUNKS[0]))
    made, gain = hold((made, gain))
    sums = add_halves(made)
    made = start_chunk(gain, 1, kept, (CHUNKS[0], tiles - CHUNKS[0]))
    sums, made, gain, span_offset = hold((sums, made, gain, span_offset))

    arrived = cross(sums)
    sums = add_halves(made)
    waiting = [start_chunk(gain, index, kept) for index in range(2, chunk_count)]
    ((keep, send),), squares = product(gain, 0, [(0, tiles)], kept, with_squares=True)
    squares = [squares] + [
        lax.ppermute(squares, "tensor", [(i, (i + step) % tensor_count) for i in range(tensor_count)])
        for step in range(1, tensor_count)
    ]
    table = tables(span_offset[own_index])
    arrived, sums, waiting, keep, send, squares, table = hold(
        (arrived, sums, waiting, keep, send, squares, table)
    )

    arrivals = [arrived, cross(sums)] + [cross(add_halves(made)) for made in waiting]
    received = lax.ppermute(send, "tensor", swap)
    result = None
    for index in range(chunk_count):
        result = finish(
            firsts[index], CHUNKS[index], keep, received, table, squares, arrivals[index], result
        )
    return result


def solution(mesh):
    in_specs = (
        P(("groups", "serve"), "tensor"),
        P("tensor"),
        P("tensor", None),
        P("groups"),
        P("groups"),
    )
    out_specs = P(("groups", "serve"), "tensor")
    return jax.shard_map(shards, mesh=mesh, in_specs=in_specs, out_specs=out_specs, check_vma=False)
```

```python
import functools

import jax
import jax.numpy as jnp
import numpy as np
from jax import lax
from jax.experimental import pallas as pl
from jax.experimental.pallas import tpu as pltpu
from jax.sharding import PartitionSpec as P

HD = 128
PAGE = 256
BLOCK = 64
LANES = 128

rope_base = 500000.0
norm_eps = 1e-05

TILE = 256
CHUNKS = (2, 2, 2)

PARAMS = pltpu.CompilerParams(vmem_limit_bytes=16 * 1024 * 1024)
FIRST = pltpu.CompilerParams(vmem_limit_bytes=56 * 1024 * 1024)
COST = pl.CostEstimate(flops=1, bytes_accessed=1, transcendentals=0)


def square_sums(rows):
    total = jnp.zeros((rows.shape[0], LANES), jnp.float32)
    for part in range(rows.shape[1] // LANES):
        wide = rows[:, part * LANES : (part + 1) * LANES].astype(jnp.float32)
        total += wide * wide
    return total


def product_kernel(step, chip_count, chunks, staged, with_squares, tokens, gain, weight, *refs):
    refs = list(refs)
    outs = [refs.pop(0) for _ in range(2 * len(chunks))]
    squares = refs.pop(0) if with_squares else None
    depth, width = tokens.shape[1], 2 * outs[0].shape[1]
    me = lax.axis_index("tensor")
    core = lax.rem(me, 2)
    chip = lax.rem(lax.div(me, 2) + step, chip_count)
    place = pl.ds(pl.multiple_of(chip * width, width), width)

    weight_copies, row_copies = [], {}
    if staged:
        rows_buf, weight_buf, gain_buf, weight_sems, row_sems, gain_sem = refs
        cuts = weight_sems.shape[0]
        cut = depth // cuts
        gain_copy = pltpu.make_async_copy(gain, gain_buf, gain_sem)
        weight_copies = [
            pltpu.make_async_copy(
                weight.at[pl.ds(index * cut, cut), place],
                weight_buf.at[pl.ds(index * cut, cut), :],
                weight_sems.at[index],
            )
            for index in range(cuts)
        ]
        at = 0
        for first, count in chunks:
            for tile in range(first, first + count):
                buf = rows_buf.at[pl.ds(at * TILE, TILE), :]
                row_copies[tile] = (
                    pltpu.make_async_copy(tokens.at[pl.ds(tile * TILE, TILE), :], buf, row_sems.at[at]),
                    buf,
                )
                at += 1
        in_order = [copy for copy, _ in row_copies.values()]
        for copy in [gain_copy] + in_order[:1] + weight_copies + in_order[1:]:
            copy.start()
        gain_copy.wait()
        gains = gain_buf[...].reshape(1, depth)
    else:
        gains = gain[...].reshape(1, depth)

    for index, (first, count) in enumerate(chunks):
        for tile in range(first, first + count):
            if staged:
                row_copies[tile][0].wait()
                rows = row_copies[tile][1][...]
            else:
                rows = tokens[pl.ds(tile * TILE, TILE), :]
            scaled = rows * gains
            if weight_copies:
                product = jnp.zeros((TILE, width), jnp.float32)
                for part, copy in enumerate(weight_copies):
                    copy.wait()
                    span = slice(part * cut, (part + 1) * cut)
                    product += jnp.dot(
                        scaled[:, span], weight_buf[span, :], preferred_element_type=jnp.float32
                    )
                weight_copies = []
            else:
                columns = weight_buf[...] if staged else weight[:, place]
                product = jnp.dot(scaled, columns, preferred_element_type=jnp.float32)
            left = product[:, : width // 2].astype(jnp.bfloat16)
            right = product[:, width // 2 :].astype(jnp.bfloat16)
            inside = pl.ds((tile - first) * TILE, TILE)
            outs[2 * index][inside, :] = jnp.where(core == 0, left, right)
            outs[2 * index + 1][inside, :] = jnp.where(core == 0, right, left)
            if with_squares:
                total = square_sums(rows)
                for part in range(TILE // LANES):
                    turned = jnp.transpose(total[part * LANES : (part + 1) * LANES])
                    row = tile * (TILE // LANES) + part
                    squares[row : row + 1, :] = jnp.sum(turned, axis=0, keepdims=True)


def add_kernel(keep, received, out):
    out[...] = (keep[...].astype(jnp.float32) + received[...].astype(jnp.float32)).astype(out.dtype)


def table_kernel(span, frequencies, far_cos, far_sin, near_cos, near_sin):
    blocks = far_cos.shape[0]
    start = span[lax.axis_index("serve")] * PAGE
    first = start + BLOCK * lax.broadcasted_iota(jnp.int32, (blocks, HD), 0)
    far = first.astype(jnp.float32) * frequencies[...]
    near = lax.broadcasted_iota(jnp.int32, (BLOCK, HD), 0).astype(jnp.float32) * frequencies[...]
    far_cos[...] = jnp.cos(far)
    far_sin[...] = jnp.sin(far)
    near_cos[...] = jnp.cos(near)
    near_sin[...] = jnp.sin(near)


def finish_kernel(first_tile, tensor_count, model_dim, live, *refs):
    keep, received, far_cos, far_sin, near_cos, near_sin = refs[:6]
    squares, arrived, out = refs[6 : 6 + tensor_count], refs[6 + tensor_count : -2], refs[-1]
    values = keep[...].astype(jnp.float32) + received[...].astype(jnp.float32)
    for part in arrived:
        values += part[...].astype(jnp.float32)
    on_diagonal = lax.broadcasted_iota(jnp.int32, (LANES, LANES), 0) == lax.broadcasted_iota(
        jnp.int32, (LANES, LANES), 1
    )
    tile = first_tile + pl.program_id(0)
    columns = []
    for part in range(TILE // LANES):
        row = pl.ds(tile * (TILE // LANES) + part, 1)
        totals = functools.reduce(jnp.add, [ref[row, :] for ref in squares])
        columns.append(jnp.sum(jnp.where(on_diagonal, totals, 0.0), axis=1, keepdims=True))
    scales = 1.0 / jnp.sqrt(jnp.concatenate(columns, axis=0) / model_dim + norm_eps)
    row = tile * TILE + lax.broadcasted_iota(jnp.int32, (TILE, 1), 0)
    alive = row < live[lax.axis_index("serve")] * BLOCK
    sign = jnp.where(lax.broadcasted_iota(jnp.int32, (1, HD), 1) < HD // 2, -1.0, 1.0)
    cosines, sines = [], []
    for part in range(TILE // BLOCK):
        block = pl.ds(tile * (TILE // BLOCK) + part, 1)
        block_cos = far_cos[block, :]
        block_sin = far_sin[block, :]
        cosines.append(block_cos * near_cos[...] - block_sin * near_sin[...])
        sines.append((sign * block_sin) * near_cos[...] + (sign * block_cos) * near_sin[...])
    cosine = jnp.concatenate(cosines, axis=0)
    sine = jnp.concatenate(sines, axis=0)
    for start in range(0, out.shape[1], 2 * HD):
        key = values[:, start : start + HD] * scales
        turned = key * cosine + pltpu.roll(key, HD // 2, 1) * sine
        out[:, start : start + HD] = jnp.where(alive, turned, 0.0).astype(out.dtype)
        value = values[:, start + HD : start + 2 * HD] * scales
        out[:, start + HD : start + 2 * HD] = jnp.where(alive, value, 0.0).astype(out.dtype)


def shards(tokens, norm_gain, kv_weight, live_blocks, span_offset):
    tensor_count = lax.axis_size("tensor")
    chip_count = tensor_count // 2
    me = lax.axis_index("tensor")
    slot_rows, depth = tokens.shape
    columns = kv_weight.shape[1] // tensor_count
    tiles = slot_rows // TILE
    model_dim = depth * tensor_count

    swap = [(i, i ^ 1) for i in range(tensor_count)]

    def shift(step):
        return [(i, (i + 2 * step) % tensor_count) for i in range(tensor_count)]

    def product(gain, step, chunks, staged=False, with_squares=False):
        vmem = pl.BlockSpec(memory_space=pltpu.VMEM)
        out_shape = [
            jax.ShapeDtypeStruct((count * TILE, columns), jnp.bfloat16) for _, count in chunks for _ in range(2)
        ]
        if with_squares:
            out_shape.append(jax.ShapeDtypeStruct((slot_rows // LANES, LANES), jnp.float32))
        count = sum(count for _, count in chunks)
        scratch = [
            pltpu.VMEM((count * TILE, depth), jnp.bfloat16),
            pltpu.VMEM((depth, 2 * columns), jnp.bfloat16),
            pltpu.VMEM((depth,), jnp.bfloat16),
            pltpu.SemaphoreType.DMA((4,)),
            pltpu.SemaphoreType.DMA((count,)),
            pltpu.SemaphoreType.DMA,
        ]
        made = pl.pallas_call(
            functools.partial(product_kernel, step, chip_count, chunks, staged, with_squares),
            in_specs=[pl.BlockSpec(memory_space=pltpu.HBM) if staged else vmem] * 3,
            out_shape=out_shape,
            out_specs=[vmem] * len(out_shape),
            scratch_shapes=scratch if staged else [],
            compiler_params=FIRST if staged else PARAMS,
            cost_estimate=COST,
        )(tokens, gain, kv_weight)
        made = list(made)
        squares = made.pop() if with_squares else None
        return list(zip(made[::2], made[1::2])), squares

    def tables(span_offset):
        frequencies = rope_base ** (-(np.arange(HD // 2, dtype=np.float32) * 2.0) / HD)
        frequencies = np.concatenate([frequencies, frequencies])[None, :].astype(np.float32)
        shapes = [(slot_rows // BLOCK, HD)] * 2 + [(BLOCK, HD)] * 2
        made = pl.pallas_call(
            table_kernel,
            in_specs=[pl.BlockSpec(memory_space=pltpu.SMEM), pl.BlockSpec(memory_space=pltpu.VMEM)],
            out_shape=[jax.ShapeDtypeStruct(shape, jnp.float32) for shape in shapes],
            out_specs=[pl.BlockSpec(memory_space=pltpu.VMEM)] * 4,
            compiler_params=PARAMS,
            cost_estimate=COST,
        )(span_offset, jnp.asarray(frequencies))
        return list(made)

    def finish(first, count, keep, received, table, squares, arrived, result):
        operands = [keep, received] + table + squares + arrived
        specs = (
            [pl.BlockSpec((TILE, columns), lambda i, *_: (first + i, 0))] * 2
            + [pl.BlockSpec((slot_rows // BLOCK, HD), lambda i, *_: (0, 0))] * 2
            + [pl.BlockSpec((BLOCK, HD), lambda i, *_: (0, 0))] * 2
            + [pl.BlockSpec((slot_rows // LANES, LANES), lambda i, *_: (0, 0))] * tensor_count
            + [pl.BlockSpec((TILE, columns), lambda i, *_: (i, 0))] * len(arrived)
        )
        if result is None:
            result = keep
            aliases = {}
        else:
            aliases = {1 + len(operands): 0}
        return pl.pallas_call(
            functools.partial(finish_kernel, first, tensor_count, model_dim),
            grid_spec=pltpu.PrefetchScalarGridSpec(
                num_scalar_prefetch=1,
                grid=(count,),
                in_specs=specs + [pl.BlockSpec(memory_space=pl.ANY)],
                out_specs=pl.BlockSpec((TILE, columns), lambda i, *_: (first + i, 0)),
            ),
            out_shape=jax.ShapeDtypeStruct((slot_rows, columns), jnp.bfloat16),
            input_output_aliases=aliases,
            compiler_params=PARAMS,
            cost_estimate=COST,
        )(live_blocks, *operands, result)

    others = range(1, chip_count)
    firsts = [sum(CHUNKS[:index]) for index in range(len(CHUNKS))]
    chunk_count = len(CHUNKS)

    def start_chunk(gain, index, staged=False):
        made = []
        for step in others:
            made += product(gain, step, [(firsts[index], CHUNKS[index])], staged)[0]
        return made

    def add_halves(made):
        return [
            pl.pallas_call(
                add_kernel,
                out_shape=jax.ShapeDtypeStruct(keep.shape, keep.dtype),
                compiler_params=PARAMS,
                cost_estimate=COST,
            )(keep, lax.ppermute(send, "tensor", swap))
            for keep, send in made
        ]

    def cross(sums):
        return [lax.ppermute(part, "tensor", shift(step)) for step, part in zip(others, sums)]

    hold = lax.optimization_barrier
    made = start_chunk(norm_gain, 0, staged=True)
    made, gain = hold((made, norm_gain))
    sums = add_halves(made)
    made = start_chunk(gain, 1)
    sums, made, gain, span_offset = hold((sums, made, gain, span_offset))

    arrived = cross(sums)
    sums = add_halves(made)
    waiting = [start_chunk(gain, index) for index in range(2, chunk_count)]
    ((keep, send),), squares = product(gain, 0, [(0, tiles)], with_squares=True)
    squares = [squares] + [
        lax.ppermute(squares, "tensor", [(i, (i + step) % tensor_count) for i in range(tensor_count)])
        for step in range(1, tensor_count)
    ]
    table = tables(span_offset)
    arrived, sums, waiting, keep, send, squares, table = hold(
        (arrived, sums, waiting, keep, send, squares, table)
    )

    arrivals = [arrived, cross(sums)] + [cross(add_halves(made)) for made in waiting]
    received = lax.ppermute(send, "tensor", swap)
    result = None
    for index in range(chunk_count):
        result = finish(
            firsts[index], CHUNKS[index], keep, received, table, squares, arrivals[index], result
        )
    return result


def solution(mesh):
    in_specs = (
        P(("groups", "serve"), "tensor"),
        P("tensor"),
        P("tensor", None),
        P("groups"),
        P("groups"),
    )
    out_specs = P(("groups", "serve"), "tensor")
    return jax.shard_map(shards, mesh=mesh, in_specs=in_specs, out_specs=out_specs, check_vma=False)
```

```python
import functools

import jax
import jax.numpy as jnp
import numpy as np
from jax import lax
from jax.experimental import pallas as pl
from jax.experimental.pallas import tpu as pltpu
from jax.sharding import PartitionSpec as P

HD = 128
PAGE = 256
BLOCK = 64
LANES = 128

rope_base = 500000.0
norm_eps = 1e-05

UNIT = 128
TILE = 256

PARAMS = pltpu.CompilerParams(vmem_limit_bytes=16 * 1024 * 1024)
FIRST = pltpu.CompilerParams(vmem_limit_bytes=56 * 1024 * 1024)
COST = pl.CostEstimate(flops=1, bytes_accessed=1, transcendentals=0)


def square_sums(rows):
    total = jnp.zeros((rows.shape[0], LANES), jnp.float32)
    for part in range(rows.shape[1] // LANES):
        wide = rows[:, part * LANES : (part + 1) * LANES].astype(jnp.float32)
        total += wide * wide
    return total


def choice_of(live, counts, options):
    sessions, blocks = counts
    choice = jnp.int32(len(options))
    for index, (most, shift) in reversed(list(enumerate(options))):
        fits = True
        for session in range(sessions):
            helper = live[(session + shift) % sessions] <= 2 * most - blocks
            fits = fits & ((live[session] <= most) | helper)
        choice = jnp.where(fits, jnp.int32(index), choice)
    return choice


def product_kernel(step, chip_count, groups, staged, with_squares, counts, options, tokens, gain, weight, *refs):
    refs = list(refs)
    live = refs.pop(0) if staged else None
    outs = [refs.pop(0) for _ in range(2 * len(groups))]
    squares = refs.pop(0) if with_squares else None
    depth, width = tokens.shape[1], 2 * outs[0].shape[1]
    me = lax.axis_index("tensor")
    core = lax.rem(me, 2)
    chip = lax.rem(lax.div(me, 2) + step, chip_count)
    place = pl.ds(pl.multiple_of(chip * width, width), width)

    pieces = []
    for index, runs in enumerate(groups):
        at = 0
        for first, count in runs:
            for unit in range(first, first + count, TILE // UNIT):
                size = min(TILE, (first + count - unit) * UNIT)
                pieces.append((index, at, unit * UNIT, size))
                at += size

    weight_copies, row_copies = [], []
    if staged:
        choice, rows_buf, weight_buf, gain_buf, live_buf, weight_sems, row_sems, gain_sem, live_sem = refs
        cuts = weight_sems.shape[0]
        cut = depth // cuts
        gain_copy = pltpu.make_async_copy(gain, gain_buf, gain_sem)
        live_copy = pltpu.make_async_copy(live, live_buf, live_sem)
        weight_copies = [
            pltpu.make_async_copy(
                weight.at[pl.ds(index * cut, cut), place],
                weight_buf.at[pl.ds(index * cut, cut), :],
                weight_sems.at[index],
            )
            for index in range(cuts)
        ]
        at = 0
        for index, (_, _, row, size) in enumerate(pieces):
            buf = rows_buf.at[pl.ds(at, size), :]
            copy = pltpu.make_async_copy(tokens.at[pl.ds(row, size), :], buf, row_sems.at[index])
            row_copies.append((copy, buf))
            at += size
        in_order = [copy for copy, _ in row_copies]
        for copy in [gain_copy] + in_order[:1] + weight_copies + in_order[1:] + [live_copy]:
            copy.start()
        gain_copy.wait()
        gains = gain_buf[...].reshape(1, depth)
    else:
        gains = gain[...].reshape(1, depth)

    for number, (index, at, row, size) in enumerate(pieces):
        if staged:
            row_copies[number][0].wait()
            rows = row_copies[number][1][...]
        else:
            rows = tokens[pl.ds(row, size), :]
        scaled = rows * gains
        if weight_copies:
            product = jnp.zeros((size, width), jnp.float32)
            for part, copy in enumerate(weight_copies):
                copy.wait()
                span = slice(part * cut, (part + 1) * cut)
                product += jnp.dot(scaled[:, span], weight_buf[span, :], preferred_element_type=jnp.float32)
            weight_copies = []
        else:
            columns = weight_buf[...] if staged else weight[:, place]
            product = jnp.dot(scaled, columns, preferred_element_type=jnp.float32)
        left = product[:, : width // 2].astype(jnp.bfloat16)
        right = product[:, width // 2 :].astype(jnp.bfloat16)
        inside = pl.ds(at, size)
        outs[2 * index][inside, :] = jnp.where(core == 0, left, right)
        outs[2 * index + 1][inside, :] = jnp.where(core == 0, right, left)
        if with_squares:
            total = square_sums(rows)
            for part in range(size // LANES):
                turned = jnp.transpose(total[part * LANES : (part + 1) * LANES])
                place_row = row // LANES + part
                squares[place_row : place_row + 1, :] = jnp.sum(turned, axis=0, keepdims=True)
    if staged:
        live_copy.wait()
        choice[0] = choice_of(live_buf, counts, options)


def add_kernel(cuts, keep, received, *outs):
    for (low, size), out in zip(cuts, outs):
        rows = pl.ds(low, size)
        out[...] = (keep[rows, :].astype(jnp.float32) + received[rows, :].astype(jnp.float32)).astype(out.dtype)


def pick_kernel(most, shift, sessions, live, guest, own, out):
    helped = lax.rem(lax.axis_index("serve") + sessions - shift, sessions)
    out[...] = jnp.where(live[helped] > most, guest[...], own[...])


def table_kernel(span, frequencies, far_cos, far_sin, near_cos, near_sin):
    blocks = far_cos.shape[0]
    start = span[lax.axis_index("serve")] * PAGE
    first = start + BLOCK * lax.broadcasted_iota(jnp.int32, (blocks, HD), 0)
    far = first.astype(jnp.float32) * frequencies[...]
    near = lax.broadcasted_iota(jnp.int32, (BLOCK, HD), 0).astype(jnp.float32) * frequencies[...]
    far_cos[...] = jnp.cos(far)
    far_sin[...] = jnp.sin(far)
    near_cos[...] = jnp.cos(near)
    near_sin[...] = jnp.sin(near)


def finish_kernel(first_tile, tensor_count, model_dim, live, *refs):
    keep, received, far_cos, far_sin, near_cos, near_sin = refs[:6]
    squares, arrived, out = refs[6 : 6 + tensor_count], refs[6 + tensor_count : -2], refs[-1]
    size = out.shape[0]
    values = keep[...].astype(jnp.float32) + received[...].astype(jnp.float32)
    for part in arrived:
        values += part[...].astype(jnp.float32)
    on_diagonal = lax.broadcasted_iota(jnp.int32, (LANES, LANES), 0) == lax.broadcasted_iota(
        jnp.int32, (LANES, LANES), 1
    )
    tile = first_tile + pl.program_id(0)
    columns = []
    for part in range(size // LANES):
        row = pl.ds(tile * (size // LANES) + part, 1)
        totals = functools.reduce(jnp.add, [ref[row, :] for ref in squares])
        columns.append(jnp.sum(jnp.where(on_diagonal, totals, 0.0), axis=1, keepdims=True))
    scales = 1.0 / jnp.sqrt(jnp.concatenate(columns, axis=0) / model_dim + norm_eps)
    row = tile * size + lax.broadcasted_iota(jnp.int32, (size, 1), 0)
    alive = row < live[lax.axis_index("serve")] * BLOCK
    sign = jnp.where(lax.broadcasted_iota(jnp.int32, (1, HD), 1) < HD // 2, -1.0, 1.0)
    cosines, sines = [], []
    for part in range(size // BLOCK):
        block = pl.ds(tile * (size // BLOCK) + part, 1)
        block_cos = far_cos[block, :]
        block_sin = far_sin[block, :]
        cosines.append(block_cos * near_cos[...] - block_sin * near_sin[...])
        sines.append((sign * block_sin) * near_cos[...] + (sign * block_cos) * near_sin[...])
    cosine = jnp.concatenate(cosines, axis=0)
    sine = jnp.concatenate(sines, axis=0)
    for start in range(0, out.shape[1], 2 * HD):
        key = values[:, start : start + HD] * scales
        turned = key * cosine + pltpu.roll(key, HD // 2, 1) * sine
        out[:, start : start + HD] = jnp.where(alive, turned, 0.0).astype(out.dtype)
        value = values[:, start + HD : start + 2 * HD] * scales
        out[:, start + HD : start + 2 * HD] = jnp.where(alive, value, 0.0).astype(out.dtype)


def shards(tokens, norm_gain, kv_weight, live_blocks, span_offset):
    tensor_count = lax.axis_size("tensor")
    serve_count = lax.axis_size("serve")
    chip_count = tensor_count // 2
    slot_rows, depth = tokens.shape
    columns = kv_weight.shape[1] // tensor_count
    units = slot_rows // UNIT
    blocks = slot_rows // BLOCK
    model_dim = depth * tensor_count
    others = range(1, chip_count)
    vmem = pl.BlockSpec(memory_space=pltpu.VMEM)
    smem = pl.BlockSpec(memory_space=pltpu.SMEM)
    hbm = pl.BlockSpec(memory_space=pltpu.HBM)
    hold = lax.optimization_barrier

    third = units // 3
    pair = TILE // UNIT
    first_runs = [(2 * third, third), (0, pair), (2 * third - pair, pair)]
    second_runs = [(pair, 2 * third - 2 * pair)]
    shifts = sorted({1 % serve_count, (serve_count - 1) % serve_count} - {0})
    per_unit = UNIT // BLOCK
    options = [(most * per_unit, shift) for most in (2 * third, 2 * third + 1) for shift in shifts]
    if units != 12:
        options = []

    swap = [(i, i ^ 1) for i in range(tensor_count)]

    def swapped(array):
        return lax.ppermute(array, "tensor", swap)

    def cross(parts):
        return [
            lax.ppermute(part, "tensor", [(i, (i + 2 * step) % tensor_count) for i in range(tensor_count)])
            for step, part in zip(others, parts)
        ]

    def move(parts, shift):
        return [
            lax.ppermute(part, "serve", [(i, (i + shift) % serve_count) for i in range(serve_count)])
            for part in parts
        ]

    def kernel(body, out_shape, in_specs, params=PARAMS, **more):
        return pl.pallas_call(
            body, out_shape=out_shape, in_specs=in_specs, compiler_params=params, cost_estimate=COST, **more
        )

    def bf16(rows, width=columns):
        return jax.ShapeDtypeStruct((rows, width), jnp.bfloat16)

    def product(gain, step, groups, staged=False, with_squares=False):
        rows = [sum(count for _, count in runs) * UNIT for runs in groups]
        out_shape = [bf16(size) for size in rows for _ in range(2)]
        out_specs = [vmem] * len(out_shape)
        if with_squares:
            out_shape.append(jax.ShapeDtypeStruct((slot_rows // LANES, LANES), jnp.float32))
            out_specs.append(vmem)
        more = {}
        if staged:
            out_shape.append(jax.ShapeDtypeStruct((1,), jnp.int32))
            out_specs.append(smem)
            more["scratch_shapes"] = [
                pltpu.VMEM((sum(rows), depth), jnp.bfloat16),
                pltpu.VMEM((depth, 2 * columns), jnp.bfloat16),
                pltpu.VMEM((depth,), jnp.bfloat16),
                pltpu.SMEM((serve_count,), jnp.int32),
                pltpu.SemaphoreType.DMA((4,)),
                pltpu.SemaphoreType.DMA((sum(rows) // UNIT,)),
                pltpu.SemaphoreType.DMA,
                pltpu.SemaphoreType.DMA,
            ]
        body = functools.partial(
            product_kernel, step, chip_count, groups, staged, with_squares, (serve_count, blocks), options
        )
        made = kernel(
            body,
            out_shape,
            [hbm] * 4 if staged else [vmem] * 3,
            FIRST if staged else PARAMS,
            out_specs=out_specs,
            **more,
        )(tokens, gain, kv_weight, *([live_blocks] if staged else []))
        made = list(made)
        extra = made[2 * len(groups) :]
        return list(zip(made[::2], made[1::2]))[: len(groups)], extra

    def add(keep, received, cuts):
        made = [
            kernel(functools.partial(add_kernel, cuts), [bf16(size) for _, size in cuts], [vmem] * 2)(*both)
            for both in zip(keep, received)
        ]
        return [list(parts) for parts in zip(*made)]

    def pick(most, shift, live, guest, own):
        body = functools.partial(pick_kernel, most, shift, serve_count)
        return [kernel(body, bf16(one.shape[0]), [smem, vmem, vmem])(live, *both) for one, *both in
                [(a, a, b) for a, b in zip(guest, own)]]

    def tables(span):
        frequencies = rope_base ** (-(np.arange(HD // 2, dtype=np.float32) * 2.0) / HD)
        frequencies = np.concatenate([frequencies, frequencies])[None, :].astype(np.float32)
        shapes = [(slot_rows // BLOCK, HD)] * 2 + [(BLOCK, HD)] * 2
        out_shape = [jax.ShapeDtypeStruct(shape, jnp.float32) for shape in shapes]
        return list(kernel(table_kernel, out_shape, [smem, vmem])(span, jnp.asarray(frequencies)))

    def own_part(gain, span):
        ((keep, send),), (squares,) = product(gain, 0, [[(0, units)]], with_squares=True)
        squares = [squares] + [
            lax.ppermute(squares, "tensor", [(i, (i + step) % tensor_count) for i in range(tensor_count)])
            for step in range(1, tensor_count)
        ]
        return keep, send, tables(span), squares

    def finish(run, live, own, arrived, result):
        first, count = run
        size = TILE if first % pair == 0 and count % pair == 0 else UNIT
        start = first * UNIT // size
        keep, received, table, squares = own
        operands = [keep, received] + table + squares + arrived
        specs = (
            [pl.BlockSpec((size, columns), lambda i, *_: (start + i, 0))] * 2
            + [pl.BlockSpec((slot_rows // BLOCK, HD), lambda i, *_: (0, 0))] * 2
            + [pl.BlockSpec((BLOCK, HD), lambda i, *_: (0, 0))] * 2
            + [pl.BlockSpec((slot_rows // LANES, LANES), lambda i, *_: (0, 0))] * tensor_count
            + [pl.BlockSpec((size, columns), lambda i, *_: (i, 0))] * len(arrived)
        )
        aliases = {1 + len(operands): 0}
        if result is None:
            result, aliases = keep, {}
        return pl.pallas_call(
            functools.partial(finish_kernel, start, tensor_count, model_dim),
            grid_spec=pltpu.PrefetchScalarGridSpec(
                num_scalar_prefetch=1,
                grid=(count * UNIT // size,),
                in_specs=specs + [pl.BlockSpec(memory_space=pl.ANY)],
                out_specs=pl.BlockSpec((size, columns), lambda i, *_: (start + i, 0)),
            ),
            out_shape=bf16(slot_rows),
            input_output_aliases=aliases,
            compiler_params=PARAMS,
            cost_estimate=COST,
        )(live, *operands, result)

    def rows_of(runs, wanted):
        at = 0
        for first, count in runs:
            if first <= wanted[0] and sum(wanted) <= first + count:
                return (at + wanted[0] - first) * UNIT, wanted[1] * UNIT
            at += count


    def direct(keep, received, second, gain, live, span):
        sums = add(keep, received, [rows_of(first_runs, run) for run in first_runs])
        sums, second, gain, span = hold((sums, second, gain, span))
        arrived = cross(sums[0])
        own = own_part(gain, span)
        arrived, sums, second, own = hold((arrived, sums, second, own))
        late = [cross(part) for part in sums[1:]]
        keep, send = zip(*second)
        (rest,) = add(keep, [swapped(part) for part in send], [rows_of(second_runs, second_runs[0])])
        late.append(cross(rest))
        keep, send, table, squares = own
        own = keep, swapped(send), table, squares
        result = finish(first_runs[0], live, own, arrived, None)
        for run, parts in zip(first_runs[1:] + second_runs, late):
            result = finish(run, live, own, parts, result)
        return result

    def balanced(most, shift, keep, received, second, gain, live, span):
        most_units = most // per_unit
        spare = units - most_units
        early = (0, pair)
        slots = [(2 * third - pair, pair)]
        moved = [(most_units, pair), (most_units + pair, spare - pair)]
        slots.append((most_units - spare, spare - pair) if most_units == 2 * third else (2 * third, spare - pair))
        cuts = [early, slots[0]] + moved
        second_cuts = [(pair, most_units - spare - pair)]
        if most_units == 2 * third:
            second_cuts.append(slots[1])
        else:
            cuts.append(slots[1])

        sums = add(keep, received, [rows_of(first_runs, run) for run in cuts])
        sums, second, gain, span, live = hold((sums, second, gain, span, live))

        out_a = move(sums[2], shift)
        out_b = move(sums[3], shift)
        at_start = cross(sums[0])
        own = own_part(gain, span)
        out_a, at_start, sums, second, own = hold((out_a, at_start, sums, second, own))

        slot_a = cross(pick(most, shift, live, out_a, sums[1]))
        keep, send = zip(*second)
        rest = add(keep, [swapped(part) for part in send], [rows_of(second_runs, run) for run in second_cuts])
        out_b, rest, own = hold((out_b, rest, own))

        slot_b = cross(pick(most, shift, live, out_b, rest[1] if len(rest) > 1 else sums[4]))
        at_end = cross(rest[0])
        keep, send, table, squares = own
        own = keep, swapped(send), table, squares
        slot_a, own = hold((slot_a, own))

        back_a = move(slot_a, -shift)
        result = finish(early, live, own, at_start, None)
        slot_b, result = hold((slot_b, result))

        back_b = move(slot_b, -shift)
        result = finish(slots[0], live, own, slot_a, result)
        result = finish(slots[1], live, own, slot_b, result)
        result = finish(moved[0], live, own, back_a, result)
        result = finish(second_cuts[0], live, own, at_end, result)
        return finish(moved[1], live, own, back_b, result)

    keep, send = [], []
    for step in others:
        ((near, far),), extra = product(norm_gain, step, [first_runs], staged=True)
        keep.append(near)
        send.append(far)
    choice = extra[0]
    send, gain, choice = hold((send, norm_gain, choice))
    received = [swapped(part) for part in send]
    second = [product(gain, step, [second_runs])[0][0] for step in others]
    received, second, gain, span, live = hold((received, second, gain, span_offset, live_blocks))
    branches = [functools.partial(balanced, most, shift) for most, shift in options] + [direct]
    if len(branches) == 1:
        return direct(keep, received, second, gain, live, span)
    return lax.switch(choice[0], branches, keep, received, second, gain, live, span)


def solution(mesh):
    in_specs = (
        P(("groups", "serve"), "tensor"),
        P("tensor"),
        P("tensor", None),
        P("groups"),
        P("groups"),
    )
    out_specs = P(("groups", "serve"), "tensor")
    return jax.shard_map(shards, mesh=mesh, in_specs=in_specs, out_specs=out_specs, check_vma=False)
```

```python
import functools

import jax
import jax.numpy as jnp
import numpy as np
from jax import lax
from jax.experimental import pallas as pl
from jax.experimental.pallas import tpu as pltpu
from jax.sharding import PartitionSpec as P

HD = 128
PAGE = 256
BLOCK = 64
LANES = 128

rope_base = 500000.0
norm_eps = 1e-05

TILE = 256
CHUNKS = (2, 3, 1)

PARAMS = pltpu.CompilerParams(vmem_limit_bytes=16 * 1024 * 1024)
FIRST = pltpu.CompilerParams(vmem_limit_bytes=56 * 1024 * 1024)
COST = pl.CostEstimate(flops=1, bytes_accessed=1, transcendentals=0)


def square_sums(rows):
    total = jnp.zeros((rows.shape[0], LANES), jnp.float32)
    for part in range(rows.shape[1] // LANES):
        wide = rows[:, part * LANES : (part + 1) * LANES].astype(jnp.float32)
        total += wide * wide
    return total


def product_kernel(step, chip_count, chunks, staged, with_squares, tokens, gain, weight, *refs):
    refs = list(refs)
    outs = [refs.pop(0) for _ in range(2 * len(chunks))]
    squares = refs.pop(0) if with_squares else None
    depth, width = tokens.shape[1], 2 * outs[0].shape[1]
    me = lax.axis_index("tensor")
    core = lax.rem(me, 2)
    chip = lax.rem(lax.div(me, 2) + step, chip_count)
    place = pl.ds(pl.multiple_of(chip * width, width), width)

    weight_copies, row_copies = [], {}
    if staged:
        rows_buf, weight_buf, gain_buf, weight_sems, row_sems, gain_sem = refs
        cuts = weight_sems.shape[0]
        cut = depth // cuts
        gain_copy = pltpu.make_async_copy(gain, gain_buf, gain_sem)
        weight_copies = [
            pltpu.make_async_copy(
                weight.at[pl.ds(index * cut, cut), place],
                weight_buf.at[pl.ds(index * cut, cut), :],
                weight_sems.at[index],
            )
            for index in range(cuts)
        ]
        at = 0
        for first, count in chunks:
            for tile in range(first, first + count):
                buf = rows_buf.at[pl.ds(at * TILE, TILE), :]
                row_copies[tile] = (
                    pltpu.make_async_copy(tokens.at[pl.ds(tile * TILE, TILE), :], buf, row_sems.at[at]),
                    buf,
                )
                at += 1
        in_order = [copy for copy, _ in row_copies.values()]
        for copy in [gain_copy] + in_order[:1] + weight_copies + in_order[1:]:
            copy.start()
        gain_copy.wait()
        gains = gain_buf[...].reshape(1, depth)
    else:
        gains = gain[...].reshape(1, depth)

    for index, (first, count) in enumerate(chunks):
        for tile in range(first, first + count):
            if staged:
                row_copies[tile][0].wait()
                rows = row_copies[tile][1][...]
            else:
                rows = tokens[pl.ds(tile * TILE, TILE), :]
            scaled = rows * gains
            if weight_copies:
                product = jnp.zeros((TILE, width), jnp.float32)
                for part, copy in enumerate(weight_copies):
                    copy.wait()
                    span = slice(part * cut, (part + 1) * cut)
                    product += jnp.dot(
                        scaled[:, span], weight_buf[span, :], preferred_element_type=jnp.float32
                    )
                weight_copies = []
            else:
                columns = weight_buf[...] if staged else weight[:, place]
                product = jnp.dot(scaled, columns, preferred_element_type=jnp.float32)
            left = product[:, : width // 2].astype(jnp.bfloat16)
            right = product[:, width // 2 :].astype(jnp.bfloat16)
            inside = pl.ds((tile - first) * TILE, TILE)
            outs[2 * index][inside, :] = jnp.where(core == 0, left, right)
            outs[2 * index + 1][inside, :] = jnp.where(core == 0, right, left)
            if with_squares:
                total = square_sums(rows)
                for part in range(TILE // LANES):
                    turned = jnp.transpose(total[part * LANES : (part + 1) * LANES])
                    row = tile * (TILE // LANES) + part
                    squares[row : row + 1, :] = jnp.sum(turned, axis=0, keepdims=True)


def add_kernel(keep, received, out):
    out[...] = (keep[...].astype(jnp.float32) + received[...].astype(jnp.float32)).astype(out.dtype)


def table_kernel(span, frequencies, far_cos, far_sin, near_cos, near_sin):
    blocks = far_cos.shape[0]
    start = span[lax.axis_index("serve")] * PAGE
    first = start + BLOCK * lax.broadcasted_iota(jnp.int32, (blocks, HD), 0)
    far = first.astype(jnp.float32) * frequencies[...]
    near = lax.broadcasted_iota(jnp.int32, (BLOCK, HD), 0).astype(jnp.float32) * frequencies[...]
    far_cos[...] = jnp.cos(far)
    far_sin[...] = jnp.sin(far)
    near_cos[...] = jnp.cos(near)
    near_sin[...] = jnp.sin(near)


def finish_kernel(first, count, tensor_count, model_dim, *refs):
    live, keep, received, far_cos, far_sin, near_cos, near_sin = refs[:7]
    squares, arrived = refs[7 : 7 + tensor_count], refs[7 + tensor_count : -4]
    out, staged, sems = refs[-3:]
    on_diagonal = lax.broadcasted_iota(jnp.int32, (LANES, LANES), 0) == lax.broadcasted_iota(
        jnp.int32, (LANES, LANES), 1
    )
    sign = jnp.where(lax.broadcasted_iota(jnp.int32, (1, HD), 1) < HD // 2, -1.0, 1.0)
    live_rows = live[lax.axis_index("serve")] * BLOCK
    copies = []
    for index in range(count):
        start = (first + index) * TILE
        rows, inside = pl.ds(start, TILE), pl.ds(index * TILE, TILE)
        values = keep[rows, :].astype(jnp.float32) + received[rows, :].astype(jnp.float32)
        for part in arrived:
            values += part[inside, :].astype(jnp.float32)
        columns = []
        for row in range(start // LANES, (start + TILE) // LANES):
            totals = functools.reduce(jnp.add, [ref[row : row + 1, :] for ref in squares])
            columns.append(jnp.sum(jnp.where(on_diagonal, totals, 0.0), axis=1, keepdims=True))
        scales = 1.0 / jnp.sqrt(jnp.concatenate(columns, axis=0) / model_dim + norm_eps)
        alive = start + lax.broadcasted_iota(jnp.int32, (TILE, 1), 0) < live_rows
        cosines, sines = [], []
        for block in range(start // BLOCK, (start + TILE) // BLOCK):
            block_cos = far_cos[block : block + 1, :]
            block_sin = far_sin[block : block + 1, :]
            cosines.append(block_cos * near_cos[...] - block_sin * near_sin[...])
            sines.append((sign * block_sin) * near_cos[...] + (sign * block_cos) * near_sin[...])
        cosine = jnp.concatenate(cosines, axis=0)
        sine = jnp.concatenate(sines, axis=0)
        for low in range(0, out.shape[1], 2 * HD):
            key = values[:, low : low + HD] * scales
            turned = key * cosine + pltpu.roll(key, HD // 2, 1) * sine
            staged[inside, low : low + HD] = jnp.where(alive, turned, 0.0).astype(out.dtype)
            value = values[:, low + HD : low + 2 * HD] * scales
            staged[inside, low + HD : low + 2 * HD] = jnp.where(alive, value, 0.0).astype(out.dtype)
        copies.append(pltpu.make_async_copy(staged.at[inside, :], out.at[rows, :], sems.at[index]))
        copies[-1].start()
    for copy in copies:
        copy.wait()


def shards(tokens, norm_gain, kv_weight, live_blocks, span_offset):
    tensor_count = lax.axis_size("tensor")
    chip_count = tensor_count // 2
    me = lax.axis_index("tensor")
    slot_rows, depth = tokens.shape
    columns = kv_weight.shape[1] // tensor_count
    tiles = slot_rows // TILE
    model_dim = depth * tensor_count

    swap = [(i, i ^ 1) for i in range(tensor_count)]

    def shift(step):
        return [(i, (i + 2 * step) % tensor_count) for i in range(tensor_count)]

    def product(gain, step, chunks, staged=False, with_squares=False):
        vmem = pl.BlockSpec(memory_space=pltpu.VMEM)
        out_shape = [
            jax.ShapeDtypeStruct((count * TILE, columns), jnp.bfloat16) for _, count in chunks for _ in range(2)
        ]
        if with_squares:
            out_shape.append(jax.ShapeDtypeStruct((slot_rows // LANES, LANES), jnp.float32))
        count = sum(count for _, count in chunks)
        scratch = [
            pltpu.VMEM((count * TILE, depth), jnp.bfloat16),
            pltpu.VMEM((depth, 2 * columns), jnp.bfloat16),
            pltpu.VMEM((depth,), jnp.bfloat16),
            pltpu.SemaphoreType.DMA((4,)),
            pltpu.SemaphoreType.DMA((count,)),
            pltpu.SemaphoreType.DMA,
        ]
        made = pl.pallas_call(
            functools.partial(product_kernel, step, chip_count, chunks, staged, with_squares),
            in_specs=[pl.BlockSpec(memory_space=pltpu.HBM) if staged else vmem] * 3,
            out_shape=out_shape,
            out_specs=[vmem] * len(out_shape),
            scratch_shapes=scratch if staged else [],
            compiler_params=FIRST if staged else PARAMS,
            cost_estimate=COST,
        )(tokens, gain, kv_weight)
        made = list(made)
        squares = made.pop() if with_squares else None
        return list(zip(made[::2], made[1::2])), squares

    def tables(span_offset):
        frequencies = rope_base ** (-(np.arange(HD // 2, dtype=np.float32) * 2.0) / HD)
        frequencies = np.concatenate([frequencies, frequencies])[None, :].astype(np.float32)
        shapes = [(slot_rows // BLOCK, HD)] * 2 + [(BLOCK, HD)] * 2
        made = pl.pallas_call(
            table_kernel,
            in_specs=[pl.BlockSpec(memory_space=pltpu.SMEM), pl.BlockSpec(memory_space=pltpu.VMEM)],
            out_shape=[jax.ShapeDtypeStruct(shape, jnp.float32) for shape in shapes],
            out_specs=[pl.BlockSpec(memory_space=pltpu.VMEM)] * 4,
            compiler_params=PARAMS,
            cost_estimate=COST,
        )(span_offset, jnp.asarray(frequencies))
        return list(made)

    def finish(first, count, keep, received, table, squares, arrived, result):
        vmem = pl.BlockSpec(memory_space=pltpu.VMEM)
        operands = [live_blocks, keep, received] + table + squares + arrived
        aliases = {len(operands): 0}
        if result is None:
            result, aliases = jnp.zeros((1,), jnp.bfloat16), {}
        return pl.pallas_call(
            functools.partial(finish_kernel, first, count, tensor_count, model_dim),
            in_specs=[pl.BlockSpec(memory_space=pltpu.SMEM)]
            + [vmem] * (len(operands) - 1)
            + [pl.BlockSpec(memory_space=pl.ANY)],
            out_shape=jax.ShapeDtypeStruct((slot_rows, columns), jnp.bfloat16),
            out_specs=pl.BlockSpec(memory_space=pltpu.HBM),
            scratch_shapes=[pltpu.VMEM((count * TILE, columns), jnp.bfloat16), pltpu.SemaphoreType.DMA((count,))],
            input_output_aliases=aliases,
            compiler_params=PARAMS,
            cost_estimate=COST,
        )(*operands, result)

    others = range(1, chip_count)
    firsts = [sum(CHUNKS[:index]) for index in range(len(CHUNKS))]
    chunk_count = len(CHUNKS)

    def start_chunk(gain, index, staged=False):
        made = []
        for step in others:
            made += product(gain, step, [(firsts[index], CHUNKS[index])], staged)[0]
        return made

    def add_halves(made):
        return [
            pl.pallas_call(
                add_kernel,
                out_shape=jax.ShapeDtypeStruct(keep.shape, keep.dtype),
                compiler_params=PARAMS,
                cost_estimate=COST,
            )(keep, lax.ppermute(send, "tensor", swap))
            for keep, send in made
        ]

    def cross(sums):
        return [lax.ppermute(part, "tensor", shift(step)) for step, part in zip(others, sums)]

    hold = lax.optimization_barrier
    made = start_chunk(norm_gain, 0, staged=True)
    made, gain = hold((made, norm_gain))
    sums = add_halves(made)
    made = start_chunk(gain, 1)
    sums, made, gain, span_offset = hold((sums, made, gain, span_offset))

    arrived = cross(sums)
    sums = add_halves(made)
    waiting = [start_chunk(gain, index) for index in range(2, chunk_count)]
    ((keep, send),), squares = product(gain, 0, [(0, tiles)], with_squares=True)
    squares = [squares] + [
        lax.ppermute(squares, "tensor", [(i, (i + step) % tensor_count) for i in range(tensor_count)])
        for step in range(1, tensor_count)
    ]
    table = tables(span_offset)
    arrived, sums, waiting, keep, send, squares, table = hold(
        (arrived, sums, waiting, keep, send, squares, table)
    )

    arrivals = [arrived, cross(sums)] + [cross(add_halves(made)) for made in waiting]
    received = lax.ppermute(send, "tensor", swap)
    result = None
    for index in range(chunk_count):
        result = finish(
            firsts[index], CHUNKS[index], keep, received, table, squares, arrivals[index], result
        )
    return result


def solution(mesh):
    in_specs = (
        P(("groups", "serve"), "tensor"),
        P("tensor"),
        P("tensor", None),
        P("groups"),
        P("groups"),
    )
    out_specs = P(("groups", "serve"), "tensor")
    return jax.shard_map(shards, mesh=mesh, in_specs=in_specs, out_specs=out_specs, check_vma=False)
```

```python
import functools

import jax
import jax.numpy as jnp
import numpy as np
from jax import lax
from jax.experimental import pallas as pl
from jax.experimental.pallas import tpu as pltpu
from jax.sharding import PartitionSpec as P

HD = 128
PAGE = 256
BLOCK = 64
LANES = 128

rope_base = 500000.0
norm_eps = 1e-05

TILE = 256
CHUNKS = (2, 3, 1)

PARAMS = pltpu.CompilerParams(vmem_limit_bytes=16 * 1024 * 1024)
FIRST = pltpu.CompilerParams(vmem_limit_bytes=56 * 1024 * 1024)
COST = pl.CostEstimate(flops=1, bytes_accessed=1, transcendentals=0)


def square_sums(rows):
    total = jnp.zeros((rows.shape[0], LANES), jnp.float32)
    for part in range(rows.shape[1] // LANES):
        wide = rows[:, part * LANES : (part + 1) * LANES].astype(jnp.float32)
        total += wide * wide
    return total


def product_kernel(step, chip_count, first, count, staged, with_squares, tokens, gain, weight, *refs):
    keep, send = refs[:2]
    squares = refs[2] if with_squares else None
    depth, width = tokens.shape[1], 2 * keep.shape[1]
    me = lax.axis_index("tensor")
    core = lax.rem(me, 2)
    chip = lax.rem(lax.div(me, 2) + step, chip_count)
    place = pl.ds(pl.multiple_of(chip * width, width), width)

    def split(product, inside):
        left = product[:, : width // 2].astype(jnp.bfloat16)
        right = product[:, width // 2 :].astype(jnp.bfloat16)
        keep[inside, :] = jnp.where(core == 0, left, right)
        send[inside, :] = jnp.where(core == 0, right, left)

    if staged:
        rows_buf, weight_buf, gain_buf, total, weight_sems, row_sem, gain_sem = refs[2:]
        cuts = weight_sems.shape[0]
        cut = depth // cuts
        gain_copy = pltpu.make_async_copy(gain, gain_buf, gain_sem)
        row_copy = pltpu.make_async_copy(tokens.at[pl.ds(first * TILE, count * TILE), :], rows_buf, row_sem)
        weight_copies = [
            pltpu.make_async_copy(
                weight.at[pl.ds(index * cut, cut), place],
                weight_buf.at[pl.ds(index * cut, cut), :],
                weight_sems.at[index],
            )
            for index in range(cuts)
        ]
        for copy in [gain_copy, row_copy] + weight_copies:
            copy.start()
        gain_copy.wait()
        row_copy.wait()
        gains = gain_buf[...].reshape(1, depth)

        @pl.loop(0, count * TILE // BLOCK)
        def _(block):
            inside = pl.ds(pl.multiple_of(block * BLOCK, BLOCK), BLOCK)
            rows_buf[inside, :] = rows_buf[inside, :] * gains

        for index, copy in enumerate(weight_copies):
            copy.wait()
            span = slice(index * cut, (index + 1) * cut)

            @pl.loop(0, count)
            def _(tile):
                inside = pl.ds(pl.multiple_of(tile * TILE, TILE), TILE)
                part = jnp.dot(rows_buf[inside, span], weight_buf[span, :], preferred_element_type=jnp.float32)
                if index:
                    part += total[inside, :]
                if index + 1 < cuts:
                    total[inside, :] = part
                else:
                    split(part, inside)

        return

    gains = gain[...].reshape(1, depth)

    @pl.loop(0, count)
    def _(tile):
        source = pl.multiple_of((first + tile) * TILE, TILE)
        rows = tokens[pl.ds(source, TILE), :]
        split(
            jnp.dot(rows * gains, weight[:, place], preferred_element_type=jnp.float32),
            pl.ds(pl.multiple_of(tile * TILE, TILE), TILE),
        )
        if with_squares:
            for part in range(TILE // LANES):
                sums = square_sums(rows[part * LANES : (part + 1) * LANES])
                row = (first + tile) * (TILE // LANES) + part
                squares[pl.ds(row, 1), :] = jnp.sum(jnp.transpose(sums), axis=0, keepdims=True)


def add_kernel(keep, received, out):
    out[...] = (keep[...].astype(jnp.float32) + received[...].astype(jnp.float32)).astype(out.dtype)


def table_kernel(live, span, frequencies, limit, far_cos, far_sin, near_cos, near_sin):
    limit[...] = jnp.full(limit.shape, live[lax.axis_index("serve")] * BLOCK, jnp.int32)
    blocks = far_cos.shape[0]
    start = span[lax.axis_index("serve")] * PAGE
    first = start + BLOCK * lax.broadcasted_iota(jnp.int32, (blocks, HD), 0)
    far = first.astype(jnp.float32) * frequencies[...]
    near = lax.broadcasted_iota(jnp.int32, (BLOCK, HD), 0).astype(jnp.float32) * frequencies[...]
    far_cos[...] = jnp.cos(far)
    far_sin[...] = jnp.sin(far)
    near_cos[...] = jnp.cos(near)
    near_sin[...] = jnp.sin(near)


def finish_kernel(first, count, tensor_count, model_dim, *refs):
    keep, received, limit, far_cos, far_sin, near_cos, near_sin = refs[:7]
    squares, arrived = refs[7 : 7 + tensor_count], refs[7 + tensor_count : -4]
    out, staged, sems = refs[-3:]
    blocks = count * TILE // BLOCK
    first_block = first * TILE // BLOCK
    shape = (BLOCK, LANES)
    sign = jnp.where(lax.broadcasted_iota(jnp.int32, (1, HD), 1) < HD // 2, -1.0, 1.0)

    def copy_of(index):
        inside = pl.ds(pl.multiple_of(index * BLOCK, BLOCK), BLOCK)
        rows = pl.ds(pl.multiple_of((first_block + index) * BLOCK, BLOCK), BLOCK)
        return pltpu.make_async_copy(staged.at[inside, :], out.at[rows, :], sems.at[index])

    @pl.loop(0, blocks)
    def _(index):
        block = first_block + index
        start = pl.multiple_of(block * BLOCK, BLOCK)
        rows, inside = pl.ds(start, BLOCK), pl.ds(pl.multiple_of(index * BLOCK, BLOCK), BLOCK)
        values = keep[rows, :].astype(jnp.float32) + received[rows, :].astype(jnp.float32)
        for part in arrived:
            values += part[inside, :].astype(jnp.float32)
        line = lax.rem(start, LANES) + lax.broadcasted_iota(jnp.int32, shape, 0)
        totals = functools.reduce(jnp.add, [ref[pl.ds(lax.div(start, LANES), 1), :] for ref in squares])
        picked = jnp.where(line == lax.broadcasted_iota(jnp.int32, shape, 1), totals, 0.0)
        scales = 1.0 / jnp.sqrt(jnp.sum(picked, axis=1, keepdims=True) / model_dim + norm_eps)
        alive = start + lax.broadcasted_iota(jnp.int32, shape, 0) < limit[0:1, :]
        block_cos = far_cos[pl.ds(block, 1), :]
        block_sin = far_sin[pl.ds(block, 1), :]
        cosine = block_cos * near_cos[...] - block_sin * near_sin[...]
        sine = (sign * block_sin) * near_cos[...] + (sign * block_cos) * near_sin[...]
        for low in range(0, out.shape[1], 2 * HD):
            key = values[:, low : low + HD] * scales
            turned = key * cosine + pltpu.roll(key, HD // 2, 1) * sine
            staged[inside, low : low + HD] = jnp.where(alive, turned, 0.0).astype(out.dtype)
            value = values[:, low + HD : low + 2 * HD] * scales
            staged[inside, low + HD : low + 2 * HD] = jnp.where(alive, value, 0.0).astype(out.dtype)
        copy_of(index).start()

    @pl.loop(0, blocks)
    def _(index):
        copy_of(index).wait()


def shards(tokens, norm_gain, kv_weight, live_blocks, span_offset):
    tensor_count = lax.axis_size("tensor")
    chip_count = tensor_count // 2
    me = lax.axis_index("tensor")
    slot_rows, depth = tokens.shape
    columns = kv_weight.shape[1] // tensor_count
    tiles = slot_rows // TILE
    model_dim = depth * tensor_count

    swap = [(i, i ^ 1) for i in range(tensor_count)]

    def shift(step):
        return [(i, (i + 2 * step) % tensor_count) for i in range(tensor_count)]

    def product(gain, step, first, count, staged=False, with_squares=False):
        vmem = pl.BlockSpec(memory_space=pltpu.VMEM)
        out_shape = [jax.ShapeDtypeStruct((count * TILE, columns), jnp.bfloat16)] * 2
        if with_squares:
            out_shape.append(jax.ShapeDtypeStruct((slot_rows // LANES, LANES), jnp.float32))
        scratch = [
            pltpu.VMEM((count * TILE, depth), jnp.bfloat16),
            pltpu.VMEM((depth, 2 * columns), jnp.bfloat16),
            pltpu.VMEM((depth,), jnp.bfloat16),
            pltpu.VMEM((count * TILE, 2 * columns), jnp.float32),
            pltpu.SemaphoreType.DMA((4,)),
            pltpu.SemaphoreType.DMA,
            pltpu.SemaphoreType.DMA,
        ]
        return pl.pallas_call(
            functools.partial(product_kernel, step, chip_count, first, count, staged, with_squares),
            in_specs=[pl.BlockSpec(memory_space=pltpu.HBM) if staged else vmem] * 3,
            out_shape=out_shape,
            out_specs=[vmem] * len(out_shape),
            scratch_shapes=scratch if staged else [],
            compiler_params=FIRST if staged else PARAMS,
            cost_estimate=COST,
        )(tokens, gain, kv_weight)

    def tables(span_offset):
        frequencies = rope_base ** (-(np.arange(HD // 2, dtype=np.float32) * 2.0) / HD)
        frequencies = np.concatenate([frequencies, frequencies])[None, :].astype(np.float32)
        shapes = [(slot_rows // BLOCK, HD)] * 2 + [(BLOCK, HD)] * 2
        made = pl.pallas_call(
            table_kernel,
            in_specs=[pl.BlockSpec(memory_space=pltpu.SMEM)] * 2 + [pl.BlockSpec(memory_space=pltpu.VMEM)],
            out_shape=[jax.ShapeDtypeStruct((8, LANES), jnp.int32)]
            + [jax.ShapeDtypeStruct(shape, jnp.float32) for shape in shapes],
            out_specs=[pl.BlockSpec(memory_space=pltpu.VMEM)] * 5,
            compiler_params=PARAMS,
            cost_estimate=COST,
        )(live_blocks, span_offset, jnp.asarray(frequencies))
        return list(made)

    def finish(first, count, keep, received, table, squares, arrived, result):
        vmem = pl.BlockSpec(memory_space=pltpu.VMEM)
        operands = [keep, received] + table + squares + arrived
        aliases = {len(operands): 0}
        if result is None:
            result, aliases = jnp.zeros((1,), jnp.bfloat16), {}
        return pl.pallas_call(
            functools.partial(finish_kernel, first, count, tensor_count, model_dim),
            in_specs=[vmem] * len(operands) + [pl.BlockSpec(memory_space=pl.ANY)],
            out_shape=jax.ShapeDtypeStruct((slot_rows, columns), jnp.bfloat16),
            out_specs=pl.BlockSpec(memory_space=pltpu.HBM),
            scratch_shapes=[pltpu.VMEM((count * TILE, columns), jnp.bfloat16), pltpu.SemaphoreType.DMA((count * TILE // BLOCK,))],
            input_output_aliases=aliases,
            compiler_params=PARAMS,
            cost_estimate=COST,
        )(*operands, result)

    others = range(1, chip_count)
    firsts = [sum(CHUNKS[:index]) for index in range(len(CHUNKS))]
    chunk_count = len(CHUNKS)

    def start_chunk(gain, index, staged=False):
        made = []
        for step in others:
            made.append(product(gain, step, firsts[index], CHUNKS[index], staged))
        return made

    def add_halves(made):
        return [
            pl.pallas_call(
                add_kernel,
                out_shape=jax.ShapeDtypeStruct(keep.shape, keep.dtype),
                compiler_params=PARAMS,
                cost_estimate=COST,
            )(keep, lax.ppermute(send, "tensor", swap))
            for keep, send in made
        ]

    def cross(sums):
        return [lax.ppermute(part, "tensor", shift(step)) for step, part in zip(others, sums)]

    hold = lax.optimization_barrier
    made = start_chunk(norm_gain, 0, staged=True)
    made, gain = hold((made, norm_gain))
    sums = add_halves(made)
    made = start_chunk(gain, 1)
    sums, made, gain, span_offset = hold((sums, made, gain, span_offset))

    arrived = cross(sums)
    sums = add_halves(made)
    waiting = [start_chunk(gain, index) for index in range(2, chunk_count)]
    keep, send, squares = product(gain, 0, 0, tiles, with_squares=True)
    squares = [squares] + [
        lax.ppermute(squares, "tensor", [(i, (i + step) % tensor_count) for i in range(tensor_count)])
        for step in range(1, tensor_count)
    ]
    table = tables(span_offset)
    arrived, sums, waiting, keep, send, squares, table = hold(
        (arrived, sums, waiting, keep, send, squares, table)
    )

    arrivals = [arrived, cross(sums)] + [cross(add_halves(made)) for made in waiting]
    received = lax.ppermute(send, "tensor", swap)
    result = None
    for index in range(chunk_count):
        result = finish(
            firsts[index], CHUNKS[index], keep, received, table, squares, arrivals[index], result
        )
    return result


def solution(mesh):
    in_specs = (
        P(("groups", "serve"), "tensor"),
        P("tensor"),
        P("tensor", None),
        P("groups"),
        P("groups"),
    )
    out_specs = P(("groups", "serve"), "tensor")
    return jax.shard_map(shards, mesh=mesh, in_specs=in_specs, out_specs=out_specs, check_vma=False)
```

```python
import functools

import jax
import jax.numpy as jnp
import numpy as np
from jax import lax
from jax.experimental import pallas as pl
from jax.experimental.pallas import tpu as pltpu
from jax.sharding import PartitionSpec as P

HD = 128
PAGE = 256
BLOCK = 64
LANES = 128

rope_base = 500000.0
norm_eps = 1e-05

TILE = 256
CHUNKS = (2, 2, 2)

PARAMS = pltpu.CompilerParams(vmem_limit_bytes=16 * 1024 * 1024)
FIRST = pltpu.CompilerParams(vmem_limit_bytes=56 * 1024 * 1024)
COST = pl.CostEstimate(flops=1, bytes_accessed=1, transcendentals=0)


def square_sums(rows):
    total = jnp.zeros((rows.shape[0], LANES), jnp.float32)
    for part in range(rows.shape[1] // LANES):
        wide = rows[:, part * LANES : (part + 1) * LANES].astype(jnp.float32)
        total += wide * wide
    return total


def product_kernel(step, chip_count, chunks, staged, with_squares, tokens, gain, weight, *refs):
    refs = list(refs)
    outs = [refs.pop(0) for _ in range(2 * len(chunks))]
    squares = refs.pop(0) if with_squares else None
    depth, width = tokens.shape[1], 2 * outs[0].shape[1]
    me = lax.axis_index("tensor")
    core = lax.rem(me, 2)
    chip = lax.rem(lax.div(me, 2) + step, chip_count)
    place = pl.ds(pl.multiple_of(chip * width, width), width)

    weight_copies, row_copies = [], {}
    if staged:
        rows_buf, weight_buf, gain_buf, weight_sems, row_sems, gain_sem = refs
        cuts = weight_sems.shape[0]
        cut = depth // cuts
        gain_copy = pltpu.make_async_copy(gain, gain_buf, gain_sem)
        weight_copies = [
            pltpu.make_async_copy(
                weight.at[pl.ds(index * cut, cut), place],
                weight_buf.at[pl.ds(index * cut, cut), :],
                weight_sems.at[index],
            )
            for index in range(cuts)
        ]
        at = 0
        for first, count in chunks:
            for tile in range(first, first + count):
                buf = rows_buf.at[pl.ds(at * TILE, TILE), :]
                row_copies[tile] = (
                    pltpu.make_async_copy(tokens.at[pl.ds(tile * TILE, TILE), :], buf, row_sems.at[at]),
                    buf,
                )
                at += 1
        in_order = [copy for copy, _ in row_copies.values()]
        for copy in [gain_copy] + in_order[:1] + weight_copies + in_order[1:]:
            copy.start()
        gain_copy.wait()
        gains = gain_buf[...].reshape(1, depth)
    else:
        gains = gain[...].reshape(1, depth)

    for index, (first, count) in enumerate(chunks):
        for tile in range(first, first + count):
            if staged:
                row_copies[tile][0].wait()
                rows = row_copies[tile][1][...]
            else:
                rows = tokens[pl.ds(tile * TILE, TILE), :]
            scaled = rows * gains
            if weight_copies:
                product = jnp.zeros((TILE, width), jnp.float32)
                for part, copy in enumerate(weight_copies):
                    copy.wait()
                    span = slice(part * cut, (part + 1) * cut)
                    product += jnp.dot(
                        scaled[:, span], weight_buf[span, :], preferred_element_type=jnp.float32
                    )
                weight_copies = []
            else:
                columns = weight_buf[...] if staged else weight[:, place]
                product = jnp.dot(scaled, columns, preferred_element_type=jnp.float32)
            left = product[:, : width // 2].astype(jnp.bfloat16)
            right = product[:, width // 2 :].astype(jnp.bfloat16)
            inside = pl.ds((tile - first) * TILE, TILE)
            outs[2 * index][inside, :] = jnp.where(core == 0, left, right)
            outs[2 * index + 1][inside, :] = jnp.where(core == 0, right, left)
            if with_squares:
                total = square_sums(rows)
                for part in range(TILE // LANES):
                    turned = jnp.transpose(total[part * LANES : (part + 1) * LANES])
                    row = tile * (TILE // LANES) + part
                    squares[row : row + 1, :] = jnp.sum(turned, axis=0, keepdims=True)


def add_kernel(keep, received, out):
    out[...] = (keep[...].astype(jnp.float32) + received[...].astype(jnp.float32)).astype(out.dtype)


def table_kernel(live, span, frequencies, limit, far_cos, far_sin, near_cos, near_sin):
    limit[...] = jnp.full(limit.shape, live[lax.axis_index("serve")] * BLOCK, jnp.int32)
    blocks = far_cos.shape[0]
    start = span[lax.axis_index("serve")] * PAGE
    first = start + BLOCK * lax.broadcasted_iota(jnp.int32, (blocks, HD), 0)
    far = first.astype(jnp.float32) * frequencies[...]
    near = lax.broadcasted_iota(jnp.int32, (BLOCK, HD), 0).astype(jnp.float32) * frequencies[...]
    far_cos[...] = jnp.cos(far)
    far_sin[...] = jnp.sin(far)
    near_cos[...] = jnp.cos(near)
    near_sin[...] = jnp.sin(near)


def finish_kernel(first, count, tensor_count, model_dim, *refs):
    keep, received, limit, far_cos, far_sin, near_cos, near_sin = refs[:7]
    squares, arrived = refs[7 : 7 + tensor_count], refs[7 + tensor_count : -4]
    out, staged, sems = refs[-3:]
    on_diagonal = lax.broadcasted_iota(jnp.int32, (LANES, LANES), 0) == lax.broadcasted_iota(
        jnp.int32, (LANES, LANES), 1
    )
    sign = jnp.where(lax.broadcasted_iota(jnp.int32, (1, HD), 1) < HD // 2, -1.0, 1.0)
    copies = []
    for index in range(count):
        start = (first + index) * TILE
        rows, inside = pl.ds(start, TILE), pl.ds(index * TILE, TILE)
        values = keep[inside, :].astype(jnp.float32) + received[inside, :].astype(jnp.float32)
        for part in arrived:
            values += part[inside, :].astype(jnp.float32)
        columns = []
        for row in range(start // LANES, (start + TILE) // LANES):
            totals = functools.reduce(jnp.add, [ref[row : row + 1, :] for ref in squares])
            columns.append(jnp.sum(jnp.where(on_diagonal, totals, 0.0), axis=1, keepdims=True))
        scales = 1.0 / jnp.sqrt(jnp.concatenate(columns, axis=0) / model_dim + norm_eps)
        alive = start + lax.broadcasted_iota(jnp.int32, (TILE, LANES), 0) < limit[0:1, :]
        cosines, sines = [], []
        for block in range(start // BLOCK, (start + TILE) // BLOCK):
            block_cos = far_cos[block : block + 1, :]
            block_sin = far_sin[block : block + 1, :]
            cosines.append(block_cos * near_cos[...] - block_sin * near_sin[...])
            sines.append((sign * block_sin) * near_cos[...] + (sign * block_cos) * near_sin[...])
        cosine = jnp.concatenate(cosines, axis=0)
        sine = jnp.concatenate(sines, axis=0)
        for low in range(0, out.shape[1], 2 * HD):
            key = values[:, low : low + HD] * scales
            turned = key * cosine + pltpu.roll(key, HD // 2, 1) * sine
            staged[inside, low : low + HD] = jnp.where(alive, turned, 0.0).astype(out.dtype)
            value = values[:, low + HD : low + 2 * HD] * scales
            staged[inside, low + HD : low + 2 * HD] = jnp.where(alive, value, 0.0).astype(out.dtype)
        copies.append(pltpu.make_async_copy(staged.at[inside, :], out.at[rows, :], sems.at[index]))
        copies[-1].start()
    for copy in copies:
        copy.wait()


def shards(tokens, norm_gain, kv_weight, live_blocks, span_offset):
    tensor_count = lax.axis_size("tensor")
    chip_count = tensor_count // 2
    me = lax.axis_index("tensor")
    slot_rows, depth = tokens.shape
    columns = kv_weight.shape[1] // tensor_count
    tiles = slot_rows // TILE
    model_dim = depth * tensor_count

    swap = [(i, i ^ 1) for i in range(tensor_count)]

    def shift(step):
        return [(i, (i + 2 * step) % tensor_count) for i in range(tensor_count)]

    def product(gain, step, chunks, staged=False, with_squares=False):
        vmem = pl.BlockSpec(memory_space=pltpu.VMEM)
        out_shape = [
            jax.ShapeDtypeStruct((count * TILE, columns), jnp.bfloat16) for _, count in chunks for _ in range(2)
        ]
        if with_squares:
            out_shape.append(jax.ShapeDtypeStruct((slot_rows // LANES, LANES), jnp.float32))
        count = sum(count for _, count in chunks)
        scratch = [
            pltpu.VMEM((count * TILE, depth), jnp.bfloat16),
            pltpu.VMEM((depth, 2 * columns), jnp.bfloat16),
            pltpu.VMEM((depth,), jnp.bfloat16),
            pltpu.SemaphoreType.DMA((4,)),
            pltpu.SemaphoreType.DMA((count,)),
            pltpu.SemaphoreType.DMA,
        ]
        made = pl.pallas_call(
            functools.partial(product_kernel, step, chip_count, chunks, staged, with_squares),
            in_specs=[pl.BlockSpec(memory_space=pltpu.HBM) if staged else vmem] * 3,
            out_shape=out_shape,
            out_specs=[vmem] * len(out_shape),
            scratch_shapes=scratch if staged else [],
            compiler_params=FIRST if staged else PARAMS,
            cost_estimate=COST,
        )(tokens, gain, kv_weight)
        made = list(made)
        squares = made.pop() if with_squares else None
        return list(zip(made[::2], made[1::2])), squares

    def tables(span_offset):
        frequencies = rope_base ** (-(np.arange(HD // 2, dtype=np.float32) * 2.0) / HD)
        frequencies = np.concatenate([frequencies, frequencies])[None, :].astype(np.float32)
        shapes = [(slot_rows // BLOCK, HD)] * 2 + [(BLOCK, HD)] * 2
        made = pl.pallas_call(
            table_kernel,
            in_specs=[pl.BlockSpec(memory_space=pltpu.SMEM)] * 2 + [pl.BlockSpec(memory_space=pltpu.VMEM)],
            out_shape=[jax.ShapeDtypeStruct((8, LANES), jnp.int32)]
            + [jax.ShapeDtypeStruct(shape, jnp.float32) for shape in shapes],
            out_specs=[pl.BlockSpec(memory_space=pltpu.VMEM)] * 5,
            compiler_params=PARAMS,
            cost_estimate=COST,
        )(live_blocks, span_offset, jnp.asarray(frequencies))
        return list(made)

    def finish(first, count, keep, received, table, squares, arrived, result):
        vmem = pl.BlockSpec(memory_space=pltpu.VMEM)
        operands = [keep, received] + table + squares + arrived
        aliases = {len(operands): 0}
        if result is None:
            result, aliases = jnp.zeros((1,), jnp.bfloat16), {}
        return pl.pallas_call(
            functools.partial(finish_kernel, first, count, tensor_count, model_dim),
            in_specs=[vmem] * len(operands) + [pl.BlockSpec(memory_space=pl.ANY)],
            out_shape=jax.ShapeDtypeStruct((slot_rows, columns), jnp.bfloat16),
            out_specs=pl.BlockSpec(memory_space=pltpu.HBM),
            scratch_shapes=[pltpu.VMEM((count * TILE, columns), jnp.bfloat16), pltpu.SemaphoreType.DMA((count,))],
            input_output_aliases=aliases,
            compiler_params=PARAMS,
            cost_estimate=COST,
        )(*operands, result)

    others = range(1, chip_count)
    firsts = [sum(CHUNKS[:index]) for index in range(len(CHUNKS))]
    chunk_count = len(CHUNKS)

    chunks = list(zip(firsts, CHUNKS))

    def start_chunks(gain, wanted, staged=False):
        made = [product(gain, step, wanted, staged)[0] for step in others]
        return [list(parts) for parts in zip(*made)]

    def add_halves(made):
        return [
            pl.pallas_call(
                add_kernel,
                out_shape=jax.ShapeDtypeStruct(keep.shape, keep.dtype),
                compiler_params=PARAMS,
                cost_estimate=COST,
            )(keep, lax.ppermute(send, "tensor", swap))
            for keep, send in made
        ]

    def cross(sums):
        return [lax.ppermute(part, "tensor", shift(step)) for step, part in zip(others, sums)]

    hold = lax.optimization_barrier
    (made,) = start_chunks(norm_gain, chunks[:1], staged=True)
    made, gain = hold((made, norm_gain))
    sums = add_halves(made)
    waiting = start_chunks(gain, chunks[1:])
    sums, waiting, gain, span_offset, live_blocks = hold((sums, waiting, gain, span_offset, live_blocks))

    arrivals = [cross(sums)] + [cross(add_halves(made)) for made in waiting]
    own, squares = product(gain, 0, chunks, with_squares=True)
    squares = [squares] + [
        lax.ppermute(squares, "tensor", [(i, (i + step) % tensor_count) for i in range(tensor_count)])
        for step in range(1, tensor_count)
    ]
    table = tables(span_offset)

    result = None
    for (first, count), (keep, send), arrived in zip(chunks, own, arrivals):
        received = lax.ppermute(send, "tensor", swap)
        result = finish(first, count, keep, received, table, squares, arrived, result)
    return result


def solution(mesh):
    in_specs = (
        P(("groups", "serve"), "tensor"),
        P("tensor"),
        P("tensor", None),
        P("groups"),
        P("groups"),
    )
    out_specs = P(("groups", "serve"), "tensor")
    return jax.shard_map(shards, mesh=mesh, in_specs=in_specs, out_specs=out_specs, check_vma=False)
```

```python
import functools

import jax
import jax.numpy as jnp
import numpy as np
from jax import lax
from jax.experimental import pallas as pl
from jax.experimental.pallas import tpu as pltpu
from jax.sharding import PartitionSpec as P

HD = 128
PAGE = 256
BLOCK = 64
LANES = 128
SUBLANES = 8

rope_base = 500000.0
norm_eps = 1e-05

TILE = 256
CHUNKS = (2, 2, 2)

PARAMS = pltpu.CompilerParams(vmem_limit_bytes=16 * 1024 * 1024)
FIRST = pltpu.CompilerParams(vmem_limit_bytes=56 * 1024 * 1024)
COST = pl.CostEstimate(flops=1, bytes_accessed=1, transcendentals=0)


def square_sums(rows):
    total = jnp.zeros((rows.shape[0], LANES), jnp.float32)
    for part in range(rows.shape[1] // LANES):
        wide = rows[:, part * LANES : (part + 1) * LANES].astype(jnp.float32)
        total += wide * wide
    return total


def packed(squares, width):
    per_row = width // LANES
    row = lax.broadcasted_iota(jnp.int32, (2 * SUBLANES, LANES), 0)
    parts = []
    for place in range(per_row):
        part = jnp.zeros((2 * SUBLANES, LANES), jnp.float32)
        for index, line in enumerate(squares[place::per_row]):
            high = line.astype(jnp.bfloat16).astype(jnp.float32)
            part = jnp.where(row == index, high, part)
            part = jnp.where(row == SUBLANES + index, line - high, part)
        parts.append(part)
    return jnp.concatenate(parts, axis=1).astype(jnp.bfloat16)


def unpacked(ref, line):
    index, place = divmod(line, ref.shape[1] // LANES)
    part = ref[pl.ds(ref.shape[0] - 2 * SUBLANES, 2 * SUBLANES), place * LANES : (place + 1) * LANES]
    part = part.astype(jnp.float32)
    return part[index : index + 1] + part[SUBLANES + index : SUBLANES + index + 1]


def product_kernel(step, chip_count, chunks, carrier, staged, with_squares, tokens, gain, weight, *refs):
    refs = list(refs)
    known = refs.pop(0) if carrier is not None else None
    outs = [refs.pop(0) for _ in range(2 * len(chunks))]
    squares = refs.pop(0) if with_squares else None
    depth, width = tokens.shape[1], 2 * outs[0].shape[1]
    me = lax.axis_index("tensor")
    core = lax.rem(me, 2)
    chip = lax.rem(lax.div(me, 2) + step, chip_count)
    place = pl.ds(pl.multiple_of(chip * width, width), width)

    weight_copies, row_copies = [], {}
    if staged:
        rows_buf, weight_buf, gain_buf, weight_sems, row_sems, gain_sem = refs
        cuts = weight_sems.shape[0]
        cut = depth // cuts
        gain_copy = pltpu.make_async_copy(gain, gain_buf, gain_sem)
        weight_copies = [
            pltpu.make_async_copy(
                weight.at[pl.ds(index * cut, cut), place],
                weight_buf.at[pl.ds(index * cut, cut), :],
                weight_sems.at[index],
            )
            for index in range(cuts)
        ]
        at = 0
        for first, count in chunks:
            for tile in range(first, first + count):
                buf = rows_buf.at[pl.ds(at * TILE, TILE), :]
                row_copies[tile] = (
                    pltpu.make_async_copy(tokens.at[pl.ds(tile * TILE, TILE), :], buf, row_sems.at[at]),
                    buf,
                )
                at += 1
        in_order = [copy for copy, _ in row_copies.values()]
        for copy in [gain_copy] + in_order[:1] + weight_copies + in_order[1:]:
            copy.start()
        gain_copy.wait()
        gains = gain_buf[...].reshape(1, depth)
    else:
        gains = gain[...].reshape(1, depth)

    if carrier is not None:
        squares[...] = known[...]
    for index, (first, count) in enumerate(chunks):
        for tile in range(first, first + count):
            if staged:
                row_copies[tile][0].wait()
                rows = row_copies[tile][1][...]
            else:
                rows = tokens[pl.ds(tile * TILE, TILE), :]
            scaled = rows * gains
            if weight_copies:
                product = jnp.zeros((TILE, width), jnp.float32)
                for part, copy in enumerate(weight_copies):
                    copy.wait()
                    span = slice(part * cut, (part + 1) * cut)
                    product += jnp.dot(
                        scaled[:, span], weight_buf[span, :], preferred_element_type=jnp.float32
                    )
                weight_copies = []
            else:
                columns = weight_buf[...] if staged else weight[:, place]
                product = jnp.dot(scaled, columns, preferred_element_type=jnp.float32)
            left = product[:, : width // 2].astype(jnp.bfloat16)
            right = product[:, width // 2 :].astype(jnp.bfloat16)
            inside = pl.ds((tile - first) * TILE, TILE)
            outs[2 * index][inside, :] = jnp.where(core == 0, left, right)
            outs[2 * index + 1][inside, :] = jnp.where(core == 0, right, left)
            if with_squares:
                total = square_sums(rows)
                for part in range(TILE // LANES):
                    turned = jnp.transpose(total[part * LANES : (part + 1) * LANES])
                    row = tile * (TILE // LANES) + part
                    squares[row : row + 1, :] = jnp.sum(turned, axis=0, keepdims=True)
    if carrier is not None:
        lines = [squares[line : line + 1, :] for line in range(squares.shape[0])]
        out = outs[2 * carrier + 1]
        out[pl.ds(out.shape[0] - 2 * SUBLANES, 2 * SUBLANES), :] = packed(lines, out.shape[1])


def add_kernel(keep, received, out):
    out[...] = (keep[...].astype(jnp.float32) + received[...].astype(jnp.float32)).astype(out.dtype)


def add_carrier_kernel(keep, received, squares, out, pair_squares):
    rows = pl.ds(0, keep.shape[0])
    total = keep[...].astype(jnp.float32) + received[rows, :].astype(jnp.float32)
    out[rows, :] = total.astype(out.dtype)
    lines = []
    for line in range(squares.shape[0]):
        lines.append(squares[line : line + 1, :] + unpacked(received, line))
        pair_squares[line : line + 1, :] = lines[-1]
    out[pl.ds(keep.shape[0], 2 * SUBLANES), :] = packed(lines, out.shape[1])


def table_kernel(live, span, frequencies, limit, far_cos, far_sin, near_cos, near_sin):
    limit[...] = jnp.full(limit.shape, live[lax.axis_index("serve")] * BLOCK, jnp.int32)
    blocks = far_cos.shape[0]
    start = span[lax.axis_index("serve")] * PAGE
    first = start + BLOCK * lax.broadcasted_iota(jnp.int32, (blocks, HD), 0)
    far = first.astype(jnp.float32) * frequencies[...]
    near = lax.broadcasted_iota(jnp.int32, (BLOCK, HD), 0).astype(jnp.float32) * frequencies[...]
    far_cos[...] = jnp.cos(far)
    far_sin[...] = jnp.sin(far)
    near_cos[...] = jnp.cos(near)
    near_sin[...] = jnp.sin(near)


def finish_kernel(first, count, chip_count, model_dim, *refs):
    keep, received, limit, far_cos, far_sin, near_cos, near_sin = refs[:7]
    pair_squares, carriers, arrived = refs[7], refs[8 : 7 + chip_count], refs[7 + chip_count : -4]
    out, staged, sems = refs[-3:]
    on_diagonal = lax.broadcasted_iota(jnp.int32, (LANES, LANES), 0) == lax.broadcasted_iota(
        jnp.int32, (LANES, LANES), 1
    )
    sign = jnp.where(lax.broadcasted_iota(jnp.int32, (1, HD), 1) < HD // 2, -1.0, 1.0)
    copies = []
    for index in range(count):
        start = (first + index) * TILE
        rows, inside = pl.ds(start, TILE), pl.ds(index * TILE, TILE)
        values = keep[inside, :].astype(jnp.float32) + received[inside, :].astype(jnp.float32)
        for part in arrived:
            values += part[inside, :].astype(jnp.float32)
        columns = []
        for row in range(start // LANES, (start + TILE) // LANES):
            totals = pair_squares[row : row + 1, :]
            for ref in carriers:
                totals += unpacked(ref, row)
            columns.append(jnp.sum(jnp.where(on_diagonal, totals, 0.0), axis=1, keepdims=True))
        scales = 1.0 / jnp.sqrt(jnp.concatenate(columns, axis=0) / model_dim + norm_eps)
        alive = start + lax.broadcasted_iota(jnp.int32, (TILE, LANES), 0) < limit[0:1, :]
        cosines, sines = [], []
        for block in range(start // BLOCK, (start + TILE) // BLOCK):
            block_cos = far_cos[block : block + 1, :]
            block_sin = far_sin[block : block + 1, :]
            cosines.append(block_cos * near_cos[...] - block_sin * near_sin[...])
            sines.append((sign * block_sin) * near_cos[...] + (sign * block_cos) * near_sin[...])
        cosine = jnp.concatenate(cosines, axis=0)
        sine = jnp.concatenate(sines, axis=0)
        for low in range(0, out.shape[1], 2 * HD):
            key = values[:, low : low + HD] * scales
            turned = key * cosine + pltpu.roll(key, HD // 2, 1) * sine
            staged[inside, low : low + HD] = jnp.where(alive, turned, 0.0).astype(out.dtype)
            value = values[:, low + HD : low + 2 * HD] * scales
            staged[inside, low + HD : low + 2 * HD] = jnp.where(alive, value, 0.0).astype(out.dtype)
        copies.append(pltpu.make_async_copy(staged.at[inside, :], out.at[rows, :], sems.at[index]))
        copies[-1].start()
    for copy in copies:
        copy.wait()


def shards(tokens, norm_gain, kv_weight, live_blocks, span_offset):
    tensor_count = lax.axis_size("tensor")
    chip_count = tensor_count // 2
    me = lax.axis_index("tensor")
    slot_rows, depth = tokens.shape
    columns = kv_weight.shape[1] // tensor_count
    tiles = slot_rows // TILE
    model_dim = depth * tensor_count

    swap = [(i, i ^ 1) for i in range(tensor_count)]

    def shift(step):
        return [(i, (i + 2 * step) % tensor_count) for i in range(tensor_count)]

    def product(gain, step, chunks, staged=False, with_squares=False, carrier=None, known=None):
        vmem = pl.BlockSpec(memory_space=pltpu.VMEM)
        out_shape = [
            jax.ShapeDtypeStruct((count * TILE, columns), jnp.bfloat16) for _, count in chunks for _ in range(2)
        ]
        if carrier is not None:
            size = out_shape[2 * carrier].shape[0] + 2 * SUBLANES
            out_shape[2 * carrier + 1] = jax.ShapeDtypeStruct((size, columns), jnp.bfloat16)
        if with_squares:
            out_shape.append(jax.ShapeDtypeStruct((slot_rows // LANES, LANES), jnp.float32))
        count = sum(count for _, count in chunks)
        scratch = [
            pltpu.VMEM((count * TILE, depth), jnp.bfloat16),
            pltpu.VMEM((depth, 2 * columns), jnp.bfloat16),
            pltpu.VMEM((depth,), jnp.bfloat16),
            pltpu.SemaphoreType.DMA((4,)),
            pltpu.SemaphoreType.DMA((count,)),
            pltpu.SemaphoreType.DMA,
        ]
        made = pl.pallas_call(
            functools.partial(product_kernel, step, chip_count, chunks, carrier, staged, with_squares),
            in_specs=[pl.BlockSpec(memory_space=pltpu.HBM) if staged else vmem] * 3 + [vmem] * (known is not None),
            out_shape=out_shape,
            out_specs=[vmem] * len(out_shape),
            scratch_shapes=scratch if staged else [],
            compiler_params=FIRST if staged else PARAMS,
            cost_estimate=COST,
        )(tokens, gain, kv_weight, *([] if known is None else [known]))
        made = list(made)
        squares = made.pop() if with_squares else None
        return list(zip(made[::2], made[1::2])), squares

    def tables(span_offset):
        frequencies = rope_base ** (-(np.arange(HD // 2, dtype=np.float32) * 2.0) / HD)
        frequencies = np.concatenate([frequencies, frequencies])[None, :].astype(np.float32)
        shapes = [(slot_rows // BLOCK, HD)] * 2 + [(BLOCK, HD)] * 2
        made = pl.pallas_call(
            table_kernel,
            in_specs=[pl.BlockSpec(memory_space=pltpu.SMEM)] * 2 + [pl.BlockSpec(memory_space=pltpu.VMEM)],
            out_shape=[jax.ShapeDtypeStruct((8, LANES), jnp.int32)]
            + [jax.ShapeDtypeStruct(shape, jnp.float32) for shape in shapes],
            out_specs=[pl.BlockSpec(memory_space=pltpu.VMEM)] * 5,
            compiler_params=PARAMS,
            cost_estimate=COST,
        )(live_blocks, span_offset, jnp.asarray(frequencies))
        return list(made)

    def finish(first, count, keep, received, table, squares, arrived, result):
        vmem = pl.BlockSpec(memory_space=pltpu.VMEM)
        operands = [keep, received] + table + squares + arrived
        aliases = {len(operands): 0}
        if result is None:
            result, aliases = jnp.zeros((1,), jnp.bfloat16), {}
        return pl.pallas_call(
            functools.partial(finish_kernel, first, count, chip_count, model_dim),
            in_specs=[vmem] * len(operands) + [pl.BlockSpec(memory_space=pl.ANY)],
            out_shape=jax.ShapeDtypeStruct((slot_rows, columns), jnp.bfloat16),
            out_specs=pl.BlockSpec(memory_space=pltpu.HBM),
            scratch_shapes=[pltpu.VMEM((count * TILE, columns), jnp.bfloat16), pltpu.SemaphoreType.DMA((count,))],
            input_output_aliases=aliases,
            compiler_params=PARAMS,
            cost_estimate=COST,
        )(*operands, result)

    others = range(1, chip_count)
    firsts = [sum(CHUNKS[:index]) for index in range(len(CHUNKS))]
    chunk_count = len(CHUNKS)

    chunks = list(zip(firsts, CHUNKS))

    def add_halves(made):
        return [
            pl.pallas_call(
                add_kernel,
                out_shape=jax.ShapeDtypeStruct(keep.shape, keep.dtype),
                compiler_params=PARAMS,
                cost_estimate=COST,
            )(keep, lax.ppermute(send, "tensor", swap))
            for keep, send in made
        ]

    def add_carriers(made, squares):
        added = [
            pl.pallas_call(
                add_carrier_kernel,
                out_shape=[
                    jax.ShapeDtypeStruct(send.shape, send.dtype),
                    jax.ShapeDtypeStruct(squares.shape, squares.dtype),
                ],
                compiler_params=PARAMS,
                cost_estimate=COST,
            )(keep, lax.ppermute(send, "tensor", swap), squares)
            for keep, send in made
        ]
        return [sums for sums, _ in added], added[0][1]

    def cross(sums):
        return [lax.ppermute(part, "tensor", shift(step)) for step, part in zip(others, sums)]

    hold = lax.optimization_barrier
    made, known = [], []
    for step in others:
        halves, squares = product(norm_gain, step, chunks[:1], staged=True, with_squares=True)
        made += halves
        known.append(squares)
    made, gain, known = hold((made, norm_gain, known))
    sums = add_halves(made)
    waiting = []
    for step, squares in zip(others, known):
        halves, squares = product(gain, step, chunks[1:], with_squares=True, carrier=0, known=squares)
        waiting.append(halves)
    waiting = [list(parts) for parts in zip(*waiting)]
    sums, waiting, squares, gain, span_offset, live_blocks = hold(
        (sums, waiting, squares, gain, span_offset, live_blocks)
    )

    carrying, pair_squares = add_carriers(waiting[0], squares)
    arrivals = [cross(sums), cross(carrying)] + [cross(add_halves(made)) for made in waiting[1:]]
    own, _ = product(gain, 0, chunks)
    table = tables(span_offset)
    squares = [pair_squares] + arrivals[1]

    result = None
    for (first, count), (keep, send), arrived in zip(chunks, own, arrivals):
        received = lax.ppermute(send, "tensor", swap)
        result = finish(first, count, keep, received, table, squares, arrived, result)
    return result


def solution(mesh):
    in_specs = (
        P(("groups", "serve"), "tensor"),
        P("tensor"),
        P("tensor", None),
        P("groups"),
        P("groups"),
    )
    out_specs = P(("groups", "serve"), "tensor")
    return jax.shard_map(shards, mesh=mesh, in_specs=in_specs, out_specs=out_specs, check_vma=False)
```

```python
import functools

import jax
import jax.numpy as jnp
import numpy as np
from jax import lax
from jax.experimental import pallas as pl
from jax.experimental.pallas import tpu as pltpu
from jax.sharding import PartitionSpec as P

HD = 128
PAGE = 256
BLOCK = 64
LANES = 128
SUBLANES = 8

rope_base = 500000.0
norm_eps = 1e-05

TILE = 256
CUTS = 4
SPLIT = 4
CHUNKS = (2, 2, 2)

PARAMS = pltpu.CompilerParams(vmem_limit_bytes=16 * 1024 * 1024)
FIRST = pltpu.CompilerParams(vmem_limit_bytes=56 * 1024 * 1024)
COST = pl.CostEstimate(flops=1, bytes_accessed=1, transcendentals=0)


def square_sums(rows):
    total = jnp.zeros((rows.shape[0], LANES), jnp.float32)
    for part in range(rows.shape[1] // LANES):
        wide = rows[:, part * LANES : (part + 1) * LANES].astype(jnp.float32)
        total += wide * wide
    return total


def packed(squares, width):
    per_row = width // LANES
    row = lax.broadcasted_iota(jnp.int32, (2 * SUBLANES, LANES), 0)
    parts = []
    for place in range(per_row):
        part = jnp.zeros((2 * SUBLANES, LANES), jnp.float32)
        for index, line in enumerate(squares[place::per_row]):
            high = line.astype(jnp.bfloat16).astype(jnp.float32)
            part = jnp.where(row == index, high, part)
            part = jnp.where(row == SUBLANES + index, line - high, part)
        parts.append(part)
    return jnp.concatenate(parts, axis=1).astype(jnp.bfloat16)


def unpacked(ref, line):
    index, place = divmod(line, ref.shape[1] // LANES)
    part = ref[pl.ds(ref.shape[0] - 2 * SUBLANES, 2 * SUBLANES), place * LANES : (place + 1) * LANES]
    part = part.astype(jnp.float32)
    return part[index : index + 1] + part[SUBLANES + index : SUBLANES + index + 1]


def product_kernel(step, chip_count, chunks, carrier, staged, tokens, gain, weight, *refs):
    refs = list(refs)
    outs = [refs.pop(0) for _ in range(2 * len(chunks))]
    squares = refs.pop(0) if carrier is not None else None
    depth, width = tokens.shape[1], 2 * outs[0].shape[1]
    me = lax.axis_index("tensor")
    core = lax.rem(me, 2)
    chip = lax.rem(lax.div(me, 2) + step, chip_count)
    place = pl.ds(pl.multiple_of(chip * width, width), width)

    weight_copies, row_copies = [], {}
    if staged:
        rows_buf, weight_buf, gain_buf, weight_sems, row_sems, gain_sem = refs
        cut, piece = depth // CUTS, depth // CUTS // SPLIT
        gain_copy = pltpu.make_async_copy(gain, gain_buf, gain_sem)
        for index in range(CUTS * SPLIT):
            some = pl.ds(index * piece, piece)
            weight_copies.append(
                pltpu.make_async_copy(weight.at[some, place], weight_buf.at[some, :], weight_sems.at[index])
            )
        at, size = 0, TILE // SPLIT
        for first, count in chunks:
            for tile in range(first, first + count):
                copies = []
                for part in range(SPLIT):
                    some = pl.ds(at * TILE + part * size, size)
                    rows = tokens.at[pl.ds(tile * TILE + part * size, size), :]
                    copies.append(pltpu.make_async_copy(rows, rows_buf.at[some, :], row_sems.at[at * SPLIT + part]))
                row_copies[tile] = copies, rows_buf.at[pl.ds(at * TILE, TILE), :]
                at += 1
        in_order = [copies for copies, _ in row_copies.values()]
        for copy in [gain_copy] + in_order[0] + weight_copies + sum(in_order[1:], []):
            copy.start()
        gain_copy.wait()
        gains = gain_buf[...].reshape(1, depth)
    else:
        gains = gain[...].reshape(1, depth)

    for index, (first, count) in enumerate(chunks):
        for tile in range(first, first + count):
            if staged:
                for copy in row_copies[tile][0]:
                    copy.wait()
                rows = row_copies[tile][1][...]
            else:
                rows = tokens[pl.ds(tile * TILE, TILE), :]
            scaled = rows * gains
            if weight_copies:
                product = jnp.zeros((TILE, width), jnp.float32)
                for part in range(CUTS):
                    for copy in weight_copies[part * SPLIT : (part + 1) * SPLIT]:
                        copy.wait()
                    span = slice(part * cut, (part + 1) * cut)
                    product += jnp.dot(
                        scaled[:, span], weight_buf[span, :], preferred_element_type=jnp.float32
                    )
                weight_copies = []
            else:
                columns = weight_buf[...] if staged else weight[:, place]
                product = jnp.dot(scaled, columns, preferred_element_type=jnp.float32)
            left = product[:, : width // 2].astype(jnp.bfloat16)
            right = product[:, width // 2 :].astype(jnp.bfloat16)
            inside = pl.ds((tile - first) * TILE, TILE)
            outs[2 * index][inside, :] = jnp.where(core == 0, left, right)
            outs[2 * index + 1][inside, :] = jnp.where(core == 0, right, left)
    if carrier is not None:
        for line in range(squares.shape[0]):
            total = square_sums(tokens[pl.ds(line * LANES, LANES), :])
            squares[line : line + 1, :] = jnp.sum(jnp.transpose(total), axis=0, keepdims=True)
        lines = [squares[line : line + 1, :] for line in range(squares.shape[0])]
        out = outs[2 * carrier + 1]
        out[pl.ds(out.shape[0] - 2 * SUBLANES, 2 * SUBLANES), :] = packed(lines, out.shape[1])


def add_kernel(keep, received, out):
    out[...] = (keep[...].astype(jnp.float32) + received[...].astype(jnp.float32)).astype(out.dtype)


def add_carrier_kernel(keep, received, squares, out, pair_squares):
    rows = pl.ds(0, keep.shape[0])
    total = keep[...].astype(jnp.float32) + received[rows, :].astype(jnp.float32)
    out[rows, :] = total.astype(out.dtype)
    lines = []
    for line in range(squares.shape[0]):
        lines.append(squares[line : line + 1, :] + unpacked(received, line))
        pair_squares[line : line + 1, :] = lines[-1]
    out[pl.ds(keep.shape[0], 2 * SUBLANES), :] = packed(lines, out.shape[1])


def table_kernel(live, span, frequencies, limit, far_cos, far_sin, near_cos, near_sin):
    limit[...] = jnp.full(limit.shape, live[lax.axis_index("serve")] * BLOCK, jnp.int32)
    blocks = far_cos.shape[0]
    start = span[lax.axis_index("serve")] * PAGE
    first = start + BLOCK * lax.broadcasted_iota(jnp.int32, (blocks, HD), 0)
    far = first.astype(jnp.float32) * frequencies[...]
    near = lax.broadcasted_iota(jnp.int32, (BLOCK, HD), 0).astype(jnp.float32) * frequencies[...]
    far_cos[...] = jnp.cos(far)
    far_sin[...] = jnp.sin(far)
    near_cos[...] = jnp.cos(near)
    near_sin[...] = jnp.sin(near)


def finish_kernel(first, count, chip_count, model_dim, *refs):
    keep, received, limit, far_cos, far_sin, near_cos, near_sin = refs[:7]
    pair_squares, carriers, arrived = refs[7], refs[8 : 7 + chip_count], refs[7 + chip_count : -4]
    out, staged, sems = refs[-3:]
    on_diagonal = lax.broadcasted_iota(jnp.int32, (LANES, LANES), 0) == lax.broadcasted_iota(
        jnp.int32, (LANES, LANES), 1
    )
    sign = jnp.where(lax.broadcasted_iota(jnp.int32, (1, HD), 1) < HD // 2, -1.0, 1.0)
    copies = []
    for index in range(count):
        start = (first + index) * TILE
        rows, inside = pl.ds(start, TILE), pl.ds(index * TILE, TILE)
        values = keep[inside, :].astype(jnp.float32) + received[inside, :].astype(jnp.float32)
        for part in arrived:
            values += part[inside, :].astype(jnp.float32)
        columns = []
        for row in range(start // LANES, (start + TILE) // LANES):
            totals = pair_squares[row : row + 1, :]
            for ref in carriers:
                totals += unpacked(ref, row)
            columns.append(jnp.sum(jnp.where(on_diagonal, totals, 0.0), axis=1, keepdims=True))
        scales = 1.0 / jnp.sqrt(jnp.concatenate(columns, axis=0) / model_dim + norm_eps)
        alive = start + lax.broadcasted_iota(jnp.int32, (TILE, LANES), 0) < limit[0:1, :]
        cosines, sines = [], []
        for block in range(start // BLOCK, (start + TILE) // BLOCK):
            block_cos = far_cos[block : block + 1, :]
            block_sin = far_sin[block : block + 1, :]
            cosines.append(block_cos * near_cos[...] - block_sin * near_sin[...])
            sines.append((sign * block_sin) * near_cos[...] + (sign * block_cos) * near_sin[...])
        cosine = jnp.concatenate(cosines, axis=0)
        sine = jnp.concatenate(sines, axis=0)
        for low in range(0, out.shape[1], 2 * HD):
            key = values[:, low : low + HD] * scales
            turned = key * cosine + pltpu.roll(key, HD // 2, 1) * sine
            staged[inside, low : low + HD] = jnp.where(alive, turned, 0.0).astype(out.dtype)
            value = values[:, low + HD : low + 2 * HD] * scales
            staged[inside, low + HD : low + 2 * HD] = jnp.where(alive, value, 0.0).astype(out.dtype)
        copies.append(pltpu.make_async_copy(staged.at[inside, :], out.at[rows, :], sems.at[index]))
        copies[-1].start()
    for copy in copies:
        copy.wait()


def shards(tokens, norm_gain, kv_weight, live_blocks, span_offset):
    tensor_count = lax.axis_size("tensor")
    chip_count = tensor_count // 2
    me = lax.axis_index("tensor")
    slot_rows, depth = tokens.shape
    columns = kv_weight.shape[1] // tensor_count
    tiles = slot_rows // TILE
    model_dim = depth * tensor_count

    swap = [(i, i ^ 1) for i in range(tensor_count)]

    def shift(step):
        return [(i, (i + 2 * step) % tensor_count) for i in range(tensor_count)]

    def product(gain, step, chunks, staged=False, carrier=None):
        vmem = pl.BlockSpec(memory_space=pltpu.VMEM)
        out_shape = [
            jax.ShapeDtypeStruct((count * TILE, columns), jnp.bfloat16) for _, count in chunks for _ in range(2)
        ]
        if carrier is not None:
            size = out_shape[2 * carrier].shape[0] + 2 * SUBLANES
            out_shape[2 * carrier + 1] = jax.ShapeDtypeStruct((size, columns), jnp.bfloat16)
            out_shape.append(jax.ShapeDtypeStruct((slot_rows // LANES, LANES), jnp.float32))
        count = sum(count for _, count in chunks)
        scratch = [
            pltpu.VMEM((count * TILE, depth), jnp.bfloat16),
            pltpu.VMEM((depth, 2 * columns), jnp.bfloat16),
            pltpu.VMEM((depth,), jnp.bfloat16),
            pltpu.SemaphoreType.DMA((CUTS * SPLIT,)),
            pltpu.SemaphoreType.DMA((count * SPLIT,)),
            pltpu.SemaphoreType.DMA,
        ]
        made = pl.pallas_call(
            functools.partial(product_kernel, step, chip_count, chunks, carrier, staged),
            in_specs=[pl.BlockSpec(memory_space=pltpu.HBM) if staged else vmem] * 3,
            out_shape=out_shape,
            out_specs=[vmem] * len(out_shape),
            scratch_shapes=scratch if staged else [],
            compiler_params=FIRST if staged else PARAMS,
            cost_estimate=COST,
        )(tokens, gain, kv_weight)
        made = list(made)
        squares = made.pop() if carrier is not None else None
        return list(zip(made[::2], made[1::2])), squares

    def tables(span_offset):
        frequencies = rope_base ** (-(np.arange(HD // 2, dtype=np.float32) * 2.0) / HD)
        frequencies = np.concatenate([frequencies, frequencies])[None, :].astype(np.float32)
        shapes = [(slot_rows // BLOCK, HD)] * 2 + [(BLOCK, HD)] * 2
        made = pl.pallas_call(
            table_kernel,
            in_specs=[pl.BlockSpec(memory_space=pltpu.SMEM)] * 2 + [pl.BlockSpec(memory_space=pltpu.VMEM)],
            out_shape=[jax.ShapeDtypeStruct((8, LANES), jnp.int32)]
            + [jax.ShapeDtypeStruct(shape, jnp.float32) for shape in shapes],
            out_specs=[pl.BlockSpec(memory_space=pltpu.VMEM)] * 5,
            compiler_params=PARAMS,
            cost_estimate=COST,
        )(live_blocks, span_offset, jnp.asarray(frequencies))
        return list(made)

    def finish(first, count, keep, received, table, squares, arrived, result):
        vmem = pl.BlockSpec(memory_space=pltpu.VMEM)
        operands = [keep, received] + table + squares + arrived
        aliases = {len(operands): 0}
        if result is None:
            result, aliases = jnp.zeros((1,), jnp.bfloat16), {}
        return pl.pallas_call(
            functools.partial(finish_kernel, first, count, chip_count, model_dim),
            in_specs=[vmem] * len(operands) + [pl.BlockSpec(memory_space=pl.ANY)],
            out_shape=jax.ShapeDtypeStruct((slot_rows, columns), jnp.bfloat16),
            out_specs=pl.BlockSpec(memory_space=pltpu.HBM),
            scratch_shapes=[pltpu.VMEM((count * TILE, columns), jnp.bfloat16), pltpu.SemaphoreType.DMA((count,))],
            input_output_aliases=aliases,
            compiler_params=PARAMS,
            cost_estimate=COST,
        )(*operands, result)

    others = range(1, chip_count)
    firsts = [sum(CHUNKS[:index]) for index in range(len(CHUNKS))]
    chunk_count = len(CHUNKS)

    chunks = list(zip(firsts, CHUNKS))

    def add_halves(made):
        return [
            pl.pallas_call(
                add_kernel,
                out_shape=jax.ShapeDtypeStruct(keep.shape, keep.dtype),
                compiler_params=PARAMS,
                cost_estimate=COST,
            )(keep, lax.ppermute(send, "tensor", swap))
            for keep, send in made
        ]

    def add_carriers(made, squares):
        added = [
            pl.pallas_call(
                add_carrier_kernel,
                out_shape=[
                    jax.ShapeDtypeStruct(send.shape, send.dtype),
                    jax.ShapeDtypeStruct(squares.shape, squares.dtype),
                ],
                compiler_params=PARAMS,
                cost_estimate=COST,
            )(keep, lax.ppermute(send, "tensor", swap), squares)
            for keep, send in made
        ]
        return [sums for sums, _ in added], added[0][1]

    def cross(sums):
        return [lax.ppermute(part, "tensor", shift(step)) for step, part in zip(others, sums)]

    hold = lax.optimization_barrier
    made = [product(norm_gain, step, chunks[:1], staged=True)[0][0] for step in others]
    made, gain = hold((made, norm_gain))
    sums = add_halves(made)
    waiting = []
    for step in others:
        halves, squares = product(gain, step, chunks[1:], carrier=0)
        waiting.append(halves)
    waiting = [list(parts) for parts in zip(*waiting)]
    sums, waiting, squares, gain, span_offset, live_blocks = hold(
        (sums, waiting, squares, gain, span_offset, live_blocks)
    )

    carrying, pair_squares = add_carriers(waiting[0], squares)
    arrivals = [cross(sums), cross(carrying)] + [cross(add_halves(made)) for made in waiting[1:]]
    own, _ = product(gain, 0, chunks)
    table = tables(span_offset)
    squares = [pair_squares] + arrivals[1]

    result = None
    for (first, count), (keep, send), arrived in zip(chunks, own, arrivals):
        received = lax.ppermute(send, "tensor", swap)
        result = finish(first, count, keep, received, table, squares, arrived, result)
    return result


def solution(mesh):
    in_specs = (
        P(("groups", "serve"), "tensor"),
        P("tensor"),
        P("tensor", None),
        P("groups"),
        P("groups"),
    )
    out_specs = P(("groups", "serve"), "tensor")
    return jax.shard_map(shards, mesh=mesh, in_specs=in_specs, out_specs=out_specs, check_vma=False)
```

```python
import functools

import jax
import jax.numpy as jnp
import numpy as np
from jax import lax
from jax.experimental import pallas as pl
from jax.experimental.pallas import tpu as pltpu
from jax.sharding import PartitionSpec as P

HD = 128
PAGE = 256
BLOCK = 64
LANES = 128
SUBLANES = 8

rope_base = 500000.0
norm_eps = 1e-05

TILE = 256
CUTS = 4
CHUNKS = (2, 1, 3)

PARAMS = pltpu.CompilerParams(vmem_limit_bytes=16 * 1024 * 1024)
FIRST = pltpu.CompilerParams(vmem_limit_bytes=56 * 1024 * 1024)
LATER = pl.CostEstimate(flops=20000000000, bytes_accessed=1, transcendentals=0)
COST = pl.CostEstimate(flops=1, bytes_accessed=1, transcendentals=0)


def square_sums(rows):
    total = jnp.zeros((rows.shape[0], LANES), jnp.float32)
    for part in range(rows.shape[1] // LANES):
        wide = rows[:, part * LANES : (part + 1) * LANES].astype(jnp.float32)
        total += wide * wide
    return total


def packed(squares, width):
    per_row = width // LANES
    row = lax.broadcasted_iota(jnp.int32, (2 * SUBLANES, LANES), 0)
    parts = []
    for place in range(per_row):
        part = jnp.zeros((2 * SUBLANES, LANES), jnp.float32)
        for index, line in enumerate(squares[place::per_row]):
            high = line.astype(jnp.bfloat16).astype(jnp.float32)
            part = jnp.where(row == index, high, part)
            part = jnp.where(row == SUBLANES + index, line - high, part)
        parts.append(part)
    return jnp.concatenate(parts, axis=1).astype(jnp.bfloat16)


def unpacked(ref, line):
    index, place = divmod(line, ref.shape[1] // LANES)
    part = ref[pl.ds(ref.shape[0] - 2 * SUBLANES, 2 * SUBLANES), place * LANES : (place + 1) * LANES]
    part = part.astype(jnp.float32)
    return part[index : index + 1] + part[SUBLANES + index : SUBLANES + index + 1]


def product_kernel(step, chip_count, first, staged, carrier, tokens, gain, weight, *refs):
    refs = list(refs)
    keep, send = refs.pop(0), refs.pop(0)
    squares = refs.pop(0) if carrier else None
    count = keep.shape[0] // TILE
    depth, width = tokens.shape[1], 2 * keep.shape[1]
    me = lax.axis_index("tensor")
    core = lax.rem(me, 2)
    chip = lax.rem(lax.div(me, 2) + step, chip_count)
    place = pl.ds(pl.multiple_of(chip * width, width), width)

    weight_copies, row_copies = [], []
    if staged:
        rows_buf, weight_buf, gain_buf, weight_sems, row_sems, gain_sem = refs
        cut = depth // CUTS
        gain_copy = pltpu.make_async_copy(gain, gain_buf, gain_sem)
        for index in range(CUTS):
            some = pl.ds(index * cut, cut)
            weight_copies.append(
                pltpu.make_async_copy(weight.at[some, place], weight_buf.at[some, :], weight_sems.at[index])
            )
        for tile in range(count):
            rows = tokens.at[pl.ds((first + tile) * TILE, TILE), :]
            row_copies.append(
                pltpu.make_async_copy(rows, rows_buf.at[pl.ds(tile * TILE, TILE), :], row_sems.at[tile])
            )
        for copy in [gain_copy] + row_copies[:1] + weight_copies + row_copies[1:]:
            copy.start()
        gain_copy.wait()
        gains = gain_buf[...].reshape(1, depth)
    else:
        gains = gain[...].reshape(1, depth)

    lines = []
    for tile in range(count):
        inside = pl.ds(tile * TILE, TILE)
        if staged:
            row_copies[tile].wait()
            rows = rows_buf[inside, :]
        else:
            rows = tokens[pl.ds((first + tile) * TILE, TILE), :]
        scaled = rows * gains
        if weight_copies:
            product = jnp.zeros((TILE, width), jnp.float32)
            for index, copy in enumerate(weight_copies):
                copy.wait()
                span = slice(index * cut, (index + 1) * cut)
                product += jnp.dot(scaled[:, span], weight_buf[span, :], preferred_element_type=jnp.float32)
            weight_copies = []
        else:
            columns = weight_buf[...] if staged else weight[:, place]
            product = jnp.dot(scaled, columns, preferred_element_type=jnp.float32)
        left = product[:, : width // 2].astype(jnp.bfloat16)
        right = product[:, width // 2 :].astype(jnp.bfloat16)
        keep[inside, :] = jnp.where(core == 0, left, right)
        send[inside, :] = jnp.where(core == 0, right, left)
        if carrier:
            total = square_sums(rows)
            for part in range(TILE // LANES):
                turned = jnp.transpose(total[part * LANES : (part + 1) * LANES])
                lines.append(jnp.sum(turned, axis=0, keepdims=True))
                squares[len(lines) - 1 : len(lines), :] = lines[-1]
    if carrier:
        send[pl.ds(keep.shape[0], 2 * SUBLANES), :] = packed(lines, send.shape[1])


def add_carrier_kernel(keep, received, squares, out, pair_squares):
    rows = pl.ds(0, keep.shape[0])
    total = keep[...].astype(jnp.float32) + received[rows, :].astype(jnp.float32)
    out[rows, :] = total.astype(out.dtype)
    lines = []
    for line in range(squares.shape[0]):
        lines.append(squares[line : line + 1, :] + unpacked(received, line))
        pair_squares[line : line + 1, :] = lines[-1]
    out[pl.ds(keep.shape[0], 2 * SUBLANES), :] = packed(lines, out.shape[1])


def table_kernel(live, span, frequencies, limit, far_cos, far_sin, near_cos, near_sin):
    limit[...] = jnp.full(limit.shape, live[lax.axis_index("serve")] * BLOCK, jnp.int32)
    blocks = far_cos.shape[0]
    start = span[lax.axis_index("serve")] * PAGE
    first = start + BLOCK * lax.broadcasted_iota(jnp.int32, (blocks, HD), 0)
    far = first.astype(jnp.float32) * frequencies[...]
    near = lax.broadcasted_iota(jnp.int32, (BLOCK, HD), 0).astype(jnp.float32) * frequencies[...]
    far_cos[...] = jnp.cos(far)
    far_sin[...] = jnp.sin(far)
    near_cos[...] = jnp.cos(near)
    near_sin[...] = jnp.sin(near)


def finish_kernel(first, count, model_dim, *refs):
    keep, received, limit, far_cos, far_sin, near_cos, near_sin = refs[:7]
    pair_squares, arrived = refs[7], refs[8:-4]
    out, staged, sems = refs[-3:]
    on_diagonal = lax.broadcasted_iota(jnp.int32, (LANES, LANES), 0) == lax.broadcasted_iota(
        jnp.int32, (LANES, LANES), 1
    )
    sign = jnp.where(lax.broadcasted_iota(jnp.int32, (1, HD), 1) < HD // 2, -1.0, 1.0)
    copies = []
    for index in range(count):
        start = (first + index) * TILE
        rows, inside = pl.ds(start, TILE), pl.ds(index * TILE, TILE)
        values = keep[inside, :].astype(jnp.float32) + received[inside, :].astype(jnp.float32)
        for part in arrived:
            values += part[inside, :].astype(jnp.float32)
        columns = []
        for line in range(index * TILE // LANES, (index + 1) * TILE // LANES):
            totals = pair_squares[line : line + 1, :]
            for ref in arrived:
                totals += unpacked(ref, line)
            columns.append(jnp.sum(jnp.where(on_diagonal, totals, 0.0), axis=1, keepdims=True))
        scales = 1.0 / jnp.sqrt(jnp.concatenate(columns, axis=0) / model_dim + norm_eps)
        alive = start + lax.broadcasted_iota(jnp.int32, (TILE, LANES), 0) < limit[0:1, :]
        cosines, sines = [], []
        for block in range(start // BLOCK, (start + TILE) // BLOCK):
            block_cos = far_cos[block : block + 1, :]
            block_sin = far_sin[block : block + 1, :]
            cosines.append(block_cos * near_cos[...] - block_sin * near_sin[...])
            sines.append((sign * block_sin) * near_cos[...] + (sign * block_cos) * near_sin[...])
        cosine = jnp.concatenate(cosines, axis=0)
        sine = jnp.concatenate(sines, axis=0)
        for low in range(0, out.shape[1], 2 * HD):
            key = values[:, low : low + HD] * scales
            turned = key * cosine + pltpu.roll(key, HD // 2, 1) * sine
            staged[inside, low : low + HD] = jnp.where(alive, turned, 0.0).astype(out.dtype)
            value = values[:, low + HD : low + 2 * HD] * scales
            staged[inside, low + HD : low + 2 * HD] = jnp.where(alive, value, 0.0).astype(out.dtype)
        copies.append(pltpu.make_async_copy(staged.at[inside, :], out.at[rows, :], sems.at[index]))
        copies[-1].start()
    for copy in copies:
        copy.wait()


def shards(tokens, norm_gain, kv_weight, live_blocks, span_offset):
    tensor_count = lax.axis_size("tensor")
    chip_count = tensor_count // 2
    me = lax.axis_index("tensor")
    slot_rows, depth = tokens.shape
    columns = kv_weight.shape[1] // tensor_count
    tiles = slot_rows // TILE
    model_dim = depth * tensor_count

    swap = [(i, i ^ 1) for i in range(tensor_count)]

    def shift(step):
        return [(i, (i + 2 * step) % tensor_count) for i in range(tensor_count)]

    def product(gain, step, first, count, staged=False, carrier=True):
        vmem = pl.BlockSpec(memory_space=pltpu.VMEM)
        rows = count * TILE
        out_shape = [jax.ShapeDtypeStruct((rows, columns), jnp.bfloat16)] * 2
        if carrier:
            out_shape[1] = jax.ShapeDtypeStruct((rows + 2 * SUBLANES, columns), jnp.bfloat16)
            out_shape.append(jax.ShapeDtypeStruct((rows // LANES, LANES), jnp.float32))
        scratch = [
            pltpu.VMEM((rows, depth), jnp.bfloat16),
            pltpu.VMEM((depth, 2 * columns), jnp.bfloat16),
            pltpu.VMEM((depth,), jnp.bfloat16),
            pltpu.SemaphoreType.DMA((CUTS,)),
            pltpu.SemaphoreType.DMA((count,)),
            pltpu.SemaphoreType.DMA,
        ]
        return pl.pallas_call(
            functools.partial(product_kernel, step, chip_count, first, staged, carrier),
            in_specs=[pl.BlockSpec(memory_space=pltpu.HBM) if staged else vmem] * 3,
            out_shape=out_shape,
            out_specs=[vmem] * len(out_shape),
            scratch_shapes=scratch if staged else [],
            compiler_params=FIRST if staged else PARAMS,
            cost_estimate=COST,
        )(tokens, gain, kv_weight)

    def tables(span_offset):
        frequencies = rope_base ** (-(np.arange(HD // 2, dtype=np.float32) * 2.0) / HD)
        frequencies = np.concatenate([frequencies, frequencies])[None, :].astype(np.float32)
        shapes = [(slot_rows // BLOCK, HD)] * 2 + [(BLOCK, HD)] * 2
        made = pl.pallas_call(
            table_kernel,
            in_specs=[pl.BlockSpec(memory_space=pltpu.SMEM)] * 2 + [pl.BlockSpec(memory_space=pltpu.VMEM)],
            out_shape=[jax.ShapeDtypeStruct((8, LANES), jnp.int32)]
            + [jax.ShapeDtypeStruct(shape, jnp.float32) for shape in shapes],
            out_specs=[pl.BlockSpec(memory_space=pltpu.VMEM)] * 5,
            compiler_params=PARAMS,
            cost_estimate=COST,
        )(live_blocks, span_offset, jnp.asarray(frequencies))
        return list(made)

    def finish(first, count, keep, received, table, squares, arrived, result):
        vmem = pl.BlockSpec(memory_space=pltpu.VMEM)
        operands = [keep, received] + table + [squares] + arrived
        aliases = {len(operands): 0}
        if result is None:
            result, aliases = jnp.zeros((1,), jnp.bfloat16), {}
        return pl.pallas_call(
            functools.partial(finish_kernel, first, count, model_dim),
            in_specs=[vmem] * len(operands) + [pl.BlockSpec(memory_space=pl.ANY)],
            out_shape=jax.ShapeDtypeStruct((slot_rows, columns), jnp.bfloat16),
            out_specs=pl.BlockSpec(memory_space=pltpu.HBM),
            scratch_shapes=[pltpu.VMEM((count * TILE, columns), jnp.bfloat16), pltpu.SemaphoreType.DMA((count,))],
            input_output_aliases=aliases,
            compiler_params=PARAMS,
            cost_estimate=LATER,
        )(*operands, result)

    others = range(1, chip_count)
    firsts = [sum(CHUNKS[:index]) for index in range(len(CHUNKS))]
    chunk_count = len(CHUNKS)

    chunks = list(zip(firsts, CHUNKS))

    def add_halves(made):
        added = [
            pl.pallas_call(
                add_carrier_kernel,
                out_shape=[
                    jax.ShapeDtypeStruct(send.shape, send.dtype),
                    jax.ShapeDtypeStruct(squares.shape, squares.dtype),
                ],
                compiler_params=PARAMS,
                cost_estimate=COST,
            )(keep, lax.ppermute(send, "tensor", swap), squares)
            for keep, send, squares in made
        ]
        return [sums for sums, _ in added], added[0][1]

    def cross(sums):
        return [lax.ppermute(part, "tensor", shift(step)) for step, part in zip(others, sums)]

    hold = lax.optimization_barrier
    made = [product(norm_gain, step, *chunks[0], staged=True) for step in others]
    made, gain = hold((made, norm_gain))
    sums = add_halves(made)
    made = [product(gain, step, *chunks[1]) for step in others]
    sums, made, gain, span_offset, live_blocks = hold((sums, made, gain, span_offset, live_blocks))

    arrivals = [(cross(sums[0]), sums[1])]
    for index in range(1, chunk_count):
        if index > 1:
            made = [product(gain, step, *chunks[index]) for step in others]
        sums = add_halves(made)
        arrivals.append((cross(sums[0]), sums[1]))
    own = [product(gain, 0, first, count, carrier=False) for first, count in chunks]
    table = tables(span_offset)

    result = None
    for (first, count), (keep, send), (arrived, squares) in zip(chunks, own, arrivals):
        received = lax.ppermute(send, "tensor", swap)
        result = finish(first, count, keep, received, table, squares, arrived, result)
    return result


def solution(mesh):
    in_specs = (
        P(("groups", "serve"), "tensor"),
        P("tensor"),
        P("tensor", None),
        P("groups"),
        P("groups"),
    )
    out_specs = P(("groups", "serve"), "tensor")
    return jax.shard_map(shards, mesh=mesh, in_specs=in_specs, out_specs=out_specs, check_vma=False)
```

```python
import functools

import jax
import jax.numpy as jnp
import numpy as np
from jax import lax
from jax.experimental import pallas as pl
from jax.experimental.pallas import tpu as pltpu
from jax.sharding import PartitionSpec as P

HD = 128
PAGE = 256
BLOCK = 64
LANES = 128
SUBLANES = 8

rope_base = 500000.0
norm_eps = 1e-05

TILE = 256
CUTS = 4
CHUNKS = (2, 1, 3)

PARAMS = pltpu.CompilerParams(vmem_limit_bytes=16 * 1024 * 1024)
FIRST = pltpu.CompilerParams(vmem_limit_bytes=53248 * 1024)
LATER = pl.CostEstimate(flops=20000000000, bytes_accessed=1, transcendentals=0)
HEAVY = pl.CostEstimate(flops=1000000000000, bytes_accessed=1, transcendentals=0)
COST = pl.CostEstimate(flops=1, bytes_accessed=1, transcendentals=0)


def square_sums(rows):
    total = jnp.zeros((rows.shape[0], LANES), jnp.float32)
    for part in range(rows.shape[1] // LANES):
        wide = rows[:, part * LANES : (part + 1) * LANES].astype(jnp.float32)
        total += wide * wide
    return total


def packed(squares, width):
    per_row = width // LANES
    row = lax.broadcasted_iota(jnp.int32, (2 * SUBLANES, LANES), 0)
    parts = []
    for place in range(per_row):
        part = jnp.zeros((2 * SUBLANES, LANES), jnp.float32)
        for index, line in enumerate(squares[place::per_row]):
            high = line.astype(jnp.bfloat16).astype(jnp.float32)
            part = jnp.where(row == index, high, part)
            part = jnp.where(row == SUBLANES + index, line - high, part)
        parts.append(part)
    return jnp.concatenate(parts, axis=1).astype(jnp.bfloat16)


def unpacked(ref, line):
    index, place = divmod(line, ref.shape[1] // LANES)
    part = ref[pl.ds(ref.shape[0] - 2 * SUBLANES, 2 * SUBLANES), place * LANES : (place + 1) * LANES]
    part = part.astype(jnp.float32)
    return part[index : index + 1] + part[SUBLANES + index : SUBLANES + index + 1]


def product_kernel(step, chip_count, first, staged, carrier, tokens, gain, weight, *refs):
    refs = list(refs)
    keep, send = refs.pop(0), refs.pop(0)
    squares = refs.pop(0) if carrier else None
    count = keep.shape[0] // TILE
    depth, width = tokens.shape[1], 2 * keep.shape[1]
    me = lax.axis_index("tensor")
    core = lax.rem(me, 2)
    chip = lax.rem(lax.div(me, 2) + step, chip_count)
    place = pl.ds(pl.multiple_of(chip * width, width), width)

    weight_copies, row_copies = [], []
    if staged:
        rows_buf, weight_buf, gain_buf, weight_sems, row_sems, gain_sem = refs
        cut = depth // CUTS
        gain_copy = pltpu.make_async_copy(gain, gain_buf, gain_sem)
        for index in range(CUTS):
            some = pl.ds(index * cut, cut)
            weight_copies.append(
                pltpu.make_async_copy(weight.at[some, place], weight_buf.at[some, :], weight_sems.at[index])
            )
        for tile in range(count):
            rows = tokens.at[pl.ds((first + tile) * TILE, TILE), :]
            row_copies.append(
                pltpu.make_async_copy(rows, rows_buf.at[pl.ds(tile * TILE, TILE), :], row_sems.at[tile])
            )
        for copy in [gain_copy] + row_copies[:1] + weight_copies + row_copies[1:]:
            copy.start()
        gain_copy.wait()
        gains = gain_buf[...].reshape(1, depth)
    else:
        gains = gain[...].reshape(1, depth)

    lines = []
    for tile in range(count):
        inside = pl.ds(tile * TILE, TILE)
        if staged:
            row_copies[tile].wait()
            rows = rows_buf[inside, :]
        else:
            rows = tokens[pl.ds((first + tile) * TILE, TILE), :]
        scaled = rows * gains
        if weight_copies:
            product = jnp.zeros((TILE, width), jnp.float32)
            for index, copy in enumerate(weight_copies):
                copy.wait()
                span = slice(index * cut, (index + 1) * cut)
                product += jnp.dot(scaled[:, span], weight_buf[span, :], preferred_element_type=jnp.float32)
            weight_copies = []
        else:
            columns = weight_buf[...] if staged else weight[:, place]
            product = jnp.dot(scaled, columns, preferred_element_type=jnp.float32)
        left = product[:, : width // 2].astype(jnp.bfloat16)
        right = product[:, width // 2 :].astype(jnp.bfloat16)
        keep[inside, :] = jnp.where(core == 0, left, right)
        send[inside, :] = jnp.where(core == 0, right, left)
        if carrier:
            total = square_sums(rows)
            for part in range(TILE // LANES):
                turned = jnp.transpose(total[part * LANES : (part + 1) * LANES])
                lines.append(jnp.sum(turned, axis=0, keepdims=True))
                squares[len(lines) - 1 : len(lines), :] = lines[-1]
    if carrier:
        send[pl.ds(keep.shape[0], 2 * SUBLANES), :] = packed(lines, send.shape[1])


def add_carrier_kernel(keep, received, squares, pair_squares, out, *rest):
    low = 0
    for part in (out, *rest):
        size = part.shape[0] - (2 * SUBLANES if part is out else 0)
        rows = pl.ds(low, size)
        total = keep[rows, :].astype(jnp.float32) + received[rows, :].astype(jnp.float32)
        part[pl.ds(0, size), :] = total.astype(part.dtype)
        low += size
    lines = []
    for line in range(squares.shape[0]):
        lines.append(squares[line : line + 1, :] + unpacked(received, line))
        pair_squares[line : line + 1, :] = lines[-1]
    out[pl.ds(out.shape[0] - 2 * SUBLANES, 2 * SUBLANES), :] = packed(lines, out.shape[1])


def table_kernel(live, span, frequencies, limit, far_cos, far_sin, near_cos, near_sin):
    limit[...] = jnp.full(limit.shape, live[lax.axis_index("serve")] * BLOCK, jnp.int32)
    blocks = far_cos.shape[0]
    start = span[lax.axis_index("serve")] * PAGE
    first = start + BLOCK * lax.broadcasted_iota(jnp.int32, (blocks, HD), 0)
    far = first.astype(jnp.float32) * frequencies[...]
    near = lax.broadcasted_iota(jnp.int32, (BLOCK, HD), 0).astype(jnp.float32) * frequencies[...]
    far_cos[...] = jnp.cos(far)
    far_sin[...] = jnp.sin(far)
    near_cos[...] = jnp.cos(near)
    near_sin[...] = jnp.sin(near)


def finish_kernel(first, at, count, chip_count, model_dim, *refs):
    keep, received, limit, far_cos, far_sin, near_cos, near_sin = refs[:7]
    pair_squares, carriers = refs[7], refs[8 : 7 + chip_count]
    arrived = refs[7 + chip_count : -4] if at else carriers
    out, staged, sems = refs[-3:]
    on_diagonal = lax.broadcasted_iota(jnp.int32, (LANES, LANES), 0) == lax.broadcasted_iota(
        jnp.int32, (LANES, LANES), 1
    )
    sign = jnp.where(lax.broadcasted_iota(jnp.int32, (1, HD), 1) < HD // 2, -1.0, 1.0)
    copies = []
    for index in range(count):
        start = (first + at + index) * TILE
        rows, inside = pl.ds(start, TILE), pl.ds(index * TILE, TILE)
        of_chunk = pl.ds((at + index) * TILE, TILE)
        values = keep[of_chunk, :].astype(jnp.float32) + received[of_chunk, :].astype(jnp.float32)
        for part in arrived:
            values += part[inside, :].astype(jnp.float32)
        columns = []
        for line in range((at + index) * TILE // LANES, (at + index + 1) * TILE // LANES):
            totals = pair_squares[line : line + 1, :]
            for ref in carriers:
                totals += unpacked(ref, line)
            columns.append(jnp.sum(jnp.where(on_diagonal, totals, 0.0), axis=1, keepdims=True))
        scales = 1.0 / jnp.sqrt(jnp.concatenate(columns, axis=0) / model_dim + norm_eps)
        alive = start + lax.broadcasted_iota(jnp.int32, (TILE, LANES), 0) < limit[0:1, :]
        cosines, sines = [], []
        for block in range(start // BLOCK, (start + TILE) // BLOCK):
            block_cos = far_cos[block : block + 1, :]
            block_sin = far_sin[block : block + 1, :]
            cosines.append(block_cos * near_cos[...] - block_sin * near_sin[...])
            sines.append((sign * block_sin) * near_cos[...] + (sign * block_cos) * near_sin[...])
        cosine = jnp.concatenate(cosines, axis=0)
        sine = jnp.concatenate(sines, axis=0)
        for low in range(0, out.shape[1], 2 * HD):
            key = values[:, low : low + HD] * scales
            turned = key * cosine + pltpu.roll(key, HD // 2, 1) * sine
            staged[inside, low : low + HD] = jnp.where(alive, turned, 0.0).astype(out.dtype)
            value = values[:, low + HD : low + 2 * HD] * scales
            staged[inside, low + HD : low + 2 * HD] = jnp.where(alive, value, 0.0).astype(out.dtype)
        copies.append(pltpu.make_async_copy(staged.at[inside, :], out.at[rows, :], sems.at[index]))
        copies[-1].start()
    for copy in copies:
        copy.wait()


def shards(tokens, norm_gain, kv_weight, live_blocks, span_offset):
    tensor_count = lax.axis_size("tensor")
    chip_count = tensor_count // 2
    me = lax.axis_index("tensor")
    slot_rows, depth = tokens.shape
    columns = kv_weight.shape[1] // tensor_count
    tiles = slot_rows // TILE
    model_dim = depth * tensor_count

    swap = [(i, i ^ 1) for i in range(tensor_count)]

    def shift(step):
        return [(i, (i + 2 * step) % tensor_count) for i in range(tensor_count)]

    def product(gain, step, first, count, staged=False, carrier=True):
        vmem = pl.BlockSpec(memory_space=pltpu.VMEM)
        rows = count * TILE
        out_shape = [jax.ShapeDtypeStruct((rows, columns), jnp.bfloat16)] * 2
        if carrier:
            out_shape[1] = jax.ShapeDtypeStruct((rows + 2 * SUBLANES, columns), jnp.bfloat16)
            out_shape.append(jax.ShapeDtypeStruct((rows // LANES, LANES), jnp.float32))
        scratch = [
            pltpu.VMEM((rows, depth), jnp.bfloat16),
            pltpu.VMEM((depth, 2 * columns), jnp.bfloat16),
            pltpu.VMEM((depth,), jnp.bfloat16),
            pltpu.SemaphoreType.DMA((CUTS,)),
            pltpu.SemaphoreType.DMA((count,)),
            pltpu.SemaphoreType.DMA,
        ]
        return pl.pallas_call(
            functools.partial(product_kernel, step, chip_count, first, staged, carrier),
            in_specs=[pl.BlockSpec(memory_space=pltpu.HBM) if staged else vmem] * 3,
            out_shape=out_shape,
            out_specs=[vmem] * len(out_shape),
            scratch_shapes=scratch if staged else [],
            compiler_params=FIRST if staged else PARAMS,
            cost_estimate=HEAVY if staged else COST,
        )(tokens, gain, kv_weight)

    def tables(span_offset):
        frequencies = rope_base ** (-(np.arange(HD // 2, dtype=np.float32) * 2.0) / HD)
        frequencies = np.concatenate([frequencies, frequencies])[None, :].astype(np.float32)
        shapes = [(slot_rows // BLOCK, HD)] * 2 + [(BLOCK, HD)] * 2
        made = pl.pallas_call(
            table_kernel,
            in_specs=[pl.BlockSpec(memory_space=pltpu.SMEM)] * 2 + [pl.BlockSpec(memory_space=pltpu.VMEM)],
            out_shape=[jax.ShapeDtypeStruct((8, LANES), jnp.int32)]
            + [jax.ShapeDtypeStruct(shape, jnp.float32) for shape in shapes],
            out_specs=[pl.BlockSpec(memory_space=pltpu.VMEM)] * 5,
            compiler_params=PARAMS,
            cost_estimate=COST,
        )(live_blocks, span_offset, jnp.asarray(frequencies))
        return list(made)

    def finish(first, at, count, keep, received, table, squares, carriers, arrived, result):
        vmem = pl.BlockSpec(memory_space=pltpu.VMEM)
        operands = [keep, received] + table + [squares] + carriers + (arrived if at else [])
        aliases = {len(operands): 0}
        if result is None:
            result, aliases = jnp.zeros((1,), jnp.bfloat16), {}
        return pl.pallas_call(
            functools.partial(finish_kernel, first, at, count, chip_count, model_dim),
            in_specs=[vmem] * len(operands) + [pl.BlockSpec(memory_space=pl.ANY)],
            out_shape=jax.ShapeDtypeStruct((slot_rows, columns), jnp.bfloat16),
            out_specs=pl.BlockSpec(memory_space=pltpu.HBM),
            scratch_shapes=[pltpu.VMEM((count * TILE, columns), jnp.bfloat16), pltpu.SemaphoreType.DMA((count,))],
            input_output_aliases=aliases,
            compiler_params=PARAMS,
            cost_estimate=LATER,
        )(*operands, result)

    others = range(1, chip_count)
    firsts = [sum(CHUNKS[:index]) for index in range(len(CHUNKS))]
    chunk_count = len(CHUNKS)

    chunks = list(zip(firsts, CHUNKS))

    def add_halves(made, counts):
        sizes = [count * TILE for count in counts]
        sizes[0] += 2 * SUBLANES
        added = [
            pl.pallas_call(
                add_carrier_kernel,
                out_shape=[jax.ShapeDtypeStruct(squares.shape, squares.dtype)]
                + [jax.ShapeDtypeStruct((size, columns), keep.dtype) for size in sizes],
                compiler_params=PARAMS,
                cost_estimate=COST,
            )(keep, lax.ppermute(send, "tensor", swap), squares)
            for keep, send, squares in made
        ]
        return [list(parts) for parts in zip(*[parts[1:] for parts in added])], added[0][0]

    def cross(sums):
        return [lax.ppermute(part, "tensor", shift(step)) for step, part in zip(others, sums)]

    hold = lax.optimization_barrier
    made = [product(norm_gain, step, *chunks[0], staged=True) for step in others]
    made, gain = hold((made, norm_gain))
    sums = add_halves(made, chunks[0][1:])
    sums, gain, span_offset, live_blocks = hold((sums, gain, span_offset, live_blocks))

    arrivals = [([cross(part) for part in sums[0]], sums[1])]
    for index in range(1, chunk_count):
        made = [product(gain, step, *chunks[index]) for step in others]
        count = chunks[index][1]
        sums = add_halves(made, (count - 1, 1) if count > 2 else (count,))
        arrivals.append(([cross(part) for part in sums[0]], sums[1]))
    own = [product(gain, 0, first, count, carrier=False) for first, count in chunks]
    table = tables(span_offset)

    result = None
    for (first, count), (keep, send), (arrived, squares) in zip(chunks, own, arrivals):
        received = lax.ppermute(send, "tensor", swap)
        at = 0
        for part in arrived:
            size = part[0].shape[0] // TILE
            result = finish(first, at, size, keep, received, table, squares, arrived[0], part, result)
            at += size
    return result


def solution(mesh):
    in_specs = (
        P(("groups", "serve"), "tensor"),
        P("tensor"),
        P("tensor", None),
        P("groups"),
        P("groups"),
    )
    out_specs = P(("groups", "serve"), "tensor")
    return jax.shard_map(shards, mesh=mesh, in_specs=in_specs, out_specs=out_specs, check_vma=False)
```

```python
import functools

import jax
import jax.numpy as jnp
import numpy as np
from jax import lax
from jax.experimental import pallas as pl
from jax.experimental.pallas import tpu as pltpu
from jax.sharding import PartitionSpec as P

HD = 128
PAGE = 256
BLOCK = 64
LANES = 128
SUBLANES = 8

rope_base = 500000.0
norm_eps = 1e-05

TILE = 256
CUTS = 4
CHUNKS = (2, 1, 3)

PARAMS = pltpu.CompilerParams(vmem_limit_bytes=16 * 1024 * 1024)
FIRST = pltpu.CompilerParams(vmem_limit_bytes=57344 * 1024)
LATER = pl.CostEstimate(flops=20000000000, bytes_accessed=1, transcendentals=0)
COST = pl.CostEstimate(flops=1, bytes_accessed=1, transcendentals=0)


def square_sums(rows):
    total = jnp.zeros((rows.shape[0], LANES), jnp.float32)
    for part in range(rows.shape[1] // LANES):
        wide = rows[:, part * LANES : (part + 1) * LANES].astype(jnp.float32)
        total += wide * wide
    return total


def packed(squares, width):
    per_row = width // LANES
    row = lax.broadcasted_iota(jnp.int32, (2 * SUBLANES, LANES), 0)
    parts = []
    for place in range(per_row):
        part = jnp.zeros((2 * SUBLANES, LANES), jnp.float32)
        for index, line in enumerate(squares[place::per_row]):
            high = line.astype(jnp.bfloat16).astype(jnp.float32)
            part = jnp.where(row == index, high, part)
            part = jnp.where(row == SUBLANES + index, line - high, part)
        parts.append(part)
    return jnp.concatenate(parts, axis=1).astype(jnp.bfloat16)


def unpacked(ref, line):
    index, place = divmod(line, ref.shape[1] // LANES)
    part = ref[pl.ds(ref.shape[0] - 2 * SUBLANES, 2 * SUBLANES), place * LANES : (place + 1) * LANES]
    part = part.astype(jnp.float32)
    return part[index : index + 1] + part[SUBLANES + index : SUBLANES + index + 1]


def product_kernel(step, chip_count, first, staged, carrier, tokens, gain, weight, *refs):
    refs = list(refs)
    keep, send = refs.pop(0), refs.pop(0)
    squares = refs.pop(0) if carrier else None
    count = keep.shape[0] // TILE
    depth, width = tokens.shape[1], 2 * keep.shape[1]
    me = lax.axis_index("tensor")
    core = lax.rem(me, 2)
    chip = lax.rem(lax.div(me, 2) + step, chip_count)
    place = pl.ds(pl.multiple_of(chip * width, width), width)

    weight_copies, row_copies = [], []
    if staged:
        rows_buf, weight_buf, gain_buf, weight_sems, row_sems, gain_sem = refs
        cut = depth // CUTS
        gain_copy = pltpu.make_async_copy(gain, gain_buf, gain_sem)
        for index in range(CUTS):
            some = pl.ds(index * cut, cut)
            weight_copies.append(
                pltpu.make_async_copy(weight.at[some, place], weight_buf.at[some, :], weight_sems.at[index])
            )
        for tile in range(count):
            rows = tokens.at[pl.ds((first + tile) * TILE, TILE), :]
            row_copies.append(
                pltpu.make_async_copy(rows, rows_buf.at[pl.ds(tile * TILE, TILE), :], row_sems.at[tile])
            )
        for copy in [gain_copy] + row_copies[:1] + weight_copies + row_copies[1:]:
            copy.start()
        gain_copy.wait()
        gains = gain_buf[...].reshape(1, depth)
    else:
        gains = gain[...].reshape(1, depth)

    lines = []
    for tile in range(count):
        inside = pl.ds(tile * TILE, TILE)
        if staged:
            row_copies[tile].wait()
            rows = rows_buf[inside, :]
        else:
            rows = tokens[pl.ds((first + tile) * TILE, TILE), :]
        scaled = rows * gains
        if weight_copies:
            product = jnp.zeros((TILE, width), jnp.float32)
            for index, copy in enumerate(weight_copies):
                copy.wait()
                span = slice(index * cut, (index + 1) * cut)
                product += jnp.dot(scaled[:, span], weight_buf[span, :], preferred_element_type=jnp.float32)
            weight_copies = []
        else:
            columns = weight_buf[...] if staged else weight[:, place]
            product = jnp.dot(scaled, columns, preferred_element_type=jnp.float32)
        left = product[:, : width // 2].astype(jnp.bfloat16)
        right = product[:, width // 2 :].astype(jnp.bfloat16)
        keep[inside, :] = jnp.where(core == 0, left, right)
        send[inside, :] = jnp.where(core == 0, right, left)
        if carrier:
            total = square_sums(rows)
            for part in range(TILE // LANES):
                turned = jnp.transpose(total[part * LANES : (part + 1) * LANES])
                lines.append(jnp.sum(turned, axis=0, keepdims=True))
                squares[len(lines) - 1 : len(lines), :] = lines[-1]
    if carrier:
        send[pl.ds(keep.shape[0], 2 * SUBLANES), :] = packed(lines, send.shape[1])


def add_carrier_kernel(keep, received, squares, pair_squares, out, *rest):
    low = 0
    for part in (out, *rest):
        size = part.shape[0] - (2 * SUBLANES if part is out else 0)
        rows = pl.ds(low, size)
        total = keep[rows, :].astype(jnp.float32) + received[rows, :].astype(jnp.float32)
        part[pl.ds(0, size), :] = total.astype(part.dtype)
        low += size
    lines = []
    for line in range(squares.shape[0]):
        lines.append(squares[line : line + 1, :] + unpacked(received, line))
        pair_squares[line : line + 1, :] = lines[-1]
    out[pl.ds(out.shape[0] - 2 * SUBLANES, 2 * SUBLANES), :] = packed(lines, out.shape[1])


def table_kernel(live, span, frequencies, limit, far_cos, far_sin, near_cos, near_sin):
    limit[...] = jnp.full(limit.shape, live[lax.axis_index("serve")] * BLOCK, jnp.int32)
    blocks = far_cos.shape[0]
    start = span[lax.axis_index("serve")] * PAGE
    first = start + BLOCK * lax.broadcasted_iota(jnp.int32, (blocks, HD), 0)
    far = first.astype(jnp.float32) * frequencies[...]
    near = lax.broadcasted_iota(jnp.int32, (BLOCK, HD), 0).astype(jnp.float32) * frequencies[...]
    far_cos[...] = jnp.cos(far)
    far_sin[...] = jnp.sin(far)
    near_cos[...] = jnp.cos(near)
    near_sin[...] = jnp.sin(near)


def finish_kernel(first, at, count, chip_count, model_dim, *refs):
    keep, received, limit, far_cos, far_sin, near_cos, near_sin = refs[:7]
    pair_squares, carriers = refs[7], refs[8 : 7 + chip_count]
    arrived = refs[7 + chip_count : -4] if at else carriers
    out, staged, sems = refs[-3:]
    on_diagonal = lax.broadcasted_iota(jnp.int32, (LANES, LANES), 0) == lax.broadcasted_iota(
        jnp.int32, (LANES, LANES), 1
    )
    sign = jnp.where(lax.broadcasted_iota(jnp.int32, (1, HD), 1) < HD // 2, -1.0, 1.0)
    copies = []
    for index in range(count):
        start = (first + at + index) * TILE
        rows, inside = pl.ds(start, TILE), pl.ds(index * TILE, TILE)
        of_chunk = pl.ds((at + index) * TILE, TILE)
        values = keep[of_chunk, :].astype(jnp.float32) + received[of_chunk, :].astype(jnp.float32)
        for part in arrived:
            values += part[inside, :].astype(jnp.float32)
        columns = []
        for line in range((at + index) * TILE // LANES, (at + index + 1) * TILE // LANES):
            totals = pair_squares[line : line + 1, :]
            for ref in carriers:
                totals += unpacked(ref, line)
            columns.append(jnp.sum(jnp.where(on_diagonal, totals, 0.0), axis=1, keepdims=True))
        scales = 1.0 / jnp.sqrt(jnp.concatenate(columns, axis=0) / model_dim + norm_eps)
        alive = start + lax.broadcasted_iota(jnp.int32, (TILE, LANES), 0) < limit[0:1, :]
        cosines, sines = [], []
        for block in range(start // BLOCK, (start + TILE) // BLOCK):
            block_cos = far_cos[block : block + 1, :]
            block_sin = far_sin[block : block + 1, :]
            cosines.append(block_cos * near_cos[...] - block_sin * near_sin[...])
            sines.append((sign * block_sin) * near_cos[...] + (sign * block_cos) * near_sin[...])
        cosine = jnp.concatenate(cosines, axis=0)
        sine = jnp.concatenate(sines, axis=0)
        for low in range(0, out.shape[1], 2 * HD):
            key = values[:, low : low + HD] * scales
            turned = key * cosine + pltpu.roll(key, HD // 2, 1) * sine
            staged[inside, low : low + HD] = jnp.where(alive, turned, 0.0).astype(out.dtype)
            value = values[:, low + HD : low + 2 * HD] * scales
            staged[inside, low + HD : low + 2 * HD] = jnp.where(alive, value, 0.0).astype(out.dtype)
        copies.append(pltpu.make_async_copy(staged.at[inside, :], out.at[rows, :], sems.at[index]))
        copies[-1].start()
    for copy in copies:
        copy.wait()


def shards(tokens, norm_gain, kv_weight, live_blocks, span_offset):
    tensor_count = lax.axis_size("tensor")
    chip_count = tensor_count // 2
    me = lax.axis_index("tensor")
    slot_rows, depth = tokens.shape
    columns = kv_weight.shape[1] // tensor_count
    tiles = slot_rows // TILE
    model_dim = depth * tensor_count

    swap = [(i, i ^ 1) for i in range(tensor_count)]

    def shift(step):
        return [(i, (i + 2 * step) % tensor_count) for i in range(tensor_count)]

    def product(gain, step, first, count, staged=False, carrier=True):
        vmem = pl.BlockSpec(memory_space=pltpu.VMEM)
        rows = count * TILE
        out_shape = [jax.ShapeDtypeStruct((rows, columns), jnp.bfloat16)] * 2
        if carrier:
            out_shape[1] = jax.ShapeDtypeStruct((rows + 2 * SUBLANES, columns), jnp.bfloat16)
            out_shape.append(jax.ShapeDtypeStruct((rows // LANES, LANES), jnp.float32))
        scratch = [
            pltpu.VMEM((rows, depth), jnp.bfloat16),
            pltpu.VMEM((depth, 2 * columns), jnp.bfloat16),
            pltpu.VMEM((depth,), jnp.bfloat16),
            pltpu.SemaphoreType.DMA((CUTS,)),
            pltpu.SemaphoreType.DMA((count,)),
            pltpu.SemaphoreType.DMA,
        ]
        return pl.pallas_call(
            functools.partial(product_kernel, step, chip_count, first, staged, carrier),
            in_specs=[pl.BlockSpec(memory_space=pltpu.HBM) if staged else vmem] * 3,
            out_shape=out_shape,
            out_specs=[vmem] * len(out_shape),
            scratch_shapes=scratch if staged else [],
            compiler_params=FIRST if staged else PARAMS,
            cost_estimate=COST,
        )(tokens, gain, kv_weight)

    def tables(live_blocks, span_offset):
        frequencies = rope_base ** (-(np.arange(HD // 2, dtype=np.float32) * 2.0) / HD)
        frequencies = np.concatenate([frequencies, frequencies])[None, :].astype(np.float32)
        shapes = [(slot_rows // BLOCK, HD)] * 2 + [(BLOCK, HD)] * 2
        made = pl.pallas_call(
            table_kernel,
            in_specs=[pl.BlockSpec(memory_space=pltpu.SMEM)] * 2 + [pl.BlockSpec(memory_space=pltpu.VMEM)],
            out_shape=[jax.ShapeDtypeStruct((8, LANES), jnp.int32)]
            + [jax.ShapeDtypeStruct(shape, jnp.float32) for shape in shapes],
            out_specs=[pl.BlockSpec(memory_space=pltpu.VMEM)] * 5,
            compiler_params=PARAMS,
            cost_estimate=COST,
        )(live_blocks, span_offset, jnp.asarray(frequencies))
        return list(made)

    def finish(first, at, count, keep, received, table, squares, carriers, arrived, result):
        vmem = pl.BlockSpec(memory_space=pltpu.VMEM)
        operands = [keep, received] + table + [squares] + carriers + (arrived if at else [])
        aliases = {len(operands): 0}
        if result is None:
            result, aliases = jnp.zeros((1,), jnp.bfloat16), {}
        return pl.pallas_call(
            functools.partial(finish_kernel, first, at, count, chip_count, model_dim),
            in_specs=[vmem] * len(operands) + [pl.BlockSpec(memory_space=pl.ANY)],
            out_shape=jax.ShapeDtypeStruct((slot_rows, columns), jnp.bfloat16),
            out_specs=pl.BlockSpec(memory_space=pltpu.HBM),
            scratch_shapes=[pltpu.VMEM((count * TILE, columns), jnp.bfloat16), pltpu.SemaphoreType.DMA((count,))],
            input_output_aliases=aliases,
            compiler_params=PARAMS,
            cost_estimate=LATER,
        )(*operands, result)

    others = range(1, chip_count)
    firsts = [sum(CHUNKS[:index]) for index in range(len(CHUNKS))]
    chunk_count = len(CHUNKS)

    chunks = list(zip(firsts, CHUNKS))

    def add_halves(made, counts):
        sizes = [count * TILE for count in counts]
        sizes[0] += 2 * SUBLANES
        added = [
            pl.pallas_call(
                add_carrier_kernel,
                out_shape=[jax.ShapeDtypeStruct(squares.shape, squares.dtype)]
                + [jax.ShapeDtypeStruct((size, columns), keep.dtype) for size in sizes],
                compiler_params=PARAMS,
                cost_estimate=COST,
            )(keep, lax.ppermute(send, "tensor", swap), squares)
            for keep, send, squares in made
        ]
        return [list(parts) for parts in zip(*[parts[1:] for parts in added])], added[0][0]

    def cross(sums):
        return [lax.ppermute(part, "tensor", shift(step)) for step, part in zip(others, sums)]

    hold = lax.optimization_barrier
    made = [product(norm_gain, step, *chunks[0], staged=True) for step in others]
    made, gain = hold((made, norm_gain))
    sums = add_halves(made, chunks[0][1:])
    made = [product(gain, step, *chunks[1]) for step in others]
    sums, made, gain, span_offset, live_blocks = hold((sums, made, gain, span_offset, live_blocks))

    arrivals = [([cross(part) for part in sums[0]], sums[1])]
    for index in range(1, chunk_count):
        if index > 1:
            made = [product(gain, step, *chunks[index]) for step in others]
        count = chunks[index][1]
        sums = add_halves(made, (count - 1, 1) if count > 2 else (count,))
        arrivals.append(([cross(part) for part in sums[0]], sums[1]))
    arrivals[0], late, span_offset, live_blocks = hold((arrivals[0], gain, span_offset, live_blocks))
    own = [product(gain, 0, *chunk, carrier=False)[:2] for chunk in chunks[:-1]]
    own.append(product(late, 0, *chunks[-1], carrier=False)[:2])
    table = tables(live_blocks, span_offset)

    result = None
    for (first, count), (keep, send), (arrived, squares) in zip(chunks, own, arrivals):
        received = lax.ppermute(send, "tensor", swap)
        at = 0
        for part in arrived:
            size = part[0].shape[0] // TILE
            result = finish(first, at, size, keep, received, table, squares, arrived[0], part, result)
            at += size
    return result


def solution(mesh):
    in_specs = (
        P(("groups", "serve"), "tensor"),
        P("tensor"),
        P("tensor", None),
        P("groups"),
        P("groups"),
    )
    out_specs = P(("groups", "serve"), "tensor")
    return jax.shard_map(shards, mesh=mesh, in_specs=in_specs, out_specs=out_specs, check_vma=False)
```

```python
import functools

import jax
import jax.numpy as jnp
import numpy as np
from jax import lax
from jax.experimental import pallas as pl
from jax.experimental.pallas import tpu as pltpu
from jax.sharding import PartitionSpec as P

HD = 128
PAGE = 256
BLOCK = 64
LANES = 128
SUBLANES = 8

rope_base = 500000.0
norm_eps = 1e-05

TILE = 256
CUTS = 4
CHUNKS = (2, 1, 3)

PARAMS = pltpu.CompilerParams(vmem_limit_bytes=16 * 1024 * 1024)
FIRST = pltpu.CompilerParams(vmem_limit_bytes=56 * 1024 * 1024)
LATER = pl.CostEstimate(flops=20000000000, bytes_accessed=1, transcendentals=0)
COST = pl.CostEstimate(flops=1, bytes_accessed=1, transcendentals=0)


def square_sums(rows):
    total = jnp.zeros((rows.shape[0], LANES), jnp.float32)
    for part in range(rows.shape[1] // LANES):
        wide = rows[:, part * LANES : (part + 1) * LANES].astype(jnp.float32)
        total += wide * wide
    return total


def packed(squares, width):
    per_row = width // LANES
    row = lax.broadcasted_iota(jnp.int32, (2 * SUBLANES, LANES), 0)
    parts = []
    for place in range(per_row):
        part = jnp.zeros((2 * SUBLANES, LANES), jnp.float32)
        for index, line in enumerate(squares[place::per_row]):
            high = line.astype(jnp.bfloat16).astype(jnp.float32)
            part = jnp.where(row == index, high, part)
            part = jnp.where(row == SUBLANES + index, line - high, part)
        parts.append(part)
    return jnp.concatenate(parts, axis=1).astype(jnp.bfloat16)


def unpacked(ref, line):
    index, place = divmod(line, ref.shape[1] // LANES)
    part = ref[pl.ds(ref.shape[0] - 2 * SUBLANES, 2 * SUBLANES), place * LANES : (place + 1) * LANES]
    part = part.astype(jnp.float32)
    return part[index : index + 1] + part[SUBLANES + index : SUBLANES + index + 1]


def product_kernel(step, chip_count, first, staged, carrier, tokens, gain, weight, *refs):
    refs = list(refs)
    keep, send = refs.pop(0), refs.pop(0)
    squares = refs.pop(0) if carrier else None
    count = keep.shape[0] // TILE
    depth, width = tokens.shape[1], 2 * keep.shape[1]
    me = lax.axis_index("tensor")
    core = lax.rem(me, 2)
    chip = lax.rem(lax.div(me, 2) + step, chip_count)
    place = pl.ds(pl.multiple_of(chip * width, width), width)

    weight_copies, row_copies = [], []
    if staged:
        rows_buf, weight_buf, gain_buf, weight_sems, row_sems, gain_sem = refs
        cut = depth // CUTS
        gain_copy = pltpu.make_async_copy(gain, gain_buf, gain_sem)
        for index in range(CUTS):
            some = pl.ds(index * cut, cut)
            weight_copies.append(
                pltpu.make_async_copy(weight.at[some, place], weight_buf.at[some, :], weight_sems.at[index])
            )
        for tile in range(count):
            rows = tokens.at[pl.ds((first + tile) * TILE, TILE), :]
            row_copies.append(
                pltpu.make_async_copy(rows, rows_buf.at[pl.ds(tile * TILE, TILE), :], row_sems.at[tile])
            )
        for copy in [gain_copy] + row_copies[:1] + weight_copies + row_copies[1:]:
            copy.start()
        gain_copy.wait()
        gains = gain_buf[...].reshape(1, depth)
    else:
        gains = gain[...].reshape(1, depth)

    lines = []
    for tile in range(count):
        inside = pl.ds(tile * TILE, TILE)
        if staged:
            row_copies[tile].wait()
            rows = rows_buf[inside, :]
        else:
            rows = tokens[pl.ds((first + tile) * TILE, TILE), :]
        scaled = rows * gains
        if weight_copies:
            product = jnp.zeros((TILE, width), jnp.float32)
            for index, copy in enumerate(weight_copies):
                copy.wait()
                span = slice(index * cut, (index + 1) * cut)
                product += jnp.dot(scaled[:, span], weight_buf[span, :], preferred_element_type=jnp.float32)
            weight_copies = []
        else:
            columns = weight_buf[...] if staged else weight[:, place]
            product = jnp.dot(scaled, columns, preferred_element_type=jnp.float32)
        left = product[:, : width // 2].astype(jnp.bfloat16)
        right = product[:, width // 2 :].astype(jnp.bfloat16)
        keep[inside, :] = jnp.where(core == 0, left, right)
        send[inside, :] = jnp.where(core == 0, right, left)
        if carrier:
            total = square_sums(rows)
            for part in range(TILE // LANES):
                turned = jnp.transpose(total[part * LANES : (part + 1) * LANES])
                lines.append(jnp.sum(turned, axis=0, keepdims=True))
                squares[len(lines) - 1 : len(lines), :] = lines[-1]
    if carrier:
        send[pl.ds(keep.shape[0], 2 * SUBLANES), :] = packed(lines, send.shape[1])


def add_carrier_kernel(keep, received, squares, pair_squares, out, *rest):
    low = 0
    for part in (out, *rest):
        size = part.shape[0] - (2 * SUBLANES if part is out else 0)
        rows = pl.ds(low, size)
        total = keep[rows, :].astype(jnp.float32) + received[rows, :].astype(jnp.float32)
        part[pl.ds(0, size), :] = total.astype(part.dtype)
        low += size
    lines = []
    for line in range(squares.shape[0]):
        lines.append(squares[line : line + 1, :] + unpacked(received, line))
        pair_squares[line : line + 1, :] = lines[-1]
    out[pl.ds(out.shape[0] - 2 * SUBLANES, 2 * SUBLANES), :] = packed(lines, out.shape[1])


def table_kernel(live, span, frequencies, limit, far_cos, far_sin, near_cos, near_sin):
    limit[...] = jnp.full(limit.shape, live[lax.axis_index("serve")] * BLOCK, jnp.int32)
    blocks = far_cos.shape[0]
    start = span[lax.axis_index("serve")] * PAGE
    first = start + BLOCK * lax.broadcasted_iota(jnp.int32, (blocks, HD), 0)
    far = first.astype(jnp.float32) * frequencies[...]
    near = lax.broadcasted_iota(jnp.int32, (BLOCK, HD), 0).astype(jnp.float32) * frequencies[...]
    far_cos[...] = jnp.cos(far)
    far_sin[...] = jnp.sin(far)
    near_cos[...] = jnp.cos(near)
    near_sin[...] = jnp.sin(near)


def finish_kernel(first, at, count, chip_count, model_dim, *refs):
    keep, received, limit, far_cos, far_sin, near_cos, near_sin = refs[:7]
    pair_squares, carriers = refs[7], refs[8 : 7 + chip_count]
    arrived = refs[7 + chip_count : -4] if at else carriers
    out, staged, sems = refs[-3:]
    on_diagonal = lax.broadcasted_iota(jnp.int32, (LANES, LANES), 0) == lax.broadcasted_iota(
        jnp.int32, (LANES, LANES), 1
    )
    sign = jnp.where(lax.broadcasted_iota(jnp.int32, (1, HD), 1) < HD // 2, -1.0, 1.0)
    copies = []
    for index in range(count):
        start = (first + at + index) * TILE
        rows, inside = pl.ds(start, TILE), pl.ds(index * TILE, TILE)
        of_chunk = pl.ds((at + index) * TILE, TILE)
        values = keep[of_chunk, :].astype(jnp.float32) + received[of_chunk, :].astype(jnp.float32)
        for part in arrived:
            values += part[inside, :].astype(jnp.float32)
        columns = []
        for line in range((at + index) * TILE // LANES, (at + index + 1) * TILE // LANES):
            totals = pair_squares[line : line + 1, :]
            for ref in carriers:
                totals += unpacked(ref, line)
            columns.append(jnp.sum(jnp.where(on_diagonal, totals, 0.0), axis=1, keepdims=True))
        scales = 1.0 / jnp.sqrt(jnp.concatenate(columns, axis=0) / model_dim + norm_eps)
        alive = start + lax.broadcasted_iota(jnp.int32, (TILE, LANES), 0) < limit[0:1, :]
        cosines, sines = [], []
        for block in range(start // BLOCK, (start + TILE) // BLOCK):
            block_cos = far_cos[block : block + 1, :]
            block_sin = far_sin[block : block + 1, :]
            cosines.append(block_cos * near_cos[...] - block_sin * near_sin[...])
            sines.append((sign * block_sin) * near_cos[...] + (sign * block_cos) * near_sin[...])
        cosine = jnp.concatenate(cosines, axis=0)
        sine = jnp.concatenate(sines, axis=0)
        for low in range(0, out.shape[1], 2 * HD):
            key = values[:, low : low + HD] * scales
            turned = key * cosine + pltpu.roll(key, HD // 2, 1) * sine
            staged[inside, low : low + HD] = jnp.where(alive, turned, 0.0).astype(out.dtype)
            value = values[:, low + HD : low + 2 * HD] * scales
            staged[inside, low + HD : low + 2 * HD] = jnp.where(alive, value, 0.0).astype(out.dtype)
        copies.append(pltpu.make_async_copy(staged.at[inside, :], out.at[rows, :], sems.at[index]))
        copies[-1].start()
    for copy in copies:
        copy.wait()


def shards(tokens, norm_gain, kv_weight, live_blocks, span_offset):
    tensor_count = lax.axis_size("tensor")
    chip_count = tensor_count // 2
    me = lax.axis_index("tensor")
    slot_rows, depth = tokens.shape
    columns = kv_weight.shape[1] // tensor_count
    tiles = slot_rows // TILE
    model_dim = depth * tensor_count

    swap = [(i, i ^ 1) for i in range(tensor_count)]

    def shift(step):
        return [(i, (i + 2 * step) % tensor_count) for i in range(tensor_count)]

    def product(gain, step, first, count, staged=False, carrier=True):
        vmem = pl.BlockSpec(memory_space=pltpu.VMEM)
        rows = count * TILE
        out_shape = [jax.ShapeDtypeStruct((rows, columns), jnp.bfloat16)] * 2
        if carrier:
            out_shape[1] = jax.ShapeDtypeStruct((rows + 2 * SUBLANES, columns), jnp.bfloat16)
            out_shape.append(jax.ShapeDtypeStruct((rows // LANES, LANES), jnp.float32))
        scratch = [
            pltpu.VMEM((rows, depth), jnp.bfloat16),
            pltpu.VMEM((depth, 2 * columns), jnp.bfloat16),
            pltpu.VMEM((depth,), jnp.bfloat16),
            pltpu.SemaphoreType.DMA((CUTS,)),
            pltpu.SemaphoreType.DMA((count,)),
            pltpu.SemaphoreType.DMA,
        ]
        return pl.pallas_call(
            functools.partial(product_kernel, step, chip_count, first, staged, carrier),
            in_specs=[pl.BlockSpec(memory_space=pltpu.HBM) if staged else vmem] * 3,
            out_shape=out_shape,
            out_specs=[vmem] * len(out_shape),
            scratch_shapes=scratch if staged else [],
            compiler_params=FIRST if staged else PARAMS,
            cost_estimate=COST,
        )(tokens, gain, kv_weight)

    def tables(span_offset):
        frequencies = rope_base ** (-(np.arange(HD // 2, dtype=np.float32) * 2.0) / HD)
        frequencies = np.concatenate([frequencies, frequencies])[None, :].astype(np.float32)
        shapes = [(slot_rows // BLOCK, HD)] * 2 + [(BLOCK, HD)] * 2
        made = pl.pallas_call(
            table_kernel,
            in_specs=[pl.BlockSpec(memory_space=pltpu.SMEM)] * 2 + [pl.BlockSpec(memory_space=pltpu.VMEM)],
            out_shape=[jax.ShapeDtypeStruct((8, LANES), jnp.int32)]
            + [jax.ShapeDtypeStruct(shape, jnp.float32) for shape in shapes],
            out_specs=[pl.BlockSpec(memory_space=pltpu.VMEM)] * 5,
            compiler_params=PARAMS,
            cost_estimate=COST,
        )(live_blocks, span_offset, jnp.asarray(frequencies))
        return list(made)

    def finish(first, at, count, keep, received, table, squares, carriers, arrived, result):
        vmem = pl.BlockSpec(memory_space=pltpu.VMEM)
        operands = [keep, received] + table + [squares] + carriers + (arrived if at else [])
        aliases = {len(operands): 0}
        if result is None:
            result, aliases = jnp.zeros((1,), jnp.bfloat16), {}
        return pl.pallas_call(
            functools.partial(finish_kernel, first, at, count, chip_count, model_dim),
            in_specs=[vmem] * len(operands) + [pl.BlockSpec(memory_space=pl.ANY)],
            out_shape=jax.ShapeDtypeStruct((slot_rows, columns), jnp.bfloat16),
            out_specs=pl.BlockSpec(memory_space=pltpu.HBM),
            scratch_shapes=[pltpu.VMEM((count * TILE, columns), jnp.bfloat16), pltpu.SemaphoreType.DMA((count,))],
            input_output_aliases=aliases,
            compiler_params=PARAMS,
            cost_estimate=LATER,
        )(*operands, result)

    others = range(1, chip_count)
    firsts = [sum(CHUNKS[:index]) for index in range(len(CHUNKS))]
    chunk_count = len(CHUNKS)

    chunks = list(zip(firsts, CHUNKS))

    def add_halves(made, counts):
        sizes = [count * TILE for count in counts]
        sizes[0] += 2 * SUBLANES
        added = [
            pl.pallas_call(
                add_carrier_kernel,
                out_shape=[jax.ShapeDtypeStruct(squares.shape, squares.dtype)]
                + [jax.ShapeDtypeStruct((size, columns), keep.dtype) for size in sizes],
                compiler_params=PARAMS,
                cost_estimate=COST,
            )(keep, lax.ppermute(send, "tensor", swap), squares)
            for keep, send, squares in made
        ]
        return [list(parts) for parts in zip(*[parts[1:] for parts in added])], added[0][0]

    def cross(sums):
        return [lax.ppermute(part, "tensor", shift(step)) for step, part in zip(others, sums)]

    hold = lax.optimization_barrier
    made = [product(norm_gain, step, *chunks[0], staged=True) for step in others]
    made, gain = hold((made, norm_gain))
    sums = add_halves(made, chunks[0][1:])
    made = [product(gain, step, *chunks[1]) for step in others]
    sums, made, gain, span_offset, live_blocks = hold((sums, made, gain, span_offset, live_blocks))

    arrivals = [([cross(part) for part in sums[0]], sums[1])]
    for index in range(1, chunk_count):
        if index > 1:
            made = [product(gain, step, *chunks[index]) for step in others]
        count = chunks[index][1]
        sums = add_halves(made, (count - 1, 1) if count > 2 else (count,))
        arrivals.append(([cross(part) for part in sums[0]], sums[1]))
    own = [product(gain, 0, first, count, carrier=False) for first, count in chunks]
    table = tables(span_offset)

    result = None
    for (first, count), (keep, send), (arrived, squares) in zip(chunks, own, arrivals):
        received = lax.ppermute(send, "tensor", swap)
        at = 0
        for part in arrived:
            size = part[0].shape[0] // TILE
            result = finish(first, at, size, keep, received, table, squares, arrived[0], part, result)
            at += size
    return result


def solution(mesh):
    in_specs = (
        P(("groups", "serve"), "tensor"),
        P("tensor"),
        P("tensor", None),
        P("groups"),
        P("groups"),
    )
    out_specs = P(("groups", "serve"), "tensor")
    return jax.shard_map(shards, mesh=mesh, in_specs=in_specs, out_specs=out_specs, check_vma=False)
```

```python
import functools

import jax
import jax.numpy as jnp
import numpy as np
from jax import lax
from jax.experimental import pallas as pl
from jax.experimental.pallas import tpu as pltpu
from jax.sharding import PartitionSpec as P

HD = 128
PAGE = 256
BLOCK = 64
LANES = 128
SUBLANES = 8

rope_base = 500000.0
norm_eps = 1e-05

TILE = 256
CUTS = 4
CHUNKS = (2, 1, 3)

PARAMS = pltpu.CompilerParams(vmem_limit_bytes=16 * 1024 * 1024)
FIRST = pltpu.CompilerParams(vmem_limit_bytes=53248 * 1024)
LATER = pl.CostEstimate(flops=20000000000, bytes_accessed=1, transcendentals=0)
HEAVY = pl.CostEstimate(flops=1000000000000, bytes_accessed=1, transcendentals=0)
COST = pl.CostEstimate(flops=1, bytes_accessed=1, transcendentals=0)


def square_sums(rows):
    total = jnp.zeros((rows.shape[0], LANES), jnp.float32)
    for part in range(rows.shape[1] // LANES):
        wide = rows[:, part * LANES : (part + 1) * LANES].astype(jnp.float32)
        total += wide * wide
    return total


def packed(squares, width):
    per_row = width // LANES
    row = lax.broadcasted_iota(jnp.int32, (2 * SUBLANES, LANES), 0)
    parts = []
    for place in range(per_row):
        part = jnp.zeros((2 * SUBLANES, LANES), jnp.float32)
        for index, line in enumerate(squares[place::per_row]):
            high = line.astype(jnp.bfloat16).astype(jnp.float32)
            part = jnp.where(row == index, high, part)
            part = jnp.where(row == SUBLANES + index, line - high, part)
        parts.append(part)
    return jnp.concatenate(parts, axis=1).astype(jnp.bfloat16)


def unpacked(ref, line):
    index, place = divmod(line, ref.shape[1] // LANES)
    part = ref[pl.ds(ref.shape[0] - 2 * SUBLANES, 2 * SUBLANES), place * LANES : (place + 1) * LANES]
    part = part.astype(jnp.float32)
    return part[index : index + 1] + part[SUBLANES + index : SUBLANES + index + 1]


def product_kernel(step, chip_count, first, staged, carrier, tokens, gain, weight, *refs):
    refs = list(refs)
    keep, send = refs.pop(0), refs.pop(0)
    squares = refs.pop(0) if carrier else None
    count = keep.shape[0] // TILE
    depth, width = tokens.shape[1], 2 * keep.shape[1]
    me = lax.axis_index("tensor")
    core = lax.rem(me, 2)
    chip = lax.rem(lax.div(me, 2) + step, chip_count)
    place = pl.ds(pl.multiple_of(chip * width, width), width)

    weight_copies, row_copies = [], []
    if staged:
        rows_buf, weight_buf, gain_buf, weight_sems, row_sems, gain_sem = refs
        cut = depth // CUTS
        gain_copy = pltpu.make_async_copy(gain, gain_buf, gain_sem)
        for index in range(CUTS):
            some = pl.ds(index * cut, cut)
            weight_copies.append(
                pltpu.make_async_copy(weight.at[some, place], weight_buf.at[some, :], weight_sems.at[index])
            )
        for tile in range(count):
            rows = tokens.at[pl.ds((first + tile) * TILE, TILE), :]
            row_copies.append(
                pltpu.make_async_copy(rows, rows_buf.at[pl.ds(tile * TILE, TILE), :], row_sems.at[tile])
            )
        for copy in [gain_copy] + row_copies[:1] + weight_copies + row_copies[1:]:
            copy.start()
        gain_copy.wait()
        gains = gain_buf[...].reshape(1, depth)
    else:
        gains = gain[...].reshape(1, depth)

    lines = []
    for tile in range(count):
        inside = pl.ds(tile * TILE, TILE)
        if staged:
            row_copies[tile].wait()
            rows = rows_buf[inside, :]
        else:
            rows = tokens[pl.ds((first + tile) * TILE, TILE), :]
        scaled = rows * gains
        if weight_copies:
            product = jnp.zeros((TILE, width), jnp.float32)
            for index, copy in enumerate(weight_copies):
                copy.wait()
                span = slice(index * cut, (index + 1) * cut)
                product += jnp.dot(scaled[:, span], weight_buf[span, :], preferred_element_type=jnp.float32)
            weight_copies = []
        else:
            columns = weight_buf[...] if staged else weight[:, place]
            product = jnp.dot(scaled, columns, preferred_element_type=jnp.float32)
        left = product[:, : width // 2].astype(jnp.bfloat16)
        right = product[:, width // 2 :].astype(jnp.bfloat16)
        keep[inside, :] = jnp.where(core == 0, left, right)
        send[inside, :] = jnp.where(core == 0, right, left)
        if carrier:
            total = square_sums(rows)
            for part in range(TILE // LANES):
                turned = jnp.transpose(total[part * LANES : (part + 1) * LANES])
                lines.append(jnp.sum(turned, axis=0, keepdims=True))
                squares[len(lines) - 1 : len(lines), :] = lines[-1]
    if carrier:
        send[pl.ds(keep.shape[0], 2 * SUBLANES), :] = packed(lines, send.shape[1])


def add_carrier_kernel(keep, received, squares, pair_squares, out, *rest):
    low = 0
    for part in (out, *rest):
        size = part.shape[0] - (2 * SUBLANES if part is out else 0)
        rows = pl.ds(low, size)
        total = keep[rows, :].astype(jnp.float32) + received[rows, :].astype(jnp.float32)
        part[pl.ds(0, size), :] = total.astype(part.dtype)
        low += size
    lines = []
    for line in range(squares.shape[0]):
        lines.append(squares[line : line + 1, :] + unpacked(received, line))
        pair_squares[line : line + 1, :] = lines[-1]
    out[pl.ds(out.shape[0] - 2 * SUBLANES, 2 * SUBLANES), :] = packed(lines, out.shape[1])


def table_kernel(live, span, frequencies, limit, far_cos, far_sin, near_cos, near_sin):
    limit[...] = jnp.full(limit.shape, live[lax.axis_index("serve")] * BLOCK, jnp.int32)
    blocks = far_cos.shape[0]
    start = span[lax.axis_index("serve")] * PAGE
    first = start + BLOCK * lax.broadcasted_iota(jnp.int32, (blocks, HD), 0)
    far = first.astype(jnp.float32) * frequencies[...]
    near = lax.broadcasted_iota(jnp.int32, (BLOCK, HD), 0).astype(jnp.float32) * frequencies[...]
    far_cos[...] = jnp.cos(far)
    far_sin[...] = jnp.sin(far)
    near_cos[...] = jnp.cos(near)
    near_sin[...] = jnp.sin(near)


def finish_kernel(first, at, count, chip_count, model_dim, *refs):
    keep, received, limit, far_cos, far_sin, near_cos, near_sin = refs[:7]
    pair_squares, carriers = refs[7], refs[8 : 7 + chip_count]
    arrived = refs[7 + chip_count : -4] if at else carriers
    out, staged, sems = refs[-3:]
    on_diagonal = lax.broadcasted_iota(jnp.int32, (LANES, LANES), 0) == lax.broadcasted_iota(
        jnp.int32, (LANES, LANES), 1
    )
    sign = jnp.where(lax.broadcasted_iota(jnp.int32, (1, HD), 1) < HD // 2, -1.0, 1.0)
    copies = []
    for index in range(count):
        start = (first + at + index) * TILE
        rows, inside = pl.ds(start, TILE), pl.ds(index * TILE, TILE)
        of_chunk = pl.ds((at + index) * TILE, TILE)
        values = keep[of_chunk, :].astype(jnp.float32) + received[of_chunk, :].astype(jnp.float32)
        for part in arrived:
            values += part[inside, :].astype(jnp.float32)
        columns = []
        for line in range((at + index) * TILE // LANES, (at + index + 1) * TILE // LANES):
            totals = pair_squares[line : line + 1, :]
            for ref in carriers:
                totals += unpacked(ref, line)
            columns.append(jnp.sum(jnp.where(on_diagonal, totals, 0.0), axis=1, keepdims=True))
        scales = 1.0 / jnp.sqrt(jnp.concatenate(columns, axis=0) / model_dim + norm_eps)
        alive = start + lax.broadcasted_iota(jnp.int32, (TILE, LANES), 0) < limit[0:1, :]
        cosines, sines = [], []
        for block in range(start // BLOCK, (start + TILE) // BLOCK):
            block_cos = far_cos[block : block + 1, :]
            block_sin = far_sin[block : block + 1, :]
            cosines.append(block_cos * near_cos[...] - block_sin * near_sin[...])
            sines.append((sign * block_sin) * near_cos[...] + (sign * block_cos) * near_sin[...])
        cosine = jnp.concatenate(cosines, axis=0)
        sine = jnp.concatenate(sines, axis=0)
        for low in range(0, out.shape[1], 2 * HD):
            key = values[:, low : low + HD] * scales
            turned = key * cosine + pltpu.roll(key, HD // 2, 1) * sine
            staged[inside, low : low + HD] = jnp.where(alive, turned, 0.0).astype(out.dtype)
            value = values[:, low + HD : low + 2 * HD] * scales
            staged[inside, low + HD : low + 2 * HD] = jnp.where(alive, value, 0.0).astype(out.dtype)
        copies.append(pltpu.make_async_copy(staged.at[inside, :], out.at[rows, :], sems.at[index]))
        copies[-1].start()
    for copy in copies:
        copy.wait()


def shards(tokens, norm_gain, kv_weight, live_blocks, span_offset):
    tensor_count = lax.axis_size("tensor")
    chip_count = tensor_count // 2
    me = lax.axis_index("tensor")
    slot_rows, depth = tokens.shape
    columns = kv_weight.shape[1] // tensor_count
    tiles = slot_rows // TILE
    model_dim = depth * tensor_count

    swap = [(i, i ^ 1) for i in range(tensor_count)]

    def shift(step):
        return [(i, (i + 2 * step) % tensor_count) for i in range(tensor_count)]

    def product(gain, step, first, count, staged=False, carrier=True):
        vmem = pl.BlockSpec(memory_space=pltpu.VMEM)
        rows = count * TILE
        out_shape = [jax.ShapeDtypeStruct((rows, columns), jnp.bfloat16)] * 2
        if carrier:
            out_shape[1] = jax.ShapeDtypeStruct((rows + 2 * SUBLANES, columns), jnp.bfloat16)
            out_shape.append(jax.ShapeDtypeStruct((rows // LANES, LANES), jnp.float32))
        scratch = [
            pltpu.VMEM((rows, depth), jnp.bfloat16),
            pltpu.VMEM((depth, 2 * columns), jnp.bfloat16),
            pltpu.VMEM((depth,), jnp.bfloat16),
            pltpu.SemaphoreType.DMA((CUTS,)),
            pltpu.SemaphoreType.DMA((count,)),
            pltpu.SemaphoreType.DMA,
        ]
        return pl.pallas_call(
            functools.partial(product_kernel, step, chip_count, first, staged, carrier),
            in_specs=[pl.BlockSpec(memory_space=pltpu.HBM) if staged else vmem] * 3,
            out_shape=out_shape,
            out_specs=[vmem] * len(out_shape),
            scratch_shapes=scratch if staged else [],
            compiler_params=FIRST if staged else PARAMS,
            cost_estimate=HEAVY if staged else COST,
        )(tokens, gain, kv_weight)

    def tables(span_offset):
        frequencies = rope_base ** (-(np.arange(HD // 2, dtype=np.float32) * 2.0) / HD)
        frequencies = np.concatenate([frequencies, frequencies])[None, :].astype(np.float32)
        shapes = [(slot_rows // BLOCK, HD)] * 2 + [(BLOCK, HD)] * 2
        made = pl.pallas_call(
            table_kernel,
            in_specs=[pl.BlockSpec(memory_space=pltpu.SMEM)] * 2 + [pl.BlockSpec(memory_space=pltpu.VMEM)],
            out_shape=[jax.ShapeDtypeStruct((8, LANES), jnp.int32)]
            + [jax.ShapeDtypeStruct(shape, jnp.float32) for shape in shapes],
            out_specs=[pl.BlockSpec(memory_space=pltpu.VMEM)] * 5,
            compiler_params=PARAMS,
            cost_estimate=COST,
        )(live_blocks, span_offset, jnp.asarray(frequencies))
        return list(made)

    def finish(first, at, count, keep, received, table, squares, carriers, arrived, result):
        vmem = pl.BlockSpec(memory_space=pltpu.VMEM)
        operands = [keep, received] + table + [squares] + carriers + (arrived if at else [])
        aliases = {len(operands): 0}
        if result is None:
            result, aliases = jnp.zeros((1,), jnp.bfloat16), {}
        return pl.pallas_call(
            functools.partial(finish_kernel, first, at, count, chip_count, model_dim),
            in_specs=[vmem] * len(operands) + [pl.BlockSpec(memory_space=pl.ANY)],
            out_shape=jax.ShapeDtypeStruct((slot_rows, columns), jnp.bfloat16),
            out_specs=pl.BlockSpec(memory_space=pltpu.HBM),
            scratch_shapes=[pltpu.VMEM((count * TILE, columns), jnp.bfloat16), pltpu.SemaphoreType.DMA((count,))],
            input_output_aliases=aliases,
            compiler_params=PARAMS,
            cost_estimate=LATER,
        )(*operands, result)

    others = range(1, chip_count)
    firsts = [sum(CHUNKS[:index]) for index in range(len(CHUNKS))]
    chunk_count = len(CHUNKS)

    chunks = list(zip(firsts, CHUNKS))

    def add_halves(made, counts):
        sizes = [count * TILE for count in counts]
        sizes[0] += 2 * SUBLANES
        added = [
            pl.pallas_call(
                add_carrier_kernel,
                out_shape=[jax.ShapeDtypeStruct(squares.shape, squares.dtype)]
                + [jax.ShapeDtypeStruct((size, columns), keep.dtype) for size in sizes],
                compiler_params=PARAMS,
                cost_estimate=COST,
            )(keep, lax.ppermute(send, "tensor", swap), squares)
            for keep, send, squares in made
        ]
        return [list(parts) for parts in zip(*[parts[1:] for parts in added])], added[0][0]

    def cross(sums):
        return [lax.ppermute(part, "tensor", shift(step)) for step, part in zip(others, sums)]

    hold = lax.optimization_barrier
    made = [product(norm_gain, step, *chunks[0], staged=True) for step in others]
    made, gain = hold((made, norm_gain))
    sums = add_halves(made, chunks[0][1:])
    sums, gain, span_offset, live_blocks = hold((sums, gain, span_offset, live_blocks))

    arrivals = [([cross(part) for part in sums[0]], sums[1])]
    for index in range(1, chunk_count):
        made = [product(gain, step, *chunks[index]) for step in others]
        count = chunks[index][1]
        sums = add_halves(made, (count - 1, 1) if count > 2 else (count,))
        if index == 2:
            sums, late = hold((sums, gain))
        arrivals.append(([cross(part) for part in sums[0]], sums[1]))
    own = [product(gain, 0, *chunk, carrier=False) for chunk in chunks[:-1]]
    own.append(product(late, 0, *chunks[-1], carrier=False))
    table = tables(span_offset)

    result = None
    for (first, count), (keep, send), (arrived, squares) in zip(chunks, own, arrivals):
        received = lax.ppermute(send, "tensor", swap)
        at = 0
        for part in arrived:
            size = part[0].shape[0] // TILE
            result = finish(first, at, size, keep, received, table, squares, arrived[0], part, result)
            at += size
    return result


def solution(mesh):
    in_specs = (
        P(("groups", "serve"), "tensor"),
        P("tensor"),
        P("tensor", None),
        P("groups"),
        P("groups"),
    )
    out_specs = P(("groups", "serve"), "tensor")
    return jax.shard_map(shards, mesh=mesh, in_specs=in_specs, out_specs=out_specs, check_vma=False)
```

```python
import functools

import jax
import jax.numpy as jnp
import numpy as np
from jax import lax
from jax.experimental import pallas as pl
from jax.experimental.pallas import tpu as pltpu
from jax.sharding import PartitionSpec as P

HD = 128
PAGE = 256
BLOCK = 64
LANES = 128
SUBLANES = 8

rope_base = 500000.0
norm_eps = 1e-05

TILE = 256
CUTS = 4
CHUNKS = (2, 1, 3)

PARAMS = pltpu.CompilerParams(vmem_limit_bytes=16 * 1024 * 1024)
FIRST = pltpu.CompilerParams(vmem_limit_bytes=53248 * 1024)
LATER = pl.CostEstimate(flops=20000000000, bytes_accessed=1, transcendentals=0)
HEAVY = pl.CostEstimate(flops=1000000000000, bytes_accessed=1, transcendentals=0)
COST = pl.CostEstimate(flops=1, bytes_accessed=1, transcendentals=0)


def square_sums(rows):
    total = jnp.zeros((rows.shape[0], LANES), jnp.float32)
    for part in range(rows.shape[1] // LANES):
        wide = rows[:, part * LANES : (part + 1) * LANES].astype(jnp.float32)
        total += wide * wide
    return total


def packed(squares, width):
    per_row = width // LANES
    row = lax.broadcasted_iota(jnp.int32, (2 * SUBLANES, LANES), 0)
    parts = []
    for place in range(per_row):
        part = jnp.zeros((2 * SUBLANES, LANES), jnp.float32)
        for index, line in enumerate(squares[place::per_row]):
            high = line.astype(jnp.bfloat16).astype(jnp.float32)
            part = jnp.where(row == index, high, part)
            part = jnp.where(row == SUBLANES + index, line - high, part)
        parts.append(part)
    return jnp.concatenate(parts, axis=1).astype(jnp.bfloat16)


def unpacked(ref, line):
    index, place = divmod(line, ref.shape[1] // LANES)
    part = ref[pl.ds(ref.shape[0] - 2 * SUBLANES, 2 * SUBLANES), place * LANES : (place + 1) * LANES]
    part = part.astype(jnp.float32)
    return part[index : index + 1] + part[SUBLANES + index : SUBLANES + index + 1]


def product_kernel(step, chip_count, first, staged, carrier, tokens, gain, weight, *refs):
    refs = list(refs)
    keep, send = refs.pop(0), refs.pop(0)
    squares = refs.pop(0) if carrier else None
    count = keep.shape[0] // TILE
    depth, width = tokens.shape[1], 2 * keep.shape[1]
    me = lax.axis_index("tensor")
    core = lax.rem(me, 2)
    chip = lax.rem(lax.div(me, 2) + step, chip_count)
    place = pl.ds(pl.multiple_of(chip * width, width), width)

    weight_copies, row_copies = [], []
    if staged:
        rows_buf, weight_buf, gain_buf, weight_sems, row_sems, gain_sem = refs
        cut = depth // CUTS
        gain_copy = pltpu.make_async_copy(gain, gain_buf, gain_sem)
        for index in range(CUTS):
            some = pl.ds(index * cut, cut)
            weight_copies.append(
                pltpu.make_async_copy(weight.at[some, place], weight_buf.at[some, :], weight_sems.at[index])
            )
        for tile in range(count):
            rows = tokens.at[pl.ds((first + tile) * TILE, TILE), :]
            row_copies.append(
                pltpu.make_async_copy(rows, rows_buf.at[pl.ds(tile * TILE, TILE), :], row_sems.at[tile])
            )
        for copy in [gain_copy] + row_copies[:1] + weight_copies + row_copies[1:]:
            copy.start()
        gain_copy.wait()
        gains = gain_buf[...].reshape(1, depth)
    else:
        gains = gain[...].reshape(1, depth)

    lines = []
    for tile in range(count):
        inside = pl.ds(tile * TILE, TILE)
        if staged:
            row_copies[tile].wait()
            rows = rows_buf[inside, :]
        else:
            rows = tokens[pl.ds((first + tile) * TILE, TILE), :]
        scaled = rows * gains
        if weight_copies:
            product = jnp.zeros((TILE, width), jnp.float32)
            for index, copy in enumerate(weight_copies):
                copy.wait()
                span = slice(index * cut, (index + 1) * cut)
                product += jnp.dot(scaled[:, span], weight_buf[span, :], preferred_element_type=jnp.float32)
            weight_copies = []
        else:
            columns = weight_buf[...] if staged else weight[:, place]
            product = jnp.dot(scaled, columns, preferred_element_type=jnp.float32)
        left = product[:, : width // 2].astype(jnp.bfloat16)
        right = product[:, width // 2 :].astype(jnp.bfloat16)
        keep[inside, :] = jnp.where(core == 0, left, right)
        send[inside, :] = jnp.where(core == 0, right, left)
        if carrier:
            total = square_sums(rows)
            for part in range(TILE // LANES):
                turned = jnp.transpose(total[part * LANES : (part + 1) * LANES])
                lines.append(jnp.sum(turned, axis=0, keepdims=True))
                squares[len(lines) - 1 : len(lines), :] = lines[-1]
    if carrier:
        send[pl.ds(keep.shape[0], 2 * SUBLANES), :] = packed(lines, send.shape[1])


def add_carrier_kernel(keep, received, squares, pair_squares, out, *rest):
    low = 0
    for part in (out, *rest):
        size = part.shape[0] - (2 * SUBLANES if part is out else 0)
        rows = pl.ds(low, size)
        total = keep[rows, :].astype(jnp.float32) + received[rows, :].astype(jnp.float32)
        part[pl.ds(0, size), :] = total.astype(part.dtype)
        low += size
    lines = []
    for line in range(squares.shape[0]):
        lines.append(squares[line : line + 1, :] + unpacked(received, line))
        pair_squares[line : line + 1, :] = lines[-1]
    out[pl.ds(out.shape[0] - 2 * SUBLANES, 2 * SUBLANES), :] = packed(lines, out.shape[1])


def table_kernel(live, span, frequencies, limit, far_cos, far_sin, near_cos, near_sin):
    limit[...] = jnp.full(limit.shape, live[lax.axis_index("serve")] * BLOCK, jnp.int32)
    blocks = far_cos.shape[0]
    start = span[lax.axis_index("serve")] * PAGE
    first = start + BLOCK * lax.broadcasted_iota(jnp.int32, (blocks, HD), 0)
    far = first.astype(jnp.float32) * frequencies[...]
    near = lax.broadcasted_iota(jnp.int32, (BLOCK, HD), 0).astype(jnp.float32) * frequencies[...]
    far_cos[...] = jnp.cos(far)
    far_sin[...] = jnp.sin(far)
    near_cos[...] = jnp.cos(near)
    near_sin[...] = jnp.sin(near)


def finish_kernel(first, at, count, chip_count, model_dim, *refs):
    keep, received, limit, far_cos, far_sin, near_cos, near_sin = refs[:7]
    pair_squares, carriers = refs[7], refs[8 : 7 + chip_count]
    arrived = refs[7 + chip_count : -4] if at else carriers
    out, staged, sems = refs[-3:]
    on_diagonal = lax.broadcasted_iota(jnp.int32, (LANES, LANES), 0) == lax.broadcasted_iota(
        jnp.int32, (LANES, LANES), 1
    )
    sign = jnp.where(lax.broadcasted_iota(jnp.int32, (1, HD), 1) < HD // 2, -1.0, 1.0)
    copies = []
    for index in range(count):
        start = (first + at + index) * TILE
        rows, inside = pl.ds(start, TILE), pl.ds(index * TILE, TILE)
        of_chunk = pl.ds((at + index) * TILE, TILE)
        values = keep[of_chunk, :].astype(jnp.float32) + received[of_chunk, :].astype(jnp.float32)
        for part in arrived:
            values += part[inside, :].astype(jnp.float32)
        columns = []
        for line in range((at + index) * TILE // LANES, (at + index + 1) * TILE // LANES):
            totals = pair_squares[line : line + 1, :]
            for ref in carriers:
                totals += unpacked(ref, line)
            columns.append(jnp.sum(jnp.where(on_diagonal, totals, 0.0), axis=1, keepdims=True))
        scales = 1.0 / jnp.sqrt(jnp.concatenate(columns, axis=0) / model_dim + norm_eps)
        alive = start + lax.broadcasted_iota(jnp.int32, (TILE, LANES), 0) < limit[0:1, :]
        cosines, sines = [], []
        for block in range(start // BLOCK, (start + TILE) // BLOCK):
            block_cos = far_cos[block : block + 1, :]
            block_sin = far_sin[block : block + 1, :]
            cosines.append(block_cos * near_cos[...] - block_sin * near_sin[...])
            sines.append((sign * block_sin) * near_cos[...] + (sign * block_cos) * near_sin[...])
        cosine = jnp.concatenate(cosines, axis=0)
        sine = jnp.concatenate(sines, axis=0)
        for low in range(0, out.shape[1], 2 * HD):
            key = values[:, low : low + HD] * scales
            turned = key * cosine + pltpu.roll(key, HD // 2, 1) * sine
            staged[inside, low : low + HD] = jnp.where(alive, turned, 0.0).astype(out.dtype)
            value = values[:, low + HD : low + 2 * HD] * scales
            staged[inside, low + HD : low + 2 * HD] = jnp.where(alive, value, 0.0).astype(out.dtype)
        copies.append(pltpu.make_async_copy(staged.at[inside, :], out.at[rows, :], sems.at[index]))
        copies[-1].start()
    for copy in copies:
        copy.wait()


def shards(tokens, norm_gain, kv_weight, live_blocks, span_offset):
    tensor_count = lax.axis_size("tensor")
    chip_count = tensor_count // 2
    me = lax.axis_index("tensor")
    slot_rows, depth = tokens.shape
    columns = kv_weight.shape[1] // tensor_count
    tiles = slot_rows // TILE
    model_dim = depth * tensor_count

    swap = [(i, i ^ 1) for i in range(tensor_count)]

    def shift(step):
        return [(i, (i + 2 * step) % tensor_count) for i in range(tensor_count)]

    def product(gain, step, first, count, staged=False, carrier=True):
        vmem = pl.BlockSpec(memory_space=pltpu.VMEM)
        rows = count * TILE
        out_shape = [jax.ShapeDtypeStruct((rows, columns), jnp.bfloat16)] * 2
        if carrier:
            out_shape[1] = jax.ShapeDtypeStruct((rows + 2 * SUBLANES, columns), jnp.bfloat16)
            out_shape.append(jax.ShapeDtypeStruct((rows // LANES, LANES), jnp.float32))
        scratch = [
            pltpu.VMEM((rows, depth), jnp.bfloat16),
            pltpu.VMEM((depth, 2 * columns), jnp.bfloat16),
            pltpu.VMEM((depth,), jnp.bfloat16),
            pltpu.SemaphoreType.DMA((CUTS,)),
            pltpu.SemaphoreType.DMA((count,)),
            pltpu.SemaphoreType.DMA,
        ]
        return pl.pallas_call(
            functools.partial(product_kernel, step, chip_count, first, staged, carrier),
            in_specs=[pl.BlockSpec(memory_space=pltpu.HBM) if staged else vmem] * 3,
            out_shape=out_shape,
            out_specs=[vmem] * len(out_shape),
            scratch_shapes=scratch if staged else [],
            compiler_params=FIRST if staged else PARAMS,
            cost_estimate=HEAVY if staged else COST,
        )(tokens, gain, kv_weight)

    def tables(live_blocks, span_offset):
        frequencies = rope_base ** (-(np.arange(HD // 2, dtype=np.float32) * 2.0) / HD)
        frequencies = np.concatenate([frequencies, frequencies])[None, :].astype(np.float32)
        shapes = [(slot_rows // BLOCK, HD)] * 2 + [(BLOCK, HD)] * 2
        made = pl.pallas_call(
            table_kernel,
            in_specs=[pl.BlockSpec(memory_space=pltpu.SMEM)] * 2 + [pl.BlockSpec(memory_space=pltpu.VMEM)],
            out_shape=[jax.ShapeDtypeStruct((8, LANES), jnp.int32)]
            + [jax.ShapeDtypeStruct(shape, jnp.float32) for shape in shapes],
            out_specs=[pl.BlockSpec(memory_space=pltpu.VMEM)] * 5,
            compiler_params=PARAMS,
            cost_estimate=COST,
        )(live_blocks, span_offset, jnp.asarray(frequencies))
        return list(made)

    def finish(first, at, count, keep, received, table, squares, carriers, arrived, result):
        vmem = pl.BlockSpec(memory_space=pltpu.VMEM)
        operands = [keep, received] + table + [squares] + carriers + (arrived if at else [])
        aliases = {len(operands): 0}
        if result is None:
            result, aliases = jnp.zeros((1,), jnp.bfloat16), {}
        return pl.pallas_call(
            functools.partial(finish_kernel, first, at, count, chip_count, model_dim),
            in_specs=[vmem] * len(operands) + [pl.BlockSpec(memory_space=pl.ANY)],
            out_shape=jax.ShapeDtypeStruct((slot_rows, columns), jnp.bfloat16),
            out_specs=pl.BlockSpec(memory_space=pltpu.HBM),
            scratch_shapes=[pltpu.VMEM((count * TILE, columns), jnp.bfloat16), pltpu.SemaphoreType.DMA((count,))],
            input_output_aliases=aliases,
            compiler_params=PARAMS,
            cost_estimate=LATER,
        )(*operands, result)

    others = range(1, chip_count)
    firsts = [sum(CHUNKS[:index]) for index in range(len(CHUNKS))]
    chunk_count = len(CHUNKS)

    chunks = list(zip(firsts, CHUNKS))

    def add_halves(made, counts):
        sizes = [count * TILE for count in counts]
        sizes[0] += 2 * SUBLANES
        added = [
            pl.pallas_call(
                add_carrier_kernel,
                out_shape=[jax.ShapeDtypeStruct(squares.shape, squares.dtype)]
                + [jax.ShapeDtypeStruct((size, columns), keep.dtype) for size in sizes],
                compiler_params=PARAMS,
                cost_estimate=COST,
            )(keep, lax.ppermute(send, "tensor", swap), squares)
            for keep, send, squares in made
        ]
        return [list(parts) for parts in zip(*[parts[1:] for parts in added])], added[0][0]

    def cross(sums):
        return [lax.ppermute(part, "tensor", shift(step)) for step, part in zip(others, sums)]

    hold = lax.optimization_barrier
    made = [product(norm_gain, step, *chunks[0], staged=True) for step in others]
    made, gain, span_offset, live_blocks = hold((made, norm_gain, span_offset, live_blocks))
    table = tables(live_blocks, span_offset)
    sums = add_halves(made, chunks[0][1:])
    sums, gain, table = hold((sums, gain, table))

    arrivals = [([cross(part) for part in sums[0]], sums[1])]
    for index in range(1, chunk_count):
        made = [product(gain, step, *chunks[index]) for step in others]
        count = chunks[index][1]
        sums = add_halves(made, (count - 1, 1) if count > 2 else (count,))
        if index == 2:
            sums, late = hold((sums, gain))
        arrivals.append(([cross(part) for part in sums[0]], sums[1]))
    own = [product(gain, 0, *chunk, carrier=False) for chunk in chunks[:-1]]
    own.append(product(late, 0, *chunks[-1], carrier=False))

    result = None
    for (first, count), (keep, send), (arrived, squares) in zip(chunks, own, arrivals):
        received = lax.ppermute(send, "tensor", swap)
        at = 0
        for part in arrived:
            size = part[0].shape[0] // TILE
            result = finish(first, at, size, keep, received, table, squares, arrived[0], part, result)
            at += size
    return result


def solution(mesh):
    in_specs = (
        P(("groups", "serve"), "tensor"),
        P("tensor"),
        P("tensor", None),
        P("groups"),
        P("groups"),
    )
    out_specs = P(("groups", "serve"), "tensor")
    return jax.shard_map(shards, mesh=mesh, in_specs=in_specs, out_specs=out_specs, check_vma=False)
```

```python
import functools

import jax
import jax.numpy as jnp
import numpy as np
from jax import lax
from jax.experimental import pallas as pl
from jax.experimental.pallas import tpu as pltpu
from jax.sharding import PartitionSpec as P

HD = 128
PAGE = 256
BLOCK = 64
LANES = 128
SUBLANES = 8

rope_base = 500000.0
norm_eps = 1e-05

TILE = 256
CUTS = 4
CHUNKS = (2, 1, 3)

PARAMS = pltpu.CompilerParams(vmem_limit_bytes=16 * 1024 * 1024)
FIRST = pltpu.CompilerParams(vmem_limit_bytes=53248 * 1024)
LATER = pl.CostEstimate(flops=20000000000, bytes_accessed=1, transcendentals=0)
HEAVY = pl.CostEstimate(flops=1000000000000, bytes_accessed=1, transcendentals=0)
COST = pl.CostEstimate(flops=1, bytes_accessed=1, transcendentals=0)


def square_lines(rows):
    lines = []
    for low in range(0, rows.shape[0], LANES):
        total = jnp.zeros((LANES, LANES), jnp.float32)
        for part in range(rows.shape[1] // LANES):
            wide = rows[low : low + LANES, part * LANES : (part + 1) * LANES].astype(jnp.float32)
            total += wide * wide
        lines.append(jnp.sum(jnp.transpose(total), axis=0, keepdims=True))
    return lines


def packed(squares, width):
    per_row = width // LANES
    row = lax.broadcasted_iota(jnp.int32, (2 * SUBLANES, LANES), 0)
    parts = []
    for place in range(per_row):
        part = jnp.zeros((2 * SUBLANES, LANES), jnp.float32)
        for index, line in enumerate(squares[place::per_row]):
            high = line.astype(jnp.bfloat16).astype(jnp.float32)
            part = jnp.where(row == index, high, part)
            part = jnp.where(row == SUBLANES + index, line - high, part)
        parts.append(part)
    return jnp.concatenate(parts, axis=1).astype(jnp.bfloat16)


def unpacked(ref, line):
    index, place = divmod(line, ref.shape[1] // LANES)
    part = ref[pl.ds(ref.shape[0] - 2 * SUBLANES, 2 * SUBLANES), place * LANES : (place + 1) * LANES]
    part = part.astype(jnp.float32)
    return part[index : index + 1] + part[SUBLANES + index : SUBLANES + index + 1]


def product_kernel(step, chip_count, first, staged, carrier, more, tokens, gain, weight, *refs):
    refs = list(refs)
    keep, send = refs.pop(0), refs.pop(0)
    squares = refs.pop(0) if carrier else None
    count = keep.shape[0] // TILE
    depth, width = tokens.shape[1], 2 * keep.shape[1]
    me = lax.axis_index("tensor")
    core = lax.rem(me, 2)
    chip = lax.rem(lax.div(me, 2) + step, chip_count)
    place = pl.ds(pl.multiple_of(chip * width, width), width)

    weight_copies, row_copies = [], []
    if staged:
        rows_buf, weight_buf, gain_buf, weight_sems, row_sems, gain_sem = refs
        cut = depth // CUTS
        gain_copy = pltpu.make_async_copy(gain, gain_buf, gain_sem)
        for index in range(CUTS):
            some = pl.ds(index * cut, cut)
            weight_copies.append(
                pltpu.make_async_copy(weight.at[some, place], weight_buf.at[some, :], weight_sems.at[index])
            )
        for tile in range(count):
            rows = tokens.at[pl.ds((first + tile) * TILE, TILE), :]
            row_copies.append(
                pltpu.make_async_copy(rows, rows_buf.at[pl.ds(tile * TILE, TILE), :], row_sems.at[tile])
            )
        for copy in [gain_copy] + row_copies[:1] + weight_copies + row_copies[1:]:
            copy.start()
        gain_copy.wait()
        gains = gain_buf[...].reshape(1, depth)
    else:
        gains = gain[...].reshape(1, depth)

    lines = []
    for tile in range(count):
        inside = pl.ds(tile * TILE, TILE)
        if staged:
            row_copies[tile].wait()
            rows = rows_buf[inside, :]
        else:
            rows = tokens[pl.ds((first + tile) * TILE, TILE), :]
        scaled = rows * gains
        if weight_copies:
            product = jnp.zeros((TILE, width), jnp.float32)
            for index, copy in enumerate(weight_copies):
                copy.wait()
                span = slice(index * cut, (index + 1) * cut)
                product += jnp.dot(scaled[:, span], weight_buf[span, :], preferred_element_type=jnp.float32)
            weight_copies = []
        else:
            columns = weight_buf[...] if staged else weight[:, place]
            product = jnp.dot(scaled, columns, preferred_element_type=jnp.float32)
        left = product[:, : width // 2].astype(jnp.bfloat16)
        right = product[:, width // 2 :].astype(jnp.bfloat16)
        keep[inside, :] = jnp.where(core == 0, left, right)
        send[inside, :] = jnp.where(core == 0, right, left)
        if carrier:
            lines += square_lines(rows)
    for tile in range(count, count + more):
        lines += square_lines(tokens[pl.ds((first + tile) * TILE, TILE), :])
    if carrier:
        for index, line in enumerate(lines):
            squares[index : index + 1, :] = line
        send[pl.ds(keep.shape[0], 2 * SUBLANES), :] = packed(lines, send.shape[1])


def add_kernel(lines, keep, received, *refs):
    refs = list(refs)
    squares, pair_squares = (refs.pop(0), refs.pop(0)) if lines else (None, None)
    low = 0
    for out in refs:
        size = out.shape[0] - (2 * SUBLANES if lines and out is refs[0] else 0)
        rows = pl.ds(low, size)
        total = keep[rows, :].astype(jnp.float32) + received[rows, :].astype(jnp.float32)
        out[pl.ds(0, size), :] = total.astype(out.dtype)
        low += size
    if lines:
        totals = []
        for line in range(lines):
            totals.append(squares[line : line + 1, :] + unpacked(received, line))
            pair_squares[line : line + 1, :] = totals[-1]
        refs[0][pl.ds(refs[0].shape[0] - 2 * SUBLANES, 2 * SUBLANES), :] = packed(totals, refs[0].shape[1])


def table_kernel(live, span, frequencies, limit, far_cos, far_sin, near_cos, near_sin):
    limit[...] = jnp.full(limit.shape, live[lax.axis_index("serve")] * BLOCK, jnp.int32)
    blocks = far_cos.shape[0]
    start = span[lax.axis_index("serve")] * PAGE
    first = start + BLOCK * lax.broadcasted_iota(jnp.int32, (blocks, HD), 0)
    far = first.astype(jnp.float32) * frequencies[...]
    near = lax.broadcasted_iota(jnp.int32, (BLOCK, HD), 0).astype(jnp.float32) * frequencies[...]
    far_cos[...] = jnp.cos(far)
    far_sin[...] = jnp.sin(far)
    near_cos[...] = jnp.cos(near)
    near_sin[...] = jnp.sin(near)


def finish_kernel(first, at, line_at, count, chip_count, model_dim, *refs):
    keep, received, limit, far_cos, far_sin, near_cos, near_sin = refs[:7]
    pair_squares, carriers = refs[7], refs[8 : 7 + chip_count]
    arrived = refs[7 + chip_count : -4] or carriers
    out, staged, sems = refs[-3:]
    on_diagonal = lax.broadcasted_iota(jnp.int32, (LANES, LANES), 0) == lax.broadcasted_iota(
        jnp.int32, (LANES, LANES), 1
    )
    sign = jnp.where(lax.broadcasted_iota(jnp.int32, (1, HD), 1) < HD // 2, -1.0, 1.0)
    copies = []
    for index in range(count):
        start = (first + at + index) * TILE
        rows, inside = pl.ds(start, TILE), pl.ds(index * TILE, TILE)
        of_chunk = pl.ds((at + index) * TILE, TILE)
        values = keep[of_chunk, :].astype(jnp.float32) + received[of_chunk, :].astype(jnp.float32)
        for part in arrived:
            values += part[inside, :].astype(jnp.float32)
        columns = []
        for line in range((line_at + index) * TILE // LANES, (line_at + index + 1) * TILE // LANES):
            totals = pair_squares[line : line + 1, :]
            for ref in carriers:
                totals += unpacked(ref, line)
            columns.append(jnp.sum(jnp.where(on_diagonal, totals, 0.0), axis=1, keepdims=True))
        scales = 1.0 / jnp.sqrt(jnp.concatenate(columns, axis=0) / model_dim + norm_eps)
        alive = start + lax.broadcasted_iota(jnp.int32, (TILE, LANES), 0) < limit[0:1, :]
        cosines, sines = [], []
        for block in range(start // BLOCK, (start + TILE) // BLOCK):
            block_cos = far_cos[block : block + 1, :]
            block_sin = far_sin[block : block + 1, :]
            cosines.append(block_cos * near_cos[...] - block_sin * near_sin[...])
            sines.append((sign * block_sin) * near_cos[...] + (sign * block_cos) * near_sin[...])
        cosine = jnp.concatenate(cosines, axis=0)
        sine = jnp.concatenate(sines, axis=0)
        for low in range(0, out.shape[1], 2 * HD):
            key = values[:, low : low + HD] * scales
            turned = key * cosine + pltpu.roll(key, HD // 2, 1) * sine
            staged[inside, low : low + HD] = jnp.where(alive, turned, 0.0).astype(out.dtype)
            value = values[:, low + HD : low + 2 * HD] * scales
            staged[inside, low + HD : low + 2 * HD] = jnp.where(alive, value, 0.0).astype(out.dtype)
        copies.append(pltpu.make_async_copy(staged.at[inside, :], out.at[rows, :], sems.at[index]))
        copies[-1].start()
    for copy in copies:
        copy.wait()


def shards(tokens, norm_gain, kv_weight, live_blocks, span_offset):
    tensor_count = lax.axis_size("tensor")
    chip_count = tensor_count // 2
    me = lax.axis_index("tensor")
    slot_rows, depth = tokens.shape
    columns = kv_weight.shape[1] // tensor_count
    tiles = slot_rows // TILE
    model_dim = depth * tensor_count

    swap = [(i, i ^ 1) for i in range(tensor_count)]

    def shift(step):
        return [(i, (i + 2 * step) % tensor_count) for i in range(tensor_count)]

    def product(gain, step, first, count, staged=False, carrier=True, more=0):
        vmem = pl.BlockSpec(memory_space=pltpu.VMEM)
        rows = count * TILE
        out_shape = [jax.ShapeDtypeStruct((rows, columns), jnp.bfloat16)] * 2
        if carrier:
            out_shape[1] = jax.ShapeDtypeStruct((rows + 2 * SUBLANES, columns), jnp.bfloat16)
            out_shape.append(jax.ShapeDtypeStruct((rows // LANES + more * TILE // LANES, LANES), jnp.float32))
        scratch = [
            pltpu.VMEM((rows, depth), jnp.bfloat16),
            pltpu.VMEM((depth, 2 * columns), jnp.bfloat16),
            pltpu.VMEM((depth,), jnp.bfloat16),
            pltpu.SemaphoreType.DMA((CUTS,)),
            pltpu.SemaphoreType.DMA((count,)),
            pltpu.SemaphoreType.DMA,
        ]
        return pl.pallas_call(
            functools.partial(product_kernel, step, chip_count, first, staged, carrier, more),
            in_specs=[pl.BlockSpec(memory_space=pltpu.HBM) if staged else vmem] * 3,
            out_shape=out_shape,
            out_specs=[vmem] * len(out_shape),
            scratch_shapes=scratch if staged else [],
            compiler_params=FIRST if staged else PARAMS,
            cost_estimate=HEAVY if staged else COST,
        )(tokens, gain, kv_weight)

    def tables(live_blocks, span_offset):
        frequencies = rope_base ** (-(np.arange(HD // 2, dtype=np.float32) * 2.0) / HD)
        frequencies = np.concatenate([frequencies, frequencies])[None, :].astype(np.float32)
        shapes = [(slot_rows // BLOCK, HD)] * 2 + [(BLOCK, HD)] * 2
        made = pl.pallas_call(
            table_kernel,
            in_specs=[pl.BlockSpec(memory_space=pltpu.SMEM)] * 2 + [pl.BlockSpec(memory_space=pltpu.VMEM)],
            out_shape=[jax.ShapeDtypeStruct((8, LANES), jnp.int32)]
            + [jax.ShapeDtypeStruct(shape, jnp.float32) for shape in shapes],
            out_specs=[pl.BlockSpec(memory_space=pltpu.VMEM)] * 5,
            compiler_params=PARAMS,
            cost_estimate=COST,
        )(live_blocks, span_offset, jnp.asarray(frequencies))
        return list(made)

    def finish(first, at, line_at, count, keep, received, table, squares, carriers, arrived, result):
        vmem = pl.BlockSpec(memory_space=pltpu.VMEM)
        operands = [keep, received] + table + [squares] + carriers + (arrived if arrived is not carriers else [])
        aliases = {len(operands): 0}
        if result is None:
            result, aliases = jnp.zeros((1,), jnp.bfloat16), {}
        return pl.pallas_call(
            functools.partial(finish_kernel, first, at, line_at, count, chip_count, model_dim),
            in_specs=[vmem] * len(operands) + [pl.BlockSpec(memory_space=pl.ANY)],
            out_shape=jax.ShapeDtypeStruct((slot_rows, columns), jnp.bfloat16),
            out_specs=pl.BlockSpec(memory_space=pltpu.HBM),
            scratch_shapes=[pltpu.VMEM((count * TILE, columns), jnp.bfloat16), pltpu.SemaphoreType.DMA((count,))],
            input_output_aliases=aliases,
            compiler_params=PARAMS,
            cost_estimate=LATER,
        )(*operands, result)

    others = range(1, chip_count)
    firsts = [sum(CHUNKS[:index]) for index in range(len(CHUNKS))]
    chunk_count = len(CHUNKS)

    chunks = list(zip(firsts, CHUNKS))

    def add_halves(made, counts):
        sizes = [count * TILE for count in counts]
        added = []
        for keep, send, *squares in made:
            lines = squares[0].shape[0] if squares else 0
            out_shape = [jax.ShapeDtypeStruct((size, columns), keep.dtype) for size in sizes]
            if lines:
                out_shape[0] = jax.ShapeDtypeStruct((sizes[0] + 2 * SUBLANES, columns), keep.dtype)
                out_shape.insert(0, jax.ShapeDtypeStruct(squares[0].shape, squares[0].dtype))
            added.append(
                pl.pallas_call(
                    functools.partial(add_kernel, lines),
                    out_shape=out_shape,
                    compiler_params=PARAMS,
                    cost_estimate=COST,
                )(keep, lax.ppermute(send, "tensor", swap), *squares)
            )
        parts = [list(same) for same in zip(*added)]
        return (parts[1:], parts[0][0]) if lines else (parts, None)

    def cross(sums):
        return [lax.ppermute(part, "tensor", shift(step)) for step, part in zip(others, sums)]

    hold = lax.optimization_barrier
    made = [product(norm_gain, step, *chunks[0], staged=True) for step in others]
    made, gain, span_offset, live_blocks = hold((made, norm_gain, span_offset, live_blocks))
    table = tables(live_blocks, span_offset)
    sums = add_halves(made, chunks[0][1:])
    sums, gain, table = hold((sums, gain, table))

    arrivals = [([cross(part) for part in sums[0]], sums[1])]
    for index in range(1, chunk_count):
        more = sum(CHUNKS[2:]) if index == 1 else 0
        made = [product(gain, step, *chunks[index], carrier=index == 1, more=more) for step in others]
        count = chunks[index][1]
        sums = add_halves(made, (count - 1, 1) if count > 2 else (count,))
        if index == 2:
            sums, late = hold((sums, gain))
        arrivals.append(([cross(part) for part in sums[0]], sums[1]))
    own = [product(gain, 0, *chunk, carrier=False) for chunk in chunks[:-1]]
    own.append(product(late, 0, *chunks[-1], carrier=False))

    result = None
    for (first, count), (keep, send), (arrived, squares) in zip(chunks, own, arrivals):
        received = lax.ppermute(send, "tensor", swap)
        if squares is not None:
            carriers, pair_squares, line_at = arrived[0], squares, 0
        at = 0
        for part in arrived:
            size = part[0].shape[0] // TILE
            result = finish(first, at, line_at, size, keep, received, table, pair_squares, carriers, part, result)
            at += size
            line_at += size
    return result


def solution(mesh):
    in_specs = (
        P(("groups", "serve"), "tensor"),
        P("tensor"),
        P("tensor", None),
        P("groups"),
        P("groups"),
    )
    out_specs = P(("groups", "serve"), "tensor")
    return jax.shard_map(shards, mesh=mesh, in_specs=in_specs, out_specs=out_specs, check_vma=False)
```

```python
import functools

import jax
import jax.numpy as jnp
import numpy as np
from jax import lax
from jax.experimental import pallas as pl
from jax.experimental.pallas import tpu as pltpu
from jax.sharding import PartitionSpec as P

HD = 128
PAGE = 256
BLOCK = 64
LANES = 128
SUBLANES = 8

rope_base = 500000.0
norm_eps = 1e-05

TILE = 256
CUTS = 4
CHUNKS = (2, 1, 3)

PARAMS = pltpu.CompilerParams(vmem_limit_bytes=16 * 1024 * 1024)
FIRST = pltpu.CompilerParams(vmem_limit_bytes=51200 * 1024)
LATER = pl.CostEstimate(flops=20000000000, bytes_accessed=1, transcendentals=0)
HEAVY = pl.CostEstimate(flops=1000000000000, bytes_accessed=1, transcendentals=0)
BRING = pltpu.CompilerParams(vmem_limit_bytes=47104 * 1024)
COST = pl.CostEstimate(flops=1, bytes_accessed=1, transcendentals=0)


def square_lines(rows):
    lines = []
    for low in range(0, rows.shape[0], LANES):
        total = jnp.zeros((LANES, LANES), jnp.float32)
        for part in range(rows.shape[1] // LANES):
            wide = rows[low : low + LANES, part * LANES : (part + 1) * LANES].astype(jnp.float32)
            total += wide * wide
        lines.append(jnp.sum(jnp.transpose(total), axis=0, keepdims=True))
    return lines


def packed(squares, width):
    per_row = width // LANES
    row = lax.broadcasted_iota(jnp.int32, (2 * SUBLANES, LANES), 0)
    parts = []
    for place in range(per_row):
        part = jnp.zeros((2 * SUBLANES, LANES), jnp.float32)
        for index, line in enumerate(squares[place::per_row]):
            high = line.astype(jnp.bfloat16).astype(jnp.float32)
            part = jnp.where(row == index, high, part)
            part = jnp.where(row == SUBLANES + index, line - high, part)
        parts.append(part)
    return jnp.concatenate(parts, axis=1).astype(jnp.bfloat16)


def unpacked(ref, line):
    index, place = divmod(line, ref.shape[1] // LANES)
    part = ref[pl.ds(ref.shape[0] - 2 * SUBLANES, 2 * SUBLANES), place * LANES : (place + 1) * LANES]
    part = part.astype(jnp.float32)
    return part[index : index + 1] + part[SUBLANES + index : SUBLANES + index + 1]


def product_kernel(step, chip_count, first, staged, carrier, more, tokens, gain, weight, *refs):
    refs = list(refs)
    keep, send = refs.pop(0), refs.pop(0)
    squares = refs.pop(0) if carrier else None
    count = keep.shape[0] // TILE
    depth, width = tokens.shape[1], 2 * keep.shape[1]
    me = lax.axis_index("tensor")
    core = lax.rem(me, 2)
    chip = lax.rem(lax.div(me, 2) + step, chip_count)
    place = pl.ds(pl.multiple_of(chip * width, width), width)

    weight_copies, row_copies = [], []
    if staged:
        weight_buf, rows_buf, gain_buf, weight_sems, row_sems, gain_sem = refs
        cut = depth // CUTS
        gain_copy = pltpu.make_async_copy(gain, gain_buf, gain_sem)
        for index in range(CUTS):
            some = pl.ds(index * cut, cut)
            weight_copies.append(
                pltpu.make_async_copy(weight.at[some, place], weight_buf.at[some, :], weight_sems.at[index])
            )
        for tile in range(count):
            rows = tokens.at[pl.ds((first + tile) * TILE, TILE), :]
            row_copies.append(
                pltpu.make_async_copy(rows, rows_buf.at[pl.ds(tile * TILE, TILE), :], row_sems.at[tile])
            )
        for copy in [gain_copy] + row_copies[:1] + weight_copies + row_copies[1:]:
            copy.start()
        gain_copy.wait()
        gains = gain_buf[...].reshape(1, depth)
    else:
        gains = gain[...].reshape(1, depth)

    lines = []
    for tile in range(count):
        inside = pl.ds(tile * TILE, TILE)
        if staged:
            row_copies[tile].wait()
            rows = rows_buf[inside, :]
        else:
            rows = tokens[pl.ds((first + tile) * TILE, TILE), :]
        scaled = rows * gains
        if weight_copies:
            product = jnp.zeros((TILE, width), jnp.float32)
            for index, copy in enumerate(weight_copies):
                copy.wait()
                span = slice(index * cut, (index + 1) * cut)
                product += jnp.dot(scaled[:, span], weight_buf[span, :], preferred_element_type=jnp.float32)
            weight_copies = []
        else:
            columns = weight_buf[...] if staged else weight[...]
            product = jnp.dot(scaled, columns, preferred_element_type=jnp.float32)
        left = product[:, : width // 2].astype(jnp.bfloat16)
        right = product[:, width // 2 :].astype(jnp.bfloat16)
        keep[inside, :] = jnp.where(core == 0, left, right)
        send[inside, :] = jnp.where(core == 0, right, left)
        if carrier:
            lines += square_lines(rows)
    for tile in range(count, count + more):
        lines += square_lines(tokens[pl.ds((first + tile) * TILE, TILE), :])
    if carrier:
        for index, line in enumerate(lines):
            squares[index : index + 1, :] = line
        send[pl.ds(keep.shape[0], 2 * SUBLANES), :] = packed(lines, send.shape[1])


def bring_kernel(tokens, gain, weight, rows_out, gain_out, weight_out, sems):
    width = weight_out.shape[1]
    chip = lax.div(lax.axis_index("tensor"), 2)
    place = pl.ds(pl.multiple_of(chip * width, width), width)
    moves = [
        pltpu.make_async_copy(tokens, rows_out, sems.at[0]),
        pltpu.make_async_copy(gain, gain_out, sems.at[1]),
        pltpu.make_async_copy(weight.at[:, place], weight_out, sems.at[2]),
    ]
    for move in moves:
        move.start()
    for move in moves:
        move.wait()


def add_kernel(lines, keep, received, *refs):
    refs = list(refs)
    squares, pair_squares = (refs.pop(0), refs.pop(0)) if lines else (None, None)
    low = 0
    for out in refs:
        size = out.shape[0] - (2 * SUBLANES if lines and out is refs[0] else 0)
        rows = pl.ds(low, size)
        total = keep[rows, :].astype(jnp.float32) + received[rows, :].astype(jnp.float32)
        out[pl.ds(0, size), :] = total.astype(out.dtype)
        low += size
    if lines:
        totals = []
        for line in range(lines):
            totals.append(squares[line : line + 1, :] + unpacked(received, line))
            pair_squares[line : line + 1, :] = totals[-1]
        refs[0][pl.ds(refs[0].shape[0] - 2 * SUBLANES, 2 * SUBLANES), :] = packed(totals, refs[0].shape[1])


def table_kernel(live, span, frequencies, limit, far_cos, far_sin, near_cos, near_sin):
    limit[...] = jnp.full(limit.shape, live[lax.axis_index("serve")] * BLOCK, jnp.int32)
    blocks = far_cos.shape[0]
    start = span[lax.axis_index("serve")] * PAGE
    first = start + BLOCK * lax.broadcasted_iota(jnp.int32, (blocks, HD), 0)
    far = first.astype(jnp.float32) * frequencies[...]
    near = lax.broadcasted_iota(jnp.int32, (BLOCK, HD), 0).astype(jnp.float32) * frequencies[...]
    far_cos[...] = jnp.cos(far)
    far_sin[...] = jnp.sin(far)
    near_cos[...] = jnp.cos(near)
    near_sin[...] = jnp.sin(near)


def finish_kernel(first, at, line_at, count, chip_count, model_dim, *refs):
    keep, received, limit, far_cos, far_sin, near_cos, near_sin = refs[:7]
    pair_squares, carriers = refs[7], refs[8 : 7 + chip_count]
    arrived = refs[7 + chip_count : -4] or carriers
    out, staged, sems = refs[-3:]
    on_diagonal = lax.broadcasted_iota(jnp.int32, (LANES, LANES), 0) == lax.broadcasted_iota(
        jnp.int32, (LANES, LANES), 1
    )
    sign = jnp.where(lax.broadcasted_iota(jnp.int32, (1, HD), 1) < HD // 2, -1.0, 1.0)
    copies = []
    for index in range(count):
        start = (first + at + index) * TILE
        rows, inside = pl.ds(start, TILE), pl.ds(index * TILE, TILE)
        of_chunk = pl.ds((at + index) * TILE, TILE)
        values = keep[of_chunk, :].astype(jnp.float32) + received[of_chunk, :].astype(jnp.float32)
        for part in arrived:
            values += part[inside, :].astype(jnp.float32)
        columns = []
        for line in range((line_at + index) * TILE // LANES, (line_at + index + 1) * TILE // LANES):
            totals = pair_squares[line : line + 1, :]
            for ref in carriers:
                totals += unpacked(ref, line)
            columns.append(jnp.sum(jnp.where(on_diagonal, totals, 0.0), axis=1, keepdims=True))
        scales = 1.0 / jnp.sqrt(jnp.concatenate(columns, axis=0) / model_dim + norm_eps)
        alive = start + lax.broadcasted_iota(jnp.int32, (TILE, LANES), 0) < limit[0:1, :]
        cosines, sines = [], []
        for block in range(start // BLOCK, (start + TILE) // BLOCK):
            block_cos = far_cos[block : block + 1, :]
            block_sin = far_sin[block : block + 1, :]
            cosines.append(block_cos * near_cos[...] - block_sin * near_sin[...])
            sines.append((sign * block_sin) * near_cos[...] + (sign * block_cos) * near_sin[...])
        cosine = jnp.concatenate(cosines, axis=0)
        sine = jnp.concatenate(sines, axis=0)
        for low in range(0, out.shape[1], 2 * HD):
            key = values[:, low : low + HD] * scales
            turned = key * cosine + pltpu.roll(key, HD // 2, 1) * sine
            staged[inside, low : low + HD] = jnp.where(alive, turned, 0.0).astype(out.dtype)
            value = values[:, low + HD : low + 2 * HD] * scales
            staged[inside, low + HD : low + 2 * HD] = jnp.where(alive, value, 0.0).astype(out.dtype)
        copies.append(pltpu.make_async_copy(staged.at[inside, :], out.at[rows, :], sems.at[index]))
        copies[-1].start()
    for copy in copies:
        copy.wait()


def shards(tokens, norm_gain, kv_weight, live_blocks, span_offset):
    tensor_count = lax.axis_size("tensor")
    chip_count = tensor_count // 2
    me = lax.axis_index("tensor")
    slot_rows, depth = tokens.shape
    columns = kv_weight.shape[1] // tensor_count
    tiles = slot_rows // TILE
    model_dim = depth * tensor_count

    swap = [(i, i ^ 1) for i in range(tensor_count)]

    def shift(step):
        return [(i, (i + 2 * step) % tensor_count) for i in range(tensor_count)]

    def product(tokens, gain, kv_weight, step, first, count, staged=False, carrier=True, more=0):
        vmem = pl.BlockSpec(memory_space=pltpu.VMEM)
        rows = count * TILE
        out_shape = [jax.ShapeDtypeStruct((rows, columns), jnp.bfloat16)] * 2
        if carrier:
            out_shape[1] = jax.ShapeDtypeStruct((rows + 2 * SUBLANES, columns), jnp.bfloat16)
            out_shape.append(jax.ShapeDtypeStruct((rows // LANES + more * TILE // LANES, LANES), jnp.float32))
        if staged:
            out_shape.append(jax.ShapeDtypeStruct((depth, 2 * columns), jnp.bfloat16))
        scratch = [
            pltpu.VMEM((rows, depth), jnp.bfloat16),
            pltpu.VMEM((depth,), jnp.bfloat16),
            pltpu.SemaphoreType.DMA((CUTS,)),
            pltpu.SemaphoreType.DMA((count,)),
            pltpu.SemaphoreType.DMA,
        ]
        return pl.pallas_call(
            functools.partial(product_kernel, step, chip_count, first, staged, carrier, more),
            in_specs=[pl.BlockSpec(memory_space=pltpu.HBM) if staged else vmem] * 3,
            out_shape=out_shape,
            out_specs=[vmem] * len(out_shape),
            scratch_shapes=scratch if staged else [],
            compiler_params=FIRST if staged else PARAMS,
            cost_estimate=HEAVY if staged else COST,
        )(tokens, gain, kv_weight)

    def tables(live_blocks, span_offset):
        frequencies = rope_base ** (-(np.arange(HD // 2, dtype=np.float32) * 2.0) / HD)
        frequencies = np.concatenate([frequencies, frequencies])[None, :].astype(np.float32)
        shapes = [(slot_rows // BLOCK, HD)] * 2 + [(BLOCK, HD)] * 2
        made = pl.pallas_call(
            table_kernel,
            in_specs=[pl.BlockSpec(memory_space=pltpu.SMEM)] * 2 + [pl.BlockSpec(memory_space=pltpu.VMEM)],
            out_shape=[jax.ShapeDtypeStruct((8, LANES), jnp.int32)]
            + [jax.ShapeDtypeStruct(shape, jnp.float32) for shape in shapes],
            out_specs=[pl.BlockSpec(memory_space=pltpu.VMEM)] * 5,
            compiler_params=PARAMS,
            cost_estimate=COST,
        )(live_blocks, span_offset, jnp.asarray(frequencies))
        return list(made)

    def finish(first, at, line_at, count, keep, received, table, squares, carriers, arrived, result):
        vmem = pl.BlockSpec(memory_space=pltpu.VMEM)
        operands = [keep, received] + table + [squares] + carriers + (arrived if arrived is not carriers else [])
        aliases = {len(operands): 0}
        if result is None:
            result, aliases = jnp.zeros((1,), jnp.bfloat16), {}
        return pl.pallas_call(
            functools.partial(finish_kernel, first, at, line_at, count, chip_count, model_dim),
            in_specs=[vmem] * len(operands) + [pl.BlockSpec(memory_space=pl.ANY)],
            out_shape=jax.ShapeDtypeStruct((slot_rows, columns), jnp.bfloat16),
            out_specs=pl.BlockSpec(memory_space=pltpu.HBM),
            scratch_shapes=[pltpu.VMEM((count * TILE, columns), jnp.bfloat16), pltpu.SemaphoreType.DMA((count,))],
            input_output_aliases=aliases,
            compiler_params=PARAMS,
            cost_estimate=LATER,
        )(*operands, result)

    others = range(1, chip_count)
    firsts = [sum(CHUNKS[:index]) for index in range(len(CHUNKS))]
    chunk_count = len(CHUNKS)

    chunks = list(zip(firsts, CHUNKS))

    def add_halves(made, counts):
        sizes = [count * TILE for count in counts]
        added = []
        for keep, send, *squares in made:
            lines = squares[0].shape[0] if squares else 0
            out_shape = [jax.ShapeDtypeStruct((size, columns), keep.dtype) for size in sizes]
            if lines:
                out_shape[0] = jax.ShapeDtypeStruct((sizes[0] + 2 * SUBLANES, columns), keep.dtype)
                out_shape.insert(0, jax.ShapeDtypeStruct(squares[0].shape, squares[0].dtype))
            added.append(
                pl.pallas_call(
                    functools.partial(add_kernel, lines),
                    out_shape=out_shape,
                    compiler_params=PARAMS,
                    cost_estimate=COST,
                )(keep, lax.ppermute(send, "tensor", swap), *squares)
            )
        parts = [list(same) for same in zip(*added)]
        return (parts[1:], parts[0][0]) if lines else (parts, None)

    def cross(sums):
        return [lax.ppermute(part, "tensor", shift(step)) for step, part in zip(others, sums)]

    hold = lax.optimization_barrier
    made = [product(tokens, norm_gain, kv_weight, step, *chunks[0], staged=True) for step in others]
    weights = {step: parts[-1] for step, parts in zip(others, made)}
    made = [parts[:-1] for parts in made]
    made, gain, span_offset, live_blocks = hold((made, norm_gain, span_offset, live_blocks))
    table = tables(live_blocks, span_offset)
    sums = add_halves(made, chunks[0][1:])
    sums, gain, table = hold((sums, gain, table))
    tokens, gain, own_weight = pl.pallas_call(
        bring_kernel,
        in_specs=[pl.BlockSpec(memory_space=pltpu.HBM)] * 3,
        out_shape=[
            jax.ShapeDtypeStruct(shape, jnp.bfloat16) for shape in (tokens.shape, gain.shape, (depth, 2 * columns))
        ],
        out_specs=[pl.BlockSpec(memory_space=pltpu.VMEM)] * 3,
        scratch_shapes=[pltpu.SemaphoreType.DMA((3,))],
        compiler_params=BRING,
        cost_estimate=COST,
    )(tokens, gain, kv_weight)

    arrivals = [([cross(part) for part in sums[0]], sums[1])]
    for index in range(1, chunk_count):
        more = sum(CHUNKS[2:]) if index == 1 else 0
        made = [product(tokens, gain, weights[step], step, *chunks[index], carrier=index == 1, more=more) for step in others]
        count = chunks[index][1]
        sums = add_halves(made, (count - 1, 1) if count > 2 else (count,))
        if index == 2:
            sums, late = hold((sums, gain))
        arrivals.append(([cross(part) for part in sums[0]], sums[1]))
    own = [product(tokens, gain, own_weight, 0, *chunk, carrier=False) for chunk in chunks[:-1]]
    own.append(product(tokens, late, own_weight, 0, *chunks[-1], carrier=False))

    result = None
    for (first, count), (keep, send), (arrived, squares) in zip(chunks, own, arrivals):
        received = lax.ppermute(send, "tensor", swap)
        if squares is not None:
            carriers, pair_squares, line_at = arrived[0], squares, 0
        at = 0
        for part in arrived:
            size = part[0].shape[0] // TILE
            result = finish(first, at, line_at, size, keep, received, table, pair_squares, carriers, part, result)
            at += size
            line_at += size
    return result


def solution(mesh):
    in_specs = (
        P(("groups", "serve"), "tensor"),
        P("tensor"),
        P("tensor", None),
        P("groups"),
        P("groups"),
    )
    out_specs = P(("groups", "serve"), "tensor")
    return jax.shard_map(shards, mesh=mesh, in_specs=in_specs, out_specs=out_specs, check_vma=False)
```

```python
import functools

import jax
import jax.numpy as jnp
import numpy as np
from jax import lax
from jax.experimental import pallas as pl
from jax.experimental.pallas import tpu as pltpu
from jax.sharding import PartitionSpec as P

HD = 128
PAGE = 256
BLOCK = 64
LANES = 128
SUBLANES = 8

rope_base = 500000.0
norm_eps = 1e-05

TILE = 256
CUTS = 4
CHUNKS = (2, 1, 3)

PARAMS = pltpu.CompilerParams(vmem_limit_bytes=16 * 1024 * 1024)
FIRST = pltpu.CompilerParams(vmem_limit_bytes=51200 * 1024)
LATER = pl.CostEstimate(flops=20000000000, bytes_accessed=1, transcendentals=0)
HEAVY = pl.CostEstimate(flops=1000000000000, bytes_accessed=1, transcendentals=0)
BRING = pltpu.CompilerParams(vmem_limit_bytes=47104 * 1024)
COST = pl.CostEstimate(flops=1, bytes_accessed=1, transcendentals=0)


def square_lines(rows):
    lines = []
    for low in range(0, rows.shape[0], LANES):
        total = jnp.zeros((LANES, LANES), jnp.float32)
        for part in range(rows.shape[1] // LANES):
            wide = rows[low : low + LANES, part * LANES : (part + 1) * LANES].astype(jnp.float32)
            total += wide * wide
        lines.append(jnp.sum(jnp.transpose(total), axis=0, keepdims=True))
    return lines


def packed(squares, width):
    per_row = width // LANES
    row = lax.broadcasted_iota(jnp.int32, (2 * SUBLANES, LANES), 0)
    parts = []
    for place in range(per_row):
        part = jnp.zeros((2 * SUBLANES, LANES), jnp.float32)
        for index, line in enumerate(squares[place::per_row]):
            high = line.astype(jnp.bfloat16).astype(jnp.float32)
            part = jnp.where(row == index, high, part)
            part = jnp.where(row == SUBLANES + index, line - high, part)
        parts.append(part)
    return jnp.concatenate(parts, axis=1).astype(jnp.bfloat16)


def unpacked(ref, line):
    index, place = divmod(line, ref.shape[1] // LANES)
    part = ref[pl.ds(ref.shape[0] - 2 * SUBLANES, 2 * SUBLANES), place * LANES : (place + 1) * LANES]
    part = part.astype(jnp.float32)
    return part[index : index + 1] + part[SUBLANES + index : SUBLANES + index + 1]


def product_kernel(step, chip_count, first, staged, carrier, more, tokens, gain, weight, *refs):
    refs = list(refs)
    keep, send = refs.pop(0), refs.pop(0)
    squares = refs.pop(0) if carrier else None
    count = keep.shape[0] // TILE
    depth, width = tokens.shape[1], 2 * keep.shape[1]
    me = lax.axis_index("tensor")
    core = lax.rem(me, 2)
    chip = lax.rem(lax.div(me, 2) + step, chip_count)
    place = pl.ds(pl.multiple_of(chip * width, width), width)

    weight_copies, row_copies = [], []
    if staged:
        weight_buf, rows_buf, gain_buf, weight_sems, row_sems, gain_sem = refs
        cut = depth // CUTS
        gain_copy = pltpu.make_async_copy(gain, gain_buf, gain_sem)
        for index in range(CUTS):
            some = pl.ds(index * cut, cut)
            weight_copies.append(
                pltpu.make_async_copy(weight.at[some, place], weight_buf.at[some, :], weight_sems.at[index])
            )
        for tile in range(count):
            rows = tokens.at[pl.ds((first + tile) * TILE, TILE), :]
            row_copies.append(
                pltpu.make_async_copy(rows, rows_buf.at[pl.ds(tile * TILE, TILE), :], row_sems.at[tile])
            )
        for copy in [gain_copy] + row_copies + weight_copies:
            copy.start()
        gain_copy.wait()
        gains = gain_buf[...].reshape(1, depth)
    else:
        gains = gain[...].reshape(1, depth)

    products, lines = [], []
    if staged:
        scaled = []
        for tile in range(count):
            row_copies[tile].wait()
            scaled.append(rows_buf[pl.ds(tile * TILE, TILE), :] * gains)
        for index, copy in enumerate(weight_copies):
            copy.wait()
            span = slice(index * cut, (index + 1) * cut)
            for tile in range(count):
                part = jnp.dot(scaled[tile][:, span], weight_buf[span, :], preferred_element_type=jnp.float32)
                products[tile : tile + 1] = [products[tile] + part if index else part]
    for tile in range(count):
        inside = pl.ds(tile * TILE, TILE)
        if staged:
            rows, product = rows_buf[inside, :], products[tile]
        else:
            rows = tokens[pl.ds((first + tile) * TILE, TILE), :]
            product = jnp.dot(rows * gains, weight[...], preferred_element_type=jnp.float32)
        left = product[:, : width // 2].astype(jnp.bfloat16)
        right = product[:, width // 2 :].astype(jnp.bfloat16)
        keep[inside, :] = jnp.where(core == 0, left, right)
        send[inside, :] = jnp.where(core == 0, right, left)
        if carrier:
            lines += square_lines(rows)
    for tile in range(count, count + more):
        lines += square_lines(tokens[pl.ds((first + tile) * TILE, TILE), :])
    if carrier:
        for index, line in enumerate(lines):
            squares[index : index + 1, :] = line
        send[pl.ds(keep.shape[0], 2 * SUBLANES), :] = packed(lines, send.shape[1])


def bring_kernel(tokens, gain, weight, rows_out, gain_out, weight_out, sems):
    width = weight_out.shape[1]
    chip = lax.div(lax.axis_index("tensor"), 2)
    place = pl.ds(pl.multiple_of(chip * width, width), width)
    moves = [
        pltpu.make_async_copy(tokens, rows_out, sems.at[0]),
        pltpu.make_async_copy(gain, gain_out, sems.at[1]),
        pltpu.make_async_copy(weight.at[:, place], weight_out, sems.at[2]),
    ]
    for move in moves:
        move.start()
    for move in moves:
        move.wait()


def add_kernel(lines, keep, received, *refs):
    refs = list(refs)
    squares, pair_squares = (refs.pop(0), refs.pop(0)) if lines else (None, None)
    low = 0
    for out in refs:
        size = out.shape[0] - (2 * SUBLANES if lines and out is refs[0] else 0)
        rows = pl.ds(low, size)
        total = keep[rows, :].astype(jnp.float32) + received[rows, :].astype(jnp.float32)
        out[pl.ds(0, size), :] = total.astype(out.dtype)
        low += size
    if lines:
        totals = []
        for line in range(lines):
            totals.append(squares[line : line + 1, :] + unpacked(received, line))
            pair_squares[line : line + 1, :] = totals[-1]
        refs[0][pl.ds(refs[0].shape[0] - 2 * SUBLANES, 2 * SUBLANES), :] = packed(totals, refs[0].shape[1])


def table_kernel(live, span, frequencies, limit, far_cos, far_sin, near_cos, near_sin):
    limit[...] = jnp.full(limit.shape, live[lax.axis_index("serve")] * BLOCK, jnp.int32)
    blocks = far_cos.shape[0]
    start = span[lax.axis_index("serve")] * PAGE
    first = start + BLOCK * lax.broadcasted_iota(jnp.int32, (blocks, HD), 0)
    far = first.astype(jnp.float32) * frequencies[...]
    near = lax.broadcasted_iota(jnp.int32, (BLOCK, HD), 0).astype(jnp.float32) * frequencies[...]
    far_cos[...] = jnp.cos(far)
    far_sin[...] = jnp.sin(far)
    near_cos[...] = jnp.cos(near)
    near_sin[...] = jnp.sin(near)


def finish_kernel(first, at, line_at, count, chip_count, model_dim, *refs):
    keep, received, limit, far_cos, far_sin, near_cos, near_sin = refs[:7]
    pair_squares, carriers = refs[7], refs[8 : 7 + chip_count]
    arrived = refs[7 + chip_count : -4] or carriers
    out, staged, sems = refs[-3:]
    on_diagonal = lax.broadcasted_iota(jnp.int32, (LANES, LANES), 0) == lax.broadcasted_iota(
        jnp.int32, (LANES, LANES), 1
    )
    sign = jnp.where(lax.broadcasted_iota(jnp.int32, (1, HD), 1) < HD // 2, -1.0, 1.0)
    copies = []
    for index in range(count):
        start = (first + at + index) * TILE
        rows, inside = pl.ds(start, TILE), pl.ds(index * TILE, TILE)
        of_chunk = pl.ds((at + index) * TILE, TILE)
        values = keep[of_chunk, :].astype(jnp.float32) + received[of_chunk, :].astype(jnp.float32)
        for part in arrived:
            values += part[inside, :].astype(jnp.float32)
        columns = []
        for line in range((line_at + index) * TILE // LANES, (line_at + index + 1) * TILE // LANES):
            totals = pair_squares[line : line + 1, :]
            for ref in carriers:
                totals += unpacked(ref, line)
            columns.append(jnp.sum(jnp.where(on_diagonal, totals, 0.0), axis=1, keepdims=True))
        scales = 1.0 / jnp.sqrt(jnp.concatenate(columns, axis=0) / model_dim + norm_eps)
        alive = start + lax.broadcasted_iota(jnp.int32, (TILE, LANES), 0) < limit[0:1, :]
        cosines, sines = [], []
        for block in range(start // BLOCK, (start + TILE) // BLOCK):
            block_cos = far_cos[block : block + 1, :]
            block_sin = far_sin[block : block + 1, :]
            cosines.append(block_cos * near_cos[...] - block_sin * near_sin[...])
            sines.append((sign * block_sin) * near_cos[...] + (sign * block_cos) * near_sin[...])
        cosine = jnp.concatenate(cosines, axis=0)
        sine = jnp.concatenate(sines, axis=0)
        for low in range(0, out.shape[1], 2 * HD):
            key = values[:, low : low + HD] * scales
            turned = key * cosine + pltpu.roll(key, HD // 2, 1) * sine
            staged[inside, low : low + HD] = jnp.where(alive, turned, 0.0).astype(out.dtype)
            value = values[:, low + HD : low + 2 * HD] * scales
            staged[inside, low + HD : low + 2 * HD] = jnp.where(alive, value, 0.0).astype(out.dtype)
        copies.append(pltpu.make_async_copy(staged.at[inside, :], out.at[rows, :], sems.at[index]))
        copies[-1].start()
    for copy in copies:
        copy.wait()


def shards(tokens, norm_gain, kv_weight, live_blocks, span_offset):
    tensor_count = lax.axis_size("tensor")
    chip_count = tensor_count // 2
    me = lax.axis_index("tensor")
    slot_rows, depth = tokens.shape
    columns = kv_weight.shape[1] // tensor_count
    tiles = slot_rows // TILE
    model_dim = depth * tensor_count

    swap = [(i, i ^ 1) for i in range(tensor_count)]

    def shift(step):
        return [(i, (i + 2 * step) % tensor_count) for i in range(tensor_count)]

    def product(tokens, gain, kv_weight, step, first, count, staged=False, carrier=True, more=0):
        vmem = pl.BlockSpec(memory_space=pltpu.VMEM)
        rows = count * TILE
        out_shape = [jax.ShapeDtypeStruct((rows, columns), jnp.bfloat16)] * 2
        if carrier:
            out_shape[1] = jax.ShapeDtypeStruct((rows + 2 * SUBLANES, columns), jnp.bfloat16)
            out_shape.append(jax.ShapeDtypeStruct((rows // LANES + more * TILE // LANES, LANES), jnp.float32))
        if staged:
            out_shape.append(jax.ShapeDtypeStruct((depth, 2 * columns), jnp.bfloat16))
        scratch = [
            pltpu.VMEM((rows, depth), jnp.bfloat16),
            pltpu.VMEM((depth,), jnp.bfloat16),
            pltpu.SemaphoreType.DMA((CUTS,)),
            pltpu.SemaphoreType.DMA((count,)),
            pltpu.SemaphoreType.DMA,
        ]
        return pl.pallas_call(
            functools.partial(product_kernel, step, chip_count, first, staged, carrier, more),
            in_specs=[pl.BlockSpec(memory_space=pltpu.HBM) if staged else vmem] * 3,
            out_shape=out_shape,
            out_specs=[vmem] * len(out_shape),
            scratch_shapes=scratch if staged else [],
            compiler_params=FIRST if staged else PARAMS,
            cost_estimate=HEAVY if staged else COST,
        )(tokens, gain, kv_weight)

    def tables(live_blocks, span_offset):
        frequencies = rope_base ** (-(np.arange(HD // 2, dtype=np.float32) * 2.0) / HD)
        frequencies = np.concatenate([frequencies, frequencies])[None, :].astype(np.float32)
        shapes = [(slot_rows // BLOCK, HD)] * 2 + [(BLOCK, HD)] * 2
        made = pl.pallas_call(
            table_kernel,
            in_specs=[pl.BlockSpec(memory_space=pltpu.SMEM)] * 2 + [pl.BlockSpec(memory_space=pltpu.VMEM)],
            out_shape=[jax.ShapeDtypeStruct((8, LANES), jnp.int32)]
            + [jax.ShapeDtypeStruct(shape, jnp.float32) for shape in shapes],
            out_specs=[pl.BlockSpec(memory_space=pltpu.VMEM)] * 5,
            compiler_params=PARAMS,
            cost_estimate=COST,
        )(live_blocks, span_offset, jnp.asarray(frequencies))
        return list(made)

    def finish(first, at, line_at, count, keep, received, table, squares, carriers, arrived, result):
        vmem = pl.BlockSpec(memory_space=pltpu.VMEM)
        operands = [keep, received] + table + [squares] + carriers + (arrived if arrived is not carriers else [])
        aliases = {len(operands): 0}
        if result is None:
            result, aliases = jnp.zeros((1,), jnp.bfloat16), {}
        return pl.pallas_call(
            functools.partial(finish_kernel, first, at, line_at, count, chip_count, model_dim),
            in_specs=[vmem] * len(operands) + [pl.BlockSpec(memory_space=pl.ANY)],
            out_shape=jax.ShapeDtypeStruct((slot_rows, columns), jnp.bfloat16),
            out_specs=pl.BlockSpec(memory_space=pltpu.HBM),
            scratch_shapes=[pltpu.VMEM((count * TILE, columns), jnp.bfloat16), pltpu.SemaphoreType.DMA((count,))],
            input_output_aliases=aliases,
            compiler_params=PARAMS,
            cost_estimate=LATER,
        )(*operands, result)

    others = range(1, chip_count)
    firsts = [sum(CHUNKS[:index]) for index in range(len(CHUNKS))]
    chunk_count = len(CHUNKS)

    chunks = list(zip(firsts, CHUNKS))

    def add_halves(made, counts):
        sizes = [count * TILE for count in counts]
        added = []
        for keep, send, *squares in made:
            lines = squares[0].shape[0] if squares else 0
            out_shape = [jax.ShapeDtypeStruct((size, columns), keep.dtype) for size in sizes]
            if lines:
                out_shape[0] = jax.ShapeDtypeStruct((sizes[0] + 2 * SUBLANES, columns), keep.dtype)
                out_shape.insert(0, jax.ShapeDtypeStruct(squares[0].shape, squares[0].dtype))
            added.append(
                pl.pallas_call(
                    functools.partial(add_kernel, lines),
                    out_shape=out_shape,
                    compiler_params=PARAMS,
                    cost_estimate=COST,
                )(keep, lax.ppermute(send, "tensor", swap), *squares)
            )
        parts = [list(same) for same in zip(*added)]
        return (parts[1:], parts[0][0]) if lines else (parts, None)

    def cross(sums):
        return [lax.ppermute(part, "tensor", shift(step)) for step, part in zip(others, sums)]

    hold = lax.optimization_barrier
    made = [product(tokens, norm_gain, kv_weight, step, *chunks[0], staged=True) for step in others]
    weights = {step: parts[-1] for step, parts in zip(others, made)}
    made = [parts[:-1] for parts in made]
    made, gain, span_offset, live_blocks = hold((made, norm_gain, span_offset, live_blocks))
    table = tables(live_blocks, span_offset)
    sums = add_halves(made, chunks[0][1:])
    sums, gain, table = hold((sums, gain, table))
    tokens, gain, own_weight = pl.pallas_call(
        bring_kernel,
        in_specs=[pl.BlockSpec(memory_space=pltpu.HBM)] * 3,
        out_shape=[
            jax.ShapeDtypeStruct(shape, jnp.bfloat16) for shape in (tokens.shape, gain.shape, (depth, 2 * columns))
        ],
        out_specs=[pl.BlockSpec(memory_space=pltpu.VMEM)] * 3,
        scratch_shapes=[pltpu.SemaphoreType.DMA((3,))],
        compiler_params=BRING,
        cost_estimate=COST,
    )(tokens, gain, kv_weight)

    arrivals = [([cross(part) for part in sums[0]], sums[1])]
    for index in range(1, chunk_count):
        more = sum(CHUNKS[2:]) if index == 1 else 0
        made = [product(tokens, gain, weights[step], step, *chunks[index], carrier=index == 1, more=more) for step in others]
        count = chunks[index][1]
        sums = add_halves(made, (count - 1, 1) if count > 2 else (count,))
        if index == 2:
            sums, late = hold((sums, gain))
        arrivals.append(([cross(part) for part in sums[0]], sums[1]))
    own = [product(tokens, gain, own_weight, 0, *chunk, carrier=False) for chunk in chunks[:-1]]
    own.append(product(tokens, late, own_weight, 0, *chunks[-1], carrier=False))

    result = None
    for (first, count), (keep, send), (arrived, squares) in zip(chunks, own, arrivals):
        received = lax.ppermute(send, "tensor", swap)
        if squares is not None:
            carriers, pair_squares, line_at = arrived[0], squares, 0
        at = 0
        for part in arrived:
            size = part[0].shape[0] // TILE
            result = finish(first, at, line_at, size, keep, received, table, pair_squares, carriers, part, result)
            at += size
            line_at += size
    return result


def solution(mesh):
    in_specs = (
        P(("groups", "serve"), "tensor"),
        P("tensor"),
        P("tensor", None),
        P("groups"),
        P("groups"),
    )
    out_specs = P(("groups", "serve"), "tensor")
    return jax.shard_map(shards, mesh=mesh, in_specs=in_specs, out_specs=out_specs, check_vma=False)
```

```python
import functools

import jax
import jax.numpy as jnp
import numpy as np
from jax import lax
from jax.experimental import pallas as pl
from jax.experimental.pallas import tpu as pltpu
from jax.sharding import PartitionSpec as P

HD = 128
PAGE = 256
BLOCK = 64
LANES = 128
SUBLANES = 8

rope_base = 500000.0
norm_eps = 1e-05

TILE = 256
CUTS = 2
CHUNKS = (2, 1, 3)

PARAMS = pltpu.CompilerParams(vmem_limit_bytes=16 * 1024 * 1024)
FIRST = pltpu.CompilerParams(vmem_limit_bytes=51200 * 1024)
LATER = pl.CostEstimate(flops=20000000000, bytes_accessed=1, transcendentals=0)
HEAVY = pl.CostEstimate(flops=1000000000000, bytes_accessed=1, transcendentals=0)
BRING = pltpu.CompilerParams(vmem_limit_bytes=47104 * 1024)
COST = pl.CostEstimate(flops=1, bytes_accessed=1, transcendentals=0)


def square_lines(rows):
    lines = []
    for low in range(0, rows.shape[0], LANES):
        total = jnp.zeros((LANES, LANES), jnp.float32)
        for part in range(rows.shape[1] // LANES):
            wide = rows[low : low + LANES, part * LANES : (part + 1) * LANES].astype(jnp.float32)
            total += wide * wide
        lines.append(jnp.sum(jnp.transpose(total), axis=0, keepdims=True))
    return lines


def packed(squares, width):
    per_row = width // LANES
    row = lax.broadcasted_iota(jnp.int32, (2 * SUBLANES, LANES), 0)
    parts = []
    for place in range(per_row):
        part = jnp.zeros((2 * SUBLANES, LANES), jnp.float32)
        for index, line in enumerate(squares[place::per_row]):
            high = line.astype(jnp.bfloat16).astype(jnp.float32)
            part = jnp.where(row == index, high, part)
            part = jnp.where(row == SUBLANES + index, line - high, part)
        parts.append(part)
    return jnp.concatenate(parts, axis=1).astype(jnp.bfloat16)


def unpacked(ref, line):
    index, place = divmod(line, ref.shape[1] // LANES)
    part = ref[pl.ds(ref.shape[0] - 2 * SUBLANES, 2 * SUBLANES), place * LANES : (place + 1) * LANES]
    part = part.astype(jnp.float32)
    return part[index : index + 1] + part[SUBLANES + index : SUBLANES + index + 1]


def product_kernel(step, chip_count, first, staged, carrier, more, tokens, gain, weight, *refs):
    refs = list(refs)
    keep, send = refs.pop(0), refs.pop(0)
    squares = refs.pop(0) if carrier else None
    count = keep.shape[0] // TILE
    depth, width = tokens.shape[1], 2 * keep.shape[1]
    me = lax.axis_index("tensor")
    core = lax.rem(me, 2)
    chip = lax.rem(lax.div(me, 2) + step, chip_count)
    place = pl.ds(pl.multiple_of(chip * width, width), width)

    weight_copies, row_copies = [], []
    if staged:
        weight_buf, rows_buf, gain_buf, weight_sems, row_sems, gain_sem = refs
        cut = depth // CUTS
        gain_copy = pltpu.make_async_copy(gain, gain_buf, gain_sem)
        for index in range(CUTS):
            some = pl.ds(index * cut, cut)
            weight_copies.append(
                pltpu.make_async_copy(weight.at[some, place], weight_buf.at[some, :], weight_sems.at[index])
            )
        for tile in range(count):
            rows = tokens.at[pl.ds((first + tile) * TILE, TILE), :]
            row_copies.append(
                pltpu.make_async_copy(rows, rows_buf.at[pl.ds(tile * TILE, TILE), :], row_sems.at[tile])
            )
        for copy in [gain_copy] + row_copies[:1] + weight_copies + row_copies[1:]:
            copy.start()
        gain_copy.wait()
        gains = gain_buf[...].reshape(1, depth)
    else:
        gains = gain[...].reshape(1, depth)

    lines = []
    for tile in range(count):
        inside = pl.ds(tile * TILE, TILE)
        if staged:
            row_copies[tile].wait()
            rows = rows_buf[inside, :]
        else:
            rows = tokens[pl.ds((first + tile) * TILE, TILE), :]
        scaled = rows * gains
        if weight_copies:
            product = jnp.zeros((TILE, width), jnp.float32)
            for index, copy in enumerate(weight_copies):
                copy.wait()
                span = slice(index * cut, (index + 1) * cut)
                product += jnp.dot(scaled[:, span], weight_buf[span, :], preferred_element_type=jnp.float32)
            weight_copies = []
        else:
            columns = weight_buf[...] if staged else weight[...]
            product = jnp.dot(scaled, columns, preferred_element_type=jnp.float32)
        left = product[:, : width // 2].astype(jnp.bfloat16)
        right = product[:, width // 2 :].astype(jnp.bfloat16)
        keep[inside, :] = jnp.where(core == 0, left, right)
        send[inside, :] = jnp.where(core == 0, right, left)
        if carrier:
            lines += square_lines(rows)
    for tile in range(count, count + more):
        lines += square_lines(tokens[pl.ds((first + tile) * TILE, TILE), :])
    if carrier:
        for index, line in enumerate(lines):
            squares[index : index + 1, :] = line
        send[pl.ds(keep.shape[0], 2 * SUBLANES), :] = packed(lines, send.shape[1])


def bring_kernel(tokens, gain, weight, rows_out, gain_out, weight_out, sems):
    width = weight_out.shape[1]
    chip = lax.div(lax.axis_index("tensor"), 2)
    place = pl.ds(pl.multiple_of(chip * width, width), width)
    moves = [
        pltpu.make_async_copy(tokens, rows_out, sems.at[0]),
        pltpu.make_async_copy(gain, gain_out, sems.at[1]),
        pltpu.make_async_copy(weight.at[:, place], weight_out, sems.at[2]),
    ]
    for move in moves:
        move.start()
    for move in moves:
        move.wait()


def add_kernel(lines, keep, received, *refs):
    refs = list(refs)
    squares, pair_squares = (refs.pop(0), refs.pop(0)) if lines else (None, None)
    low = 0
    for out in refs:
        size = out.shape[0] - (2 * SUBLANES if lines and out is refs[0] else 0)
        rows = pl.ds(low, size)
        total = keep[rows, :].astype(jnp.float32) + received[rows, :].astype(jnp.float32)
        out[pl.ds(0, size), :] = total.astype(out.dtype)
        low += size
    if lines:
        totals = []
        for line in range(lines):
            totals.append(squares[line : line + 1, :] + unpacked(received, line))
            pair_squares[line : line + 1, :] = totals[-1]
        refs[0][pl.ds(refs[0].shape[0] - 2 * SUBLANES, 2 * SUBLANES), :] = packed(totals, refs[0].shape[1])


def table_kernel(live, span, frequencies, limit, far_cos, far_sin, near_cos, near_sin):
    limit[...] = jnp.full(limit.shape, live[lax.axis_index("serve")] * BLOCK, jnp.int32)
    blocks = far_cos.shape[0]
    start = span[lax.axis_index("serve")] * PAGE
    first = start + BLOCK * lax.broadcasted_iota(jnp.int32, (blocks, HD), 0)
    far = first.astype(jnp.float32) * frequencies[...]
    near = lax.broadcasted_iota(jnp.int32, (BLOCK, HD), 0).astype(jnp.float32) * frequencies[...]
    far_cos[...] = jnp.cos(far)
    far_sin[...] = jnp.sin(far)
    near_cos[...] = jnp.cos(near)
    near_sin[...] = jnp.sin(near)


def finish_kernel(first, at, line_at, count, chip_count, model_dim, *refs):
    keep, received, limit, far_cos, far_sin, near_cos, near_sin = refs[:7]
    pair_squares, carriers = refs[7], refs[8 : 7 + chip_count]
    arrived = refs[7 + chip_count : -4] or carriers
    out, staged, sems = refs[-3:]
    on_diagonal = lax.broadcasted_iota(jnp.int32, (LANES, LANES), 0) == lax.broadcasted_iota(
        jnp.int32, (LANES, LANES), 1
    )
    sign = jnp.where(lax.broadcasted_iota(jnp.int32, (1, HD), 1) < HD // 2, -1.0, 1.0)
    copies = []
    for index in range(count):
        start = (first + at + index) * TILE
        rows, inside = pl.ds(start, TILE), pl.ds(index * TILE, TILE)
        of_chunk = pl.ds((at + index) * TILE, TILE)
        values = keep[of_chunk, :].astype(jnp.float32) + received[of_chunk, :].astype(jnp.float32)
        for part in arrived:
            values += part[inside, :].astype(jnp.float32)
        columns = []
        for line in range((line_at + index) * TILE // LANES, (line_at + index + 1) * TILE // LANES):
            totals = pair_squares[line : line + 1, :]
            for ref in carriers:
                totals += unpacked(ref, line)
            columns.append(jnp.sum(jnp.where(on_diagonal, totals, 0.0), axis=1, keepdims=True))
        scales = 1.0 / jnp.sqrt(jnp.concatenate(columns, axis=0) / model_dim + norm_eps)
        alive = start + lax.broadcasted_iota(jnp.int32, (TILE, LANES), 0) < limit[0:1, :]
        cosines, sines = [], []
        for block in range(start // BLOCK, (start + TILE) // BLOCK):
            block_cos = far_cos[block : block + 1, :]
            block_sin = far_sin[block : block + 1, :]
            cosines.append(block_cos * near_cos[...] - block_sin * near_sin[...])
            sines.append((sign * block_sin) * near_cos[...] + (sign * block_cos) * near_sin[...])
        cosine = jnp.concatenate(cosines, axis=0)
        sine = jnp.concatenate(sines, axis=0)
        for low in range(0, out.shape[1], 2 * HD):
            key = values[:, low : low + HD] * scales
            turned = key * cosine + pltpu.roll(key, HD // 2, 1) * sine
            staged[inside, low : low + HD] = jnp.where(alive, turned, 0.0).astype(out.dtype)
            value = values[:, low + HD : low + 2 * HD] * scales
            staged[inside, low + HD : low + 2 * HD] = jnp.where(alive, value, 0.0).astype(out.dtype)
        copies.append(pltpu.make_async_copy(staged.at[inside, :], out.at[rows, :], sems.at[index]))
        copies[-1].start()
    for copy in copies:
        copy.wait()


def shards(tokens, norm_gain, kv_weight, live_blocks, span_offset):
    tensor_count = lax.axis_size("tensor")
    chip_count = tensor_count // 2
    me = lax.axis_index("tensor")
    slot_rows, depth = tokens.shape
    columns = kv_weight.shape[1] // tensor_count
    tiles = slot_rows // TILE
    model_dim = depth * tensor_count

    swap = [(i, i ^ 1) for i in range(tensor_count)]

    def shift(step):
        return [(i, (i + 2 * step) % tensor_count) for i in range(tensor_count)]

    def product(tokens, gain, kv_weight, step, first, count, staged=False, carrier=True, more=0):
        vmem = pl.BlockSpec(memory_space=pltpu.VMEM)
        rows = count * TILE
        out_shape = [jax.ShapeDtypeStruct((rows, columns), jnp.bfloat16)] * 2
        if carrier:
            out_shape[1] = jax.ShapeDtypeStruct((rows + 2 * SUBLANES, columns), jnp.bfloat16)
            out_shape.append(jax.ShapeDtypeStruct((rows // LANES + more * TILE // LANES, LANES), jnp.float32))
        if staged:
            out_shape.append(jax.ShapeDtypeStruct((depth, 2 * columns), jnp.bfloat16))
        scratch = [
            pltpu.VMEM((rows, depth), jnp.bfloat16),
            pltpu.VMEM((depth,), jnp.bfloat16),
            pltpu.SemaphoreType.DMA((CUTS,)),
            pltpu.SemaphoreType.DMA((count,)),
            pltpu.SemaphoreType.DMA,
        ]
        return pl.pallas_call(
            functools.partial(product_kernel, step, chip_count, first, staged, carrier, more),
            in_specs=[pl.BlockSpec(memory_space=pltpu.HBM) if staged else vmem] * 3,
            out_shape=out_shape,
            out_specs=[vmem] * len(out_shape),
            scratch_shapes=scratch if staged else [],
            compiler_params=FIRST if staged else PARAMS,
            cost_estimate=HEAVY if staged else COST,
        )(tokens, gain, kv_weight)

    def tables(live_blocks, span_offset):
        frequencies = rope_base ** (-(np.arange(HD // 2, dtype=np.float32) * 2.0) / HD)
        frequencies = np.concatenate([frequencies, frequencies])[None, :].astype(np.float32)
        shapes = [(slot_rows // BLOCK, HD)] * 2 + [(BLOCK, HD)] * 2
        made = pl.pallas_call(
            table_kernel,
            in_specs=[pl.BlockSpec(memory_space=pltpu.SMEM)] * 2 + [pl.BlockSpec(memory_space=pltpu.VMEM)],
            out_shape=[jax.ShapeDtypeStruct((8, LANES), jnp.int32)]
            + [jax.ShapeDtypeStruct(shape, jnp.float32) for shape in shapes],
            out_specs=[pl.BlockSpec(memory_space=pltpu.VMEM)] * 5,
            compiler_params=PARAMS,
            cost_estimate=COST,
        )(live_blocks, span_offset, jnp.asarray(frequencies))
        return list(made)

    def finish(first, at, line_at, count, keep, received, table, squares, carriers, arrived, result):
        vmem = pl.BlockSpec(memory_space=pltpu.VMEM)
        operands = [keep, received] + table + [squares] + carriers + (arrived if arrived is not carriers else [])
        aliases = {len(operands): 0}
        if result is None:
            result, aliases = jnp.zeros((1,), jnp.bfloat16), {}
        return pl.pallas_call(
            functools.partial(finish_kernel, first, at, line_at, count, chip_count, model_dim),
            in_specs=[vmem] * len(operands) + [pl.BlockSpec(memory_space=pl.ANY)],
            out_shape=jax.ShapeDtypeStruct((slot_rows, columns), jnp.bfloat16),
            out_specs=pl.BlockSpec(memory_space=pltpu.HBM),
            scratch_shapes=[pltpu.VMEM((count * TILE, columns), jnp.bfloat16), pltpu.SemaphoreType.DMA((count,))],
            input_output_aliases=aliases,
            compiler_params=PARAMS,
            cost_estimate=LATER,
        )(*operands, result)

    others = range(1, chip_count)
    firsts = [sum(CHUNKS[:index]) for index in range(len(CHUNKS))]
    chunk_count = len(CHUNKS)

    chunks = list(zip(firsts, CHUNKS))

    def add_halves(made, counts):
        sizes = [count * TILE for count in counts]
        added = []
        for keep, send, *squares in made:
            lines = squares[0].shape[0] if squares else 0
            out_shape = [jax.ShapeDtypeStruct((size, columns), keep.dtype) for size in sizes]
            if lines:
                out_shape[0] = jax.ShapeDtypeStruct((sizes[0] + 2 * SUBLANES, columns), keep.dtype)
                out_shape.insert(0, jax.ShapeDtypeStruct(squares[0].shape, squares[0].dtype))
            added.append(
                pl.pallas_call(
                    functools.partial(add_kernel, lines),
                    out_shape=out_shape,
                    compiler_params=PARAMS,
                    cost_estimate=COST,
                )(keep, lax.ppermute(send, "tensor", swap), *squares)
            )
        parts = [list(same) for same in zip(*added)]
        return (parts[1:], parts[0][0]) if lines else (parts, None)

    def cross(sums):
        return [lax.ppermute(part, "tensor", shift(step)) for step, part in zip(others, sums)]

    hold = lax.optimization_barrier
    made = [product(tokens, norm_gain, kv_weight, step, *chunks[0], staged=True) for step in others]
    weights = {step: parts[-1] for step, parts in zip(others, made)}
    made = [parts[:-1] for parts in made]
    made, gain, span_offset, live_blocks = hold((made, norm_gain, span_offset, live_blocks))
    table = tables(live_blocks, span_offset)
    sums = add_halves(made, chunks[0][1:])
    sums, gain, table = hold((sums, gain, table))
    tokens, gain, own_weight = pl.pallas_call(
        bring_kernel,
        in_specs=[pl.BlockSpec(memory_space=pltpu.HBM)] * 3,
        out_shape=[
            jax.ShapeDtypeStruct(shape, jnp.bfloat16) for shape in (tokens.shape, gain.shape, (depth, 2 * columns))
        ],
        out_specs=[pl.BlockSpec(memory_space=pltpu.VMEM)] * 3,
        scratch_shapes=[pltpu.SemaphoreType.DMA((3,))],
        compiler_params=BRING,
        cost_estimate=COST,
    )(tokens, gain, kv_weight)

    arrivals = [([cross(part) for part in sums[0]], sums[1])]
    for index in range(1, chunk_count):
        more = sum(CHUNKS[2:]) if index == 1 else 0
        made = [product(tokens, gain, weights[step], step, *chunks[index], carrier=index == 1, more=more) for step in others]
        count = chunks[index][1]
        sums = add_halves(made, (count - 1, 1) if count > 2 else (count,))
        if index == 2:
            sums, late = hold((sums, gain))
        arrivals.append(([cross(part) for part in sums[0]], sums[1]))
    own = [product(tokens, gain, own_weight, 0, *chunk, carrier=False) for chunk in chunks[:-1]]
    own.append(product(tokens, late, own_weight, 0, *chunks[-1], carrier=False))

    result = None
    for (first, count), (keep, send), (arrived, squares) in zip(chunks, own, arrivals):
        received = lax.ppermute(send, "tensor", swap)
        if squares is not None:
            carriers, pair_squares, line_at = arrived[0], squares, 0
        at = 0
        for part in arrived:
            size = part[0].shape[0] // TILE
            result = finish(first, at, line_at, size, keep, received, table, pair_squares, carriers, part, result)
            at += size
            line_at += size
    return result


def solution(mesh):
    in_specs = (
        P(("groups", "serve"), "tensor"),
        P("tensor"),
        P("tensor", None),
        P("groups"),
        P("groups"),
    )
    out_specs = P(("groups", "serve"), "tensor")
    return jax.shard_map(shards, mesh=mesh, in_specs=in_specs, out_specs=out_specs, check_vma=False)
```

```python
import functools

import jax
import jax.numpy as jnp
import numpy as np
from jax import lax
from jax.experimental import pallas as pl
from jax.experimental.pallas import tpu as pltpu
from jax.sharding import PartitionSpec as P

HD = 128
PAGE = 256
BLOCK = 64
LANES = 128
SUBLANES = 8

rope_base = 500000.0
norm_eps = 1e-05

TILE = 256
CUTS = 8
CHUNKS = (2, 1, 3)

PARAMS = pltpu.CompilerParams(vmem_limit_bytes=16 * 1024 * 1024)
FIRST = pltpu.CompilerParams(vmem_limit_bytes=51200 * 1024)
LATER = pl.CostEstimate(flops=20000000000, bytes_accessed=1, transcendentals=0)
HEAVY = pl.CostEstimate(flops=1000000000000, bytes_accessed=1, transcendentals=0)
BRING = pltpu.CompilerParams(vmem_limit_bytes=47104 * 1024)
COST = pl.CostEstimate(flops=1, bytes_accessed=1, transcendentals=0)


def square_lines(rows):
    lines = []
    for low in range(0, rows.shape[0], LANES):
        total = jnp.zeros((LANES, LANES), jnp.float32)
        for part in range(rows.shape[1] // LANES):
            wide = rows[low : low + LANES, part * LANES : (part + 1) * LANES].astype(jnp.float32)
            total += wide * wide
        lines.append(jnp.sum(jnp.transpose(total), axis=0, keepdims=True))
    return lines


def packed(squares, width):
    per_row = width // LANES
    row = lax.broadcasted_iota(jnp.int32, (2 * SUBLANES, LANES), 0)
    parts = []
    for place in range(per_row):
        part = jnp.zeros((2 * SUBLANES, LANES), jnp.float32)
        for index, line in enumerate(squares[place::per_row]):
            high = line.astype(jnp.bfloat16).astype(jnp.float32)
            part = jnp.where(row == index, high, part)
            part = jnp.where(row == SUBLANES + index, line - high, part)
        parts.append(part)
    return jnp.concatenate(parts, axis=1).astype(jnp.bfloat16)


def unpacked(ref, line):
    index, place = divmod(line, ref.shape[1] // LANES)
    part = ref[pl.ds(ref.shape[0] - 2 * SUBLANES, 2 * SUBLANES), place * LANES : (place + 1) * LANES]
    part = part.astype(jnp.float32)
    return part[index : index + 1] + part[SUBLANES + index : SUBLANES + index + 1]


def product_kernel(step, chip_count, first, staged, carrier, more, tokens, gain, weight, *refs):
    refs = list(refs)
    keep, send = refs.pop(0), refs.pop(0)
    squares = refs.pop(0) if carrier else None
    count = keep.shape[0] // TILE
    depth, width = tokens.shape[1], 2 * keep.shape[1]
    me = lax.axis_index("tensor")
    core = lax.rem(me, 2)
    chip = lax.rem(lax.div(me, 2) + step, chip_count)
    place = pl.ds(pl.multiple_of(chip * width, width), width)

    weight_copies, row_copies = [], []
    if staged:
        weight_buf, rows_buf, gain_buf, weight_sems, row_sems, gain_sem = refs
        cut = depth // CUTS
        gain_copy = pltpu.make_async_copy(gain, gain_buf, gain_sem)
        for index in range(CUTS):
            some = pl.ds(index * cut, cut)
            weight_copies.append(
                pltpu.make_async_copy(weight.at[some, place], weight_buf.at[some, :], weight_sems.at[index])
            )
        for tile in range(count):
            rows = tokens.at[pl.ds((first + tile) * TILE, TILE), :]
            row_copies.append(
                pltpu.make_async_copy(rows, rows_buf.at[pl.ds(tile * TILE, TILE), :], row_sems.at[tile])
            )
        for copy in [gain_copy] + row_copies[:1] + weight_copies + row_copies[1:]:
            copy.start()
        gain_copy.wait()
        gains = gain_buf[...].reshape(1, depth)
    else:
        gains = gain[...].reshape(1, depth)

    lines = []
    for tile in range(count):
        inside = pl.ds(tile * TILE, TILE)
        if staged:
            row_copies[tile].wait()
            rows = rows_buf[inside, :]
        else:
            rows = tokens[pl.ds((first + tile) * TILE, TILE), :]
        scaled = rows * gains
        if weight_copies:
            product = jnp.zeros((TILE, width), jnp.float32)
            for index, copy in enumerate(weight_copies):
                copy.wait()
                span = slice(index * cut, (index + 1) * cut)
                product += jnp.dot(scaled[:, span], weight_buf[span, :], preferred_element_type=jnp.float32)
            weight_copies = []
        else:
            columns = weight_buf[...] if staged else weight[...]
            product = jnp.dot(scaled, columns, preferred_element_type=jnp.float32)
        left = product[:, : width // 2].astype(jnp.bfloat16)
        right = product[:, width // 2 :].astype(jnp.bfloat16)
        keep[inside, :] = jnp.where(core == 0, left, right)
        send[inside, :] = jnp.where(core == 0, right, left)
        if carrier:
            lines += square_lines(rows)
    for tile in range(count, count + more):
        lines += square_lines(tokens[pl.ds((first + tile) * TILE, TILE), :])
    if carrier:
        for index, line in enumerate(lines):
            squares[index : index + 1, :] = line
        send[pl.ds(keep.shape[0], 2 * SUBLANES), :] = packed(lines, send.shape[1])


def bring_kernel(tokens, gain, weight, rows_out, gain_out, weight_out, sems):
    width = weight_out.shape[1]
    chip = lax.div(lax.axis_index("tensor"), 2)
    place = pl.ds(pl.multiple_of(chip * width, width), width)
    moves = [
        pltpu.make_async_copy(tokens, rows_out, sems.at[0]),
        pltpu.make_async_copy(gain, gain_out, sems.at[1]),
        pltpu.make_async_copy(weight.at[:, place], weight_out, sems.at[2]),
    ]
    for move in moves:
        move.start()
    for move in moves:
        move.wait()


def add_kernel(lines, keep, received, *refs):
    refs = list(refs)
    squares, pair_squares = (refs.pop(0), refs.pop(0)) if lines else (None, None)
    low = 0
    for out in refs:
        size = out.shape[0] - (2 * SUBLANES if lines and out is refs[0] else 0)
        rows = pl.ds(low, size)
        total = keep[rows, :].astype(jnp.float32) + received[rows, :].astype(jnp.float32)
        out[pl.ds(0, size), :] = total.astype(out.dtype)
        low += size
    if lines:
        totals = []
        for line in range(lines):
            totals.append(squares[line : line + 1, :] + unpacked(received, line))
            pair_squares[line : line + 1, :] = totals[-1]
        refs[0][pl.ds(refs[0].shape[0] - 2 * SUBLANES, 2 * SUBLANES), :] = packed(totals, refs[0].shape[1])


def table_kernel(live, span, frequencies, limit, far_cos, far_sin, near_cos, near_sin):
    limit[...] = jnp.full(limit.shape, live[lax.axis_index("serve")] * BLOCK, jnp.int32)
    blocks = far_cos.shape[0]
    start = span[lax.axis_index("serve")] * PAGE
    first = start + BLOCK * lax.broadcasted_iota(jnp.int32, (blocks, HD), 0)
    far = first.astype(jnp.float32) * frequencies[...]
    near = lax.broadcasted_iota(jnp.int32, (BLOCK, HD), 0).astype(jnp.float32) * frequencies[...]
    far_cos[...] = jnp.cos(far)
    far_sin[...] = jnp.sin(far)
    near_cos[...] = jnp.cos(near)
    near_sin[...] = jnp.sin(near)


def finish_kernel(first, at, line_at, count, chip_count, model_dim, *refs):
    keep, received, limit, far_cos, far_sin, near_cos, near_sin = refs[:7]
    pair_squares, carriers = refs[7], refs[8 : 7 + chip_count]
    arrived = refs[7 + chip_count : -4] or carriers
    out, staged, sems = refs[-3:]
    on_diagonal = lax.broadcasted_iota(jnp.int32, (LANES, LANES), 0) == lax.broadcasted_iota(
        jnp.int32, (LANES, LANES), 1
    )
    sign = jnp.where(lax.broadcasted_iota(jnp.int32, (1, HD), 1) < HD // 2, -1.0, 1.0)
    copies = []
    for index in range(count):
        start = (first + at + index) * TILE
        rows, inside = pl.ds(start, TILE), pl.ds(index * TILE, TILE)
        of_chunk = pl.ds((at + index) * TILE, TILE)
        values = keep[of_chunk, :].astype(jnp.float32) + received[of_chunk, :].astype(jnp.float32)
        for part in arrived:
            values += part[inside, :].astype(jnp.float32)
        columns = []
        for line in range((line_at + index) * TILE // LANES, (line_at + index + 1) * TILE // LANES):
            totals = pair_squares[line : line + 1, :]
            for ref in carriers:
                totals += unpacked(ref, line)
            columns.append(jnp.sum(jnp.where(on_diagonal, totals, 0.0), axis=1, keepdims=True))
        scales = 1.0 / jnp.sqrt(jnp.concatenate(columns, axis=0) / model_dim + norm_eps)
        alive = start + lax.broadcasted_iota(jnp.int32, (TILE, LANES), 0) < limit[0:1, :]
        cosines, sines = [], []
        for block in range(start // BLOCK, (start + TILE) // BLOCK):
            block_cos = far_cos[block : block + 1, :]
            block_sin = far_sin[block : block + 1, :]
            cosines.append(block_cos * near_cos[...] - block_sin * near_sin[...])
            sines.append((sign * block_sin) * near_cos[...] + (sign * block_cos) * near_sin[...])
        cosine = jnp.concatenate(cosines, axis=0)
        sine = jnp.concatenate(sines, axis=0)
        for low in range(0, out.shape[1], 2 * HD):
            key = values[:, low : low + HD] * scales
            turned = key * cosine + pltpu.roll(key, HD // 2, 1) * sine
            staged[inside, low : low + HD] = jnp.where(alive, turned, 0.0).astype(out.dtype)
            value = values[:, low + HD : low + 2 * HD] * scales
            staged[inside, low + HD : low + 2 * HD] = jnp.where(alive, value, 0.0).astype(out.dtype)
        copies.append(pltpu.make_async_copy(staged.at[inside, :], out.at[rows, :], sems.at[index]))
        copies[-1].start()
    for copy in copies:
        copy.wait()


def shards(tokens, norm_gain, kv_weight, live_blocks, span_offset):
    tensor_count = lax.axis_size("tensor")
    chip_count = tensor_count // 2
    me = lax.axis_index("tensor")
    slot_rows, depth = tokens.shape
    columns = kv_weight.shape[1] // tensor_count
    tiles = slot_rows // TILE
    model_dim = depth * tensor_count

    swap = [(i, i ^ 1) for i in range(tensor_count)]

    def shift(step):
        return [(i, (i + 2 * step) % tensor_count) for i in range(tensor_count)]

    def product(tokens, gain, kv_weight, step, first, count, staged=False, carrier=True, more=0):
        vmem = pl.BlockSpec(memory_space=pltpu.VMEM)
        rows = count * TILE
        out_shape = [jax.ShapeDtypeStruct((rows, columns), jnp.bfloat16)] * 2
        if carrier:
            out_shape[1] = jax.ShapeDtypeStruct((rows + 2 * SUBLANES, columns), jnp.bfloat16)
            out_shape.append(jax.ShapeDtypeStruct((rows // LANES + more * TILE // LANES, LANES), jnp.float32))
        if staged:
            out_shape.append(jax.ShapeDtypeStruct((depth, 2 * columns), jnp.bfloat16))
        scratch = [
            pltpu.VMEM((rows, depth), jnp.bfloat16),
            pltpu.VMEM((depth,), jnp.bfloat16),
            pltpu.SemaphoreType.DMA((CUTS,)),
            pltpu.SemaphoreType.DMA((count,)),
            pltpu.SemaphoreType.DMA,
        ]
        return pl.pallas_call(
            functools.partial(product_kernel, step, chip_count, first, staged, carrier, more),
            in_specs=[pl.BlockSpec(memory_space=pltpu.HBM) if staged else vmem] * 3,
            out_shape=out_shape,
            out_specs=[vmem] * len(out_shape),
            scratch_shapes=scratch if staged else [],
            compiler_params=FIRST if staged else PARAMS,
            cost_estimate=HEAVY if staged else COST,
        )(tokens, gain, kv_weight)

    def tables(live_blocks, span_offset):
        frequencies = rope_base ** (-(np.arange(HD // 2, dtype=np.float32) * 2.0) / HD)
        frequencies = np.concatenate([frequencies, frequencies])[None, :].astype(np.float32)
        shapes = [(slot_rows // BLOCK, HD)] * 2 + [(BLOCK, HD)] * 2
        made = pl.pallas_call(
            table_kernel,
            in_specs=[pl.BlockSpec(memory_space=pltpu.SMEM)] * 2 + [pl.BlockSpec(memory_space=pltpu.VMEM)],
            out_shape=[jax.ShapeDtypeStruct((8, LANES), jnp.int32)]
            + [jax.ShapeDtypeStruct(shape, jnp.float32) for shape in shapes],
            out_specs=[pl.BlockSpec(memory_space=pltpu.VMEM)] * 5,
            compiler_params=PARAMS,
            cost_estimate=COST,
        )(live_blocks, span_offset, jnp.asarray(frequencies))
        return list(made)

    def finish(first, at, line_at, count, keep, received, table, squares, carriers, arrived, result):
        vmem = pl.BlockSpec(memory_space=pltpu.VMEM)
        operands = [keep, received] + table + [squares] + carriers + (arrived if arrived is not carriers else [])
        aliases = {len(operands): 0}
        if result is None:
            result, aliases = jnp.zeros((1,), jnp.bfloat16), {}
        return pl.pallas_call(
            functools.partial(finish_kernel, first, at, line_at, count, chip_count, model_dim),
            in_specs=[vmem] * len(operands) + [pl.BlockSpec(memory_space=pl.ANY)],
            out_shape=jax.ShapeDtypeStruct((slot_rows, columns), jnp.bfloat16),
            out_specs=pl.BlockSpec(memory_space=pltpu.HBM),
            scratch_shapes=[pltpu.VMEM((count * TILE, columns), jnp.bfloat16), pltpu.SemaphoreType.DMA((count,))],
            input_output_aliases=aliases,
            compiler_params=PARAMS,
            cost_estimate=LATER,
        )(*operands, result)

    others = range(1, chip_count)
    firsts = [sum(CHUNKS[:index]) for index in range(len(CHUNKS))]
    chunk_count = len(CHUNKS)

    chunks = list(zip(firsts, CHUNKS))

    def add_halves(made, counts):
        sizes = [count * TILE for count in counts]
        added = []
        for keep, send, *squares in made:
            lines = squares[0].shape[0] if squares else 0
            out_shape = [jax.ShapeDtypeStruct((size, columns), keep.dtype) for size in sizes]
            if lines:
                out_shape[0] = jax.ShapeDtypeStruct((sizes[0] + 2 * SUBLANES, columns), keep.dtype)
                out_shape.insert(0, jax.ShapeDtypeStruct(squares[0].shape, squares[0].dtype))
            added.append(
                pl.pallas_call(
                    functools.partial(add_kernel, lines),
                    out_shape=out_shape,
                    compiler_params=PARAMS,
                    cost_estimate=COST,
                )(keep, lax.ppermute(send, "tensor", swap), *squares)
            )
        parts = [list(same) for same in zip(*added)]
        return (parts[1:], parts[0][0]) if lines else (parts, None)

    def cross(sums):
        return [lax.ppermute(part, "tensor", shift(step)) for step, part in zip(others, sums)]

    hold = lax.optimization_barrier
    made = [product(tokens, norm_gain, kv_weight, step, *chunks[0], staged=True) for step in others]
    weights = {step: parts[-1] for step, parts in zip(others, made)}
    made = [parts[:-1] for parts in made]
    made, gain, span_offset, live_blocks = hold((made, norm_gain, span_offset, live_blocks))
    table = tables(live_blocks, span_offset)
    sums = add_halves(made, chunks[0][1:])
    sums, gain, table = hold((sums, gain, table))
    tokens, gain, own_weight = pl.pallas_call(
        bring_kernel,
        in_specs=[pl.BlockSpec(memory_space=pltpu.HBM)] * 3,
        out_shape=[
            jax.ShapeDtypeStruct(shape, jnp.bfloat16) for shape in (tokens.shape, gain.shape, (depth, 2 * columns))
        ],
        out_specs=[pl.BlockSpec(memory_space=pltpu.VMEM)] * 3,
        scratch_shapes=[pltpu.SemaphoreType.DMA((3,))],
        compiler_params=BRING,
        cost_estimate=COST,
    )(tokens, gain, kv_weight)

    arrivals = [([cross(part) for part in sums[0]], sums[1])]
    for index in range(1, chunk_count):
        more = sum(CHUNKS[2:]) if index == 1 else 0
        made = [product(tokens, gain, weights[step], step, *chunks[index], carrier=index == 1, more=more) for step in others]
        count = chunks[index][1]
        sums = add_halves(made, (count - 1, 1) if count > 2 else (count,))
        if index == 2:
            sums, late = hold((sums, gain))
        arrivals.append(([cross(part) for part in sums[0]], sums[1]))
    own = [product(tokens, gain, own_weight, 0, *chunk, carrier=False) for chunk in chunks[:-1]]
    own.append(product(tokens, late, own_weight, 0, *chunks[-1], carrier=False))

    result = None
    for (first, count), (keep, send), (arrived, squares) in zip(chunks, own, arrivals):
        received = lax.ppermute(send, "tensor", swap)
        if squares is not None:
            carriers, pair_squares, line_at = arrived[0], squares, 0
        at = 0
        for part in arrived:
            size = part[0].shape[0] // TILE
            result = finish(first, at, line_at, size, keep, received, table, pair_squares, carriers, part, result)
            at += size
            line_at += size
    return result


def solution(mesh):
    in_specs = (
        P(("groups", "serve"), "tensor"),
        P("tensor"),
        P("tensor", None),
        P("groups"),
        P("groups"),
    )
    out_specs = P(("groups", "serve"), "tensor")
    return jax.shard_map(shards, mesh=mesh, in_specs=in_specs, out_specs=out_specs, check_vma=False)
```

```python
import functools

import jax
import jax.numpy as jnp
import numpy as np
from jax import lax
from jax.experimental import pallas as pl
from jax.experimental.pallas import tpu as pltpu
from jax.sharding import PartitionSpec as P

HD = 128
PAGE = 256
BLOCK = 64
LANES = 128
SUBLANES = 8
BF16_MAX = float(jnp.finfo(jnp.bfloat16).max)

rope_base = 500000.0
norm_eps = 1e-05

TILE = 256
CUTS = 4
CHUNKS = (2, 1, 3)

PARAMS = pltpu.CompilerParams(vmem_limit_bytes=16 * 1024 * 1024)
FIRST = pltpu.CompilerParams(vmem_limit_bytes=51200 * 1024)
LATER = pl.CostEstimate(flops=20000000000, bytes_accessed=1, transcendentals=0)
HEAVY = pl.CostEstimate(flops=1000000000000, bytes_accessed=1, transcendentals=0)
BRING = pltpu.CompilerParams(vmem_limit_bytes=47104 * 1024)
COST = pl.CostEstimate(flops=1, bytes_accessed=1, transcendentals=0)


def square_lines(rows):
    lines = []
    for low in range(0, rows.shape[0], LANES):
        total = jnp.zeros((LANES, LANES), jnp.float32)
        for part in range(rows.shape[1] // LANES):
            wide = rows[low : low + LANES, part * LANES : (part + 1) * LANES].astype(jnp.float32)
            total += wide * wide
        lines.append(jnp.sum(jnp.transpose(total), axis=0, keepdims=True))
    return lines


def packed(squares, width):
    per_row = width // LANES
    row = lax.broadcasted_iota(jnp.int32, (2 * SUBLANES, LANES), 0)
    parts = []
    for place in range(per_row):
        part = jnp.zeros((2 * SUBLANES, LANES), jnp.float32)
        for index, line in enumerate(squares[place::per_row]):
            finite = line < jnp.inf
            high = jnp.where(finite, jnp.minimum(line, BF16_MAX), line).astype(jnp.bfloat16).astype(jnp.float32)
            part = jnp.where(row == index, high, part)
            part = jnp.where(row == SUBLANES + index, jnp.where(finite, line - high, 0.0), part)
        parts.append(part)
    return jnp.concatenate(parts, axis=1).astype(jnp.bfloat16)


def unpacked(ref, line):
    index, place = divmod(line, ref.shape[1] // LANES)
    part = ref[pl.ds(ref.shape[0] - 2 * SUBLANES, 2 * SUBLANES), place * LANES : (place + 1) * LANES]
    part = part.astype(jnp.float32)
    return part[index : index + 1] + part[SUBLANES + index : SUBLANES + index + 1]


def product_kernel(step, chip_count, first, staged, carrier, more, tokens, gain, weight, *refs):
    refs = list(refs)
    keep, send = refs.pop(0), refs.pop(0)
    squares = refs.pop(0) if carrier else None
    count = keep.shape[0] // TILE
    depth, width = tokens.shape[1], 2 * keep.shape[1]
    me = lax.axis_index("tensor")
    core = lax.rem(me, 2)
    chip = lax.rem(lax.div(me, 2) + step, chip_count)
    place = pl.ds(pl.multiple_of(chip * width, width), width)

    weight_copies, row_copies = [], []
    if staged:
        weight_buf, rows_buf, gain_buf, weight_sems, row_sems, gain_sem = refs
        cut = depth // CUTS
        gain_copy = pltpu.make_async_copy(gain, gain_buf, gain_sem)
        for index in range(CUTS):
            some = pl.ds(index * cut, cut)
            weight_copies.append(
                pltpu.make_async_copy(weight.at[some, place], weight_buf.at[some, :], weight_sems.at[index])
            )
        for tile in range(count):
            rows = tokens.at[pl.ds((first + tile) * TILE, TILE), :]
            row_copies.append(
                pltpu.make_async_copy(rows, rows_buf.at[pl.ds(tile * TILE, TILE), :], row_sems.at[tile])
            )
        for copy in [gain_copy] + row_copies[:1] + weight_copies + row_copies[1:]:
            copy.start()
        gain_copy.wait()
        gains = gain_buf[...].reshape(1, depth)
    else:
        gains = gain[...].reshape(1, depth)

    lines = []
    for tile in range(count):
        inside = pl.ds(tile * TILE, TILE)
        if staged:
            row_copies[tile].wait()
            rows = rows_buf[inside, :]
        else:
            rows = tokens[pl.ds((first + tile) * TILE, TILE), :]
        scaled = rows * gains
        if weight_copies:
            product = jnp.zeros((TILE, width), jnp.float32)
            for index, copy in enumerate(weight_copies):
                copy.wait()
                span = slice(index * cut, (index + 1) * cut)
                product += jnp.dot(scaled[:, span], weight_buf[span, :], preferred_element_type=jnp.float32)
            weight_copies = []
        else:
            columns = weight_buf[...] if staged else weight[...]
            product = jnp.dot(scaled, columns, preferred_element_type=jnp.float32)
        left = product[:, : width // 2].astype(jnp.bfloat16)
        right = product[:, width // 2 :].astype(jnp.bfloat16)
        keep[inside, :] = jnp.where(core == 0, left, right)
        send[inside, :] = jnp.where(core == 0, right, left)
        if carrier:
            lines += square_lines(rows)
    for tile in range(count, count + more):
        lines += square_lines(tokens[pl.ds((first + tile) * TILE, TILE), :])
    if carrier:
        for index, line in enumerate(lines):
            squares[index : index + 1, :] = line
        send[pl.ds(keep.shape[0], 2 * SUBLANES), :] = packed(lines, send.shape[1])


def bring_kernel(tokens, gain, weight, rows_out, gain_out, weight_out, sems):
    width = weight_out.shape[1]
    chip = lax.div(lax.axis_index("tensor"), 2)
    place = pl.ds(pl.multiple_of(chip * width, width), width)
    moves = [
        pltpu.make_async_copy(tokens, rows_out, sems.at[0]),
        pltpu.make_async_copy(gain, gain_out, sems.at[1]),
        pltpu.make_async_copy(weight.at[:, place], weight_out, sems.at[2]),
    ]
    for move in moves:
        move.start()
    for move in moves:
        move.wait()


def add_kernel(lines, keep, received, *refs):
    refs = list(refs)
    squares, pair_squares = (refs.pop(0), refs.pop(0)) if lines else (None, None)
    low = 0
    for out in refs:
        size = out.shape[0] - (2 * SUBLANES if lines and out is refs[0] else 0)
        rows = pl.ds(low, size)
        total = keep[rows, :].astype(jnp.float32) + received[rows, :].astype(jnp.float32)
        out[pl.ds(0, size), :] = total.astype(out.dtype)
        low += size
    if lines:
        totals = []
        for line in range(lines):
            totals.append(squares[line : line + 1, :] + unpacked(received, line))
            pair_squares[line : line + 1, :] = totals[-1]
        refs[0][pl.ds(refs[0].shape[0] - 2 * SUBLANES, 2 * SUBLANES), :] = packed(totals, refs[0].shape[1])


def table_kernel(live, span, frequencies, limit, far_cos, far_sin, near_cos, near_sin):
    limit[...] = jnp.full(limit.shape, live[lax.axis_index("serve")] * BLOCK, jnp.int32)
    blocks = far_cos.shape[0]
    start = span[lax.axis_index("serve")] * PAGE
    first = start + BLOCK * lax.broadcasted_iota(jnp.int32, (blocks, HD), 0)
    far = first.astype(jnp.float32) * frequencies[...]
    near = lax.broadcasted_iota(jnp.int32, (BLOCK, HD), 0).astype(jnp.float32) * frequencies[...]
    far_cos[...] = jnp.cos(far)
    far_sin[...] = jnp.sin(far)
    near_cos[...] = jnp.cos(near)
    near_sin[...] = jnp.sin(near)


def finish_kernel(first, at, line_at, count, chip_count, model_dim, *refs):
    keep, received, limit, far_cos, far_sin, near_cos, near_sin = refs[:7]
    pair_squares, carriers = refs[7], refs[8 : 7 + chip_count]
    arrived = refs[7 + chip_count : -4] or carriers
    out, staged, sems = refs[-3:]
    on_diagonal = lax.broadcasted_iota(jnp.int32, (LANES, LANES), 0) == lax.broadcasted_iota(
        jnp.int32, (LANES, LANES), 1
    )
    sign = jnp.where(lax.broadcasted_iota(jnp.int32, (1, HD), 1) < HD // 2, -1.0, 1.0)
    copies = []
    for index in range(count):
        start = (first + at + index) * TILE
        rows, inside = pl.ds(start, TILE), pl.ds(index * TILE, TILE)
        of_chunk = pl.ds((at + index) * TILE, TILE)
        values = keep[of_chunk, :].astype(jnp.float32) + received[of_chunk, :].astype(jnp.float32)
        for part in arrived:
            values += part[inside, :].astype(jnp.float32)
        columns = []
        for line in range((line_at + index) * TILE // LANES, (line_at + index + 1) * TILE // LANES):
            totals = pair_squares[line : line + 1, :]
            for ref in carriers:
                totals += unpacked(ref, line)
            columns.append(jnp.sum(jnp.where(on_diagonal, totals, 0.0), axis=1, keepdims=True))
        scales = 1.0 / jnp.sqrt(jnp.concatenate(columns, axis=0) / model_dim + norm_eps)
        alive = start + lax.broadcasted_iota(jnp.int32, (TILE, LANES), 0) < limit[0:1, :]
        cosines, sines = [], []
        for block in range(start // BLOCK, (start + TILE) // BLOCK):
            block_cos = far_cos[block : block + 1, :]
            block_sin = far_sin[block : block + 1, :]
            cosines.append(block_cos * near_cos[...] - block_sin * near_sin[...])
            sines.append((sign * block_sin) * near_cos[...] + (sign * block_cos) * near_sin[...])
        cosine = jnp.concatenate(cosines, axis=0)
        sine = jnp.concatenate(sines, axis=0)
        for low in range(0, out.shape[1], 2 * HD):
            key = values[:, low : low + HD] * scales
            turned = key * cosine + pltpu.roll(key, HD // 2, 1) * sine
            staged[inside, low : low + HD] = jnp.where(alive, turned, 0.0).astype(out.dtype)
            value = values[:, low + HD : low + 2 * HD] * scales
            staged[inside, low + HD : low + 2 * HD] = jnp.where(alive, value, 0.0).astype(out.dtype)
        copies.append(pltpu.make_async_copy(staged.at[inside, :], out.at[rows, :], sems.at[index]))
        copies[-1].start()
    for copy in copies:
        copy.wait()


def shards(tokens, norm_gain, kv_weight, live_blocks, span_offset):
    tensor_count = lax.axis_size("tensor")
    chip_count = tensor_count // 2
    me = lax.axis_index("tensor")
    slot_rows, depth = tokens.shape
    columns = kv_weight.shape[1] // tensor_count
    tiles = slot_rows // TILE
    model_dim = depth * tensor_count

    swap = [(i, i ^ 1) for i in range(tensor_count)]

    def shift(step):
        return [(i, (i + 2 * step) % tensor_count) for i in range(tensor_count)]

    def product(tokens, gain, kv_weight, step, first, count, staged=False, carrier=True, more=0):
        vmem = pl.BlockSpec(memory_space=pltpu.VMEM)
        rows = count * TILE
        out_shape = [jax.ShapeDtypeStruct((rows, columns), jnp.bfloat16)] * 2
        if carrier:
            out_shape[1] = jax.ShapeDtypeStruct((rows + 2 * SUBLANES, columns), jnp.bfloat16)
            out_shape.append(jax.ShapeDtypeStruct((rows // LANES + more * TILE // LANES, LANES), jnp.float32))
        if staged:
            out_shape.append(jax.ShapeDtypeStruct((depth, 2 * columns), jnp.bfloat16))
        scratch = [
            pltpu.VMEM((rows, depth), jnp.bfloat16),
            pltpu.VMEM((depth,), jnp.bfloat16),
            pltpu.SemaphoreType.DMA((CUTS,)),
            pltpu.SemaphoreType.DMA((count,)),
            pltpu.SemaphoreType.DMA,
        ]
        return pl.pallas_call(
            functools.partial(product_kernel, step, chip_count, first, staged, carrier, more),
            in_specs=[pl.BlockSpec(memory_space=pltpu.HBM) if staged else vmem] * 3,
            out_shape=out_shape,
            out_specs=[vmem] * len(out_shape),
            scratch_shapes=scratch if staged else [],
            compiler_params=FIRST if staged else PARAMS,
            cost_estimate=HEAVY if staged else COST,
        )(tokens, gain, kv_weight)

    def tables(live_blocks, span_offset):
        frequencies = rope_base ** (-(np.arange(HD // 2, dtype=np.float32) * 2.0) / HD)
        frequencies = np.concatenate([frequencies, frequencies])[None, :].astype(np.float32)
        shapes = [(slot_rows // BLOCK, HD)] * 2 + [(BLOCK, HD)] * 2
        made = pl.pallas_call(
            table_kernel,
            in_specs=[pl.BlockSpec(memory_space=pltpu.SMEM)] * 2 + [pl.BlockSpec(memory_space=pltpu.VMEM)],
            out_shape=[jax.ShapeDtypeStruct((8, LANES), jnp.int32)]
            + [jax.ShapeDtypeStruct(shape, jnp.float32) for shape in shapes],
            out_specs=[pl.BlockSpec(memory_space=pltpu.VMEM)] * 5,
            compiler_params=PARAMS,
            cost_estimate=COST,
        )(live_blocks, span_offset, jnp.asarray(frequencies))
        return list(made)

    def finish(first, at, line_at, count, keep, received, table, squares, carriers, arrived, result):
        vmem = pl.BlockSpec(memory_space=pltpu.VMEM)
        operands = [keep, received] + table + [squares] + carriers + (arrived if arrived is not carriers else [])
        aliases = {len(operands): 0}
        if result is None:
            result, aliases = jnp.zeros((1,), jnp.bfloat16), {}
        return pl.pallas_call(
            functools.partial(finish_kernel, first, at, line_at, count, chip_count, model_dim),
            in_specs=[vmem] * len(operands) + [pl.BlockSpec(memory_space=pl.ANY)],
            out_shape=jax.ShapeDtypeStruct((slot_rows, columns), jnp.bfloat16),
            out_specs=pl.BlockSpec(memory_space=pltpu.HBM),
            scratch_shapes=[pltpu.VMEM((count * TILE, columns), jnp.bfloat16), pltpu.SemaphoreType.DMA((count,))],
            input_output_aliases=aliases,
            compiler_params=PARAMS,
            cost_estimate=LATER,
        )(*operands, result)

    others = range(1, chip_count)
    firsts = [sum(CHUNKS[:index]) for index in range(len(CHUNKS))]
    chunk_count = len(CHUNKS)

    chunks = list(zip(firsts, CHUNKS))

    def add_halves(made, counts):
        sizes = [count * TILE for count in counts]
        added = []
        for keep, send, *squares in made:
            lines = squares[0].shape[0] if squares else 0
            out_shape = [jax.ShapeDtypeStruct((size, columns), keep.dtype) for size in sizes]
            if lines:
                out_shape[0] = jax.ShapeDtypeStruct((sizes[0] + 2 * SUBLANES, columns), keep.dtype)
                out_shape.insert(0, jax.ShapeDtypeStruct(squares[0].shape, squares[0].dtype))
            added.append(
                pl.pallas_call(
                    functools.partial(add_kernel, lines),
                    out_shape=out_shape,
                    compiler_params=PARAMS,
                    cost_estimate=COST,
                )(keep, lax.ppermute(send, "tensor", swap), *squares)
            )
        parts = [list(same) for same in zip(*added)]
        return (parts[1:], parts[0][0]) if lines else (parts, None)

    def cross(sums):
        return [lax.ppermute(part, "tensor", shift(step)) for step, part in zip(others, sums)]

    hold = lax.optimization_barrier
    made = [product(tokens, norm_gain, kv_weight, step, *chunks[0], staged=True) for step in others]
    weights = {step: parts[-1] for step, parts in zip(others, made)}
    made = [parts[:-1] for parts in made]
    made, gain, span_offset, live_blocks = hold((made, norm_gain, span_offset, live_blocks))
    table = tables(live_blocks, span_offset)
    sums = add_halves(made, chunks[0][1:])
    sums, gain, table = hold((sums, gain, table))
    tokens, gain, own_weight = pl.pallas_call(
        bring_kernel,
        in_specs=[pl.BlockSpec(memory_space=pltpu.HBM)] * 3,
        out_shape=[
            jax.ShapeDtypeStruct(shape, jnp.bfloat16) for shape in (tokens.shape, gain.shape, (depth, 2 * columns))
        ],
        out_specs=[pl.BlockSpec(memory_space=pltpu.VMEM)] * 3,
        scratch_shapes=[pltpu.SemaphoreType.DMA((3,))],
        compiler_params=BRING,
        cost_estimate=COST,
    )(tokens, gain, kv_weight)

    arrivals = [([cross(part) for part in sums[0]], sums[1])]
    for index in range(1, chunk_count):
        more = sum(CHUNKS[2:]) if index == 1 else 0
        made = [product(tokens, gain, weights[step], step, *chunks[index], carrier=index == 1, more=more) for step in others]
        count = chunks[index][1]
        sums = add_halves(made, (count - 1, 1) if count > 2 else (count,))
        if index == 2:
            sums, late = hold((sums, gain))
        arrivals.append(([cross(part) for part in sums[0]], sums[1]))
    own = [product(tokens, gain, own_weight, 0, *chunk, carrier=False) for chunk in chunks[:-1]]
    own.append(product(tokens, late, own_weight, 0, *chunks[-1], carrier=False))

    result = None
    for (first, count), (keep, send), (arrived, squares) in zip(chunks, own, arrivals):
        received = lax.ppermute(send, "tensor", swap)
        if squares is not None:
            carriers, pair_squares, line_at = arrived[0], squares, 0
        at = 0
        for part in arrived:
            size = part[0].shape[0] // TILE
            result = finish(first, at, line_at, size, keep, received, table, pair_squares, carriers, part, result)
            at += size
            line_at += size
    return result


def solution(mesh):
    in_specs = (
        P(("groups", "serve"), "tensor"),
        P("tensor"),
        P("tensor", None),
        P("groups"),
        P("groups"),
    )
    out_specs = P(("groups", "serve"), "tensor")
    return jax.shard_map(shards, mesh=mesh, in_specs=in_specs, out_specs=out_specs, check_vma=False)
```

```python
import functools

import jax
import jax.numpy as jnp
import numpy as np
from jax import lax
from jax.experimental import pallas as pl
from jax.experimental.pallas import tpu as pltpu
from jax.sharding import PartitionSpec as P

HD = 128
PAGE = 256
BLOCK = 64
LANES = 128
SUBLANES = 8
BF16_MAX = float(jnp.finfo(jnp.bfloat16).max)

rope_base = 500000.0
norm_eps = 1e-05

TILE = 256
CUTS = 4
CHUNKS = (2, 1, 3)

PARAMS = pltpu.CompilerParams(vmem_limit_bytes=16 * 1024 * 1024)
FIRST = pltpu.CompilerParams(vmem_limit_bytes=51200 * 1024)
LATER = pl.CostEstimate(flops=20000000000, bytes_accessed=1, transcendentals=0)
HEAVY = pl.CostEstimate(flops=1000000000000, bytes_accessed=1, transcendentals=0)
BRING = pltpu.CompilerParams(vmem_limit_bytes=47104 * 1024)
COST = pl.CostEstimate(flops=1, bytes_accessed=1, transcendentals=0)


def square_lines(rows):
    lines = []
    for low in range(0, rows.shape[0], LANES):
        total = jnp.zeros((LANES, LANES), jnp.float32)
        for part in range(rows.shape[1] // LANES):
            wide = rows[low : low + LANES, part * LANES : (part + 1) * LANES].astype(jnp.float32)
            total += wide * wide
        lines.append(jnp.sum(jnp.transpose(total), axis=0, keepdims=True))
    return lines


def packed(squares, width):
    per_row = width // LANES
    row = lax.broadcasted_iota(jnp.int32, (2 * SUBLANES, LANES), 0)
    parts = []
    for place in range(per_row):
        part = jnp.zeros((2 * SUBLANES, LANES), jnp.float32)
        for index, line in enumerate(squares[place::per_row]):
            finite = line < jnp.inf
            high = jnp.where(finite, jnp.minimum(line, BF16_MAX), line).astype(jnp.bfloat16).astype(jnp.float32)
            part = jnp.where(row == index, high, part)
            part = jnp.where(row == SUBLANES + index, jnp.where(finite, line - high, 0.0), part)
        parts.append(part)
    return jnp.concatenate(parts, axis=1).astype(jnp.bfloat16)


def unpacked(ref, line):
    index, place = divmod(line, ref.shape[1] // LANES)
    part = ref[pl.ds(ref.shape[0] - 2 * SUBLANES, 2 * SUBLANES), place * LANES : (place + 1) * LANES]
    part = part.astype(jnp.float32)
    return part[index : index + 1] + part[SUBLANES + index : SUBLANES + index + 1]


def product_kernel(step, chip_count, first, staged, carrier, more, tokens, gain, weight, *refs):
    refs = list(refs)
    keep, send = refs.pop(0), refs.pop(0)
    squares = refs.pop(0) if carrier else None
    count = keep.shape[0] // TILE
    depth, width = tokens.shape[1], 2 * keep.shape[1]
    me = lax.axis_index("tensor")
    core = lax.rem(me, 2)
    chip = lax.rem(lax.div(me, 2) + step, chip_count)
    place = pl.ds(pl.multiple_of(chip * width, width), width)

    weight_copies, row_copies = [], []
    if staged:
        weight_buf, rows_buf, gain_buf, weight_sems, row_sems, gain_sem = refs
        cut = depth // CUTS
        gain_copy = pltpu.make_async_copy(gain, gain_buf, gain_sem)
        for index in range(CUTS):
            some = pl.ds(index * cut, cut)
            weight_copies.append(
                pltpu.make_async_copy(weight.at[some, place], weight_buf.at[some, :], weight_sems.at[index])
            )
        for tile in range(count):
            rows = tokens.at[pl.ds((first + tile) * TILE, TILE), :]
            row_copies.append(
                pltpu.make_async_copy(rows, rows_buf.at[pl.ds(tile * TILE, TILE), :], row_sems.at[tile])
            )
        for copy in [gain_copy] + row_copies[:1] + weight_copies + row_copies[1:]:
            copy.start()
        gain_copy.wait()
        gains = gain_buf[...].reshape(1, depth)
    else:
        gains = gain[...].reshape(1, depth)

    lines = []
    for tile in range(count):
        inside = pl.ds(tile * TILE, TILE)
        if staged:
            row_copies[tile].wait()
            rows = rows_buf[inside, :]
        else:
            rows = tokens[pl.ds((first + tile) * TILE, TILE), :]
        scaled = rows * gains
        if weight_copies:
            product = jnp.zeros((TILE, width), jnp.float32)
            for index, copy in enumerate(weight_copies):
                copy.wait()
                span = slice(index * cut, (index + 1) * cut)
                product += jnp.dot(scaled[:, span], weight_buf[span, :], preferred_element_type=jnp.float32)
            weight_copies = []
        else:
            columns = weight_buf[...] if staged else weight[...]
            product = jnp.dot(scaled, columns, preferred_element_type=jnp.float32)
        left = product[:, : width // 2].astype(jnp.bfloat16)
        right = product[:, width // 2 :].astype(jnp.bfloat16)
        keep[inside, :] = jnp.where(core == 0, left, right)
        send[inside, :] = jnp.where(core == 0, right, left)
        if carrier:
            lines += square_lines(rows)
    for tile in range(count, count + more):
        lines += square_lines(tokens[pl.ds((first + tile) * TILE, TILE), :])
    if carrier:
        for index, line in enumerate(lines):
            squares[index : index + 1, :] = line
        send[pl.ds(keep.shape[0], 2 * SUBLANES), :] = packed(lines, send.shape[1])


def bring_kernel(tokens, gain, weight, rows_out, gain_out, weight_out, sems):
    width = weight_out.shape[1]
    chip = lax.div(lax.axis_index("tensor"), 2)
    place = pl.ds(pl.multiple_of(chip * width, width), width)
    moves = [
        pltpu.make_async_copy(tokens, rows_out, sems.at[0]),
        pltpu.make_async_copy(gain, gain_out, sems.at[1]),
        pltpu.make_async_copy(weight.at[:, place], weight_out, sems.at[2]),
    ]
    for move in moves:
        move.start()
    for move in moves:
        move.wait()


def add_kernel(lines, keep, received, *refs):
    refs = list(refs)
    squares, pair_squares = (refs.pop(0), refs.pop(0)) if lines else (None, None)
    low = 0
    for out in refs:
        size = out.shape[0] - (2 * SUBLANES if lines and out is refs[0] else 0)
        rows = pl.ds(low, size)
        total = keep[rows, :].astype(jnp.float32) + received[rows, :].astype(jnp.float32)
        out[pl.ds(0, size), :] = total.astype(out.dtype)
        low += size
    if lines:
        totals = []
        for line in range(lines):
            totals.append(squares[line : line + 1, :] + unpacked(received, line))
            pair_squares[line : line + 1, :] = totals[-1]
        refs[0][pl.ds(refs[0].shape[0] - 2 * SUBLANES, 2 * SUBLANES), :] = packed(totals, refs[0].shape[1])


def table_kernel(live, span, frequencies, limit, far_cos, far_sin, near_cos, near_sin):
    limit[...] = jnp.full(limit.shape, live[lax.axis_index("serve")] * BLOCK, jnp.int32)
    blocks = far_cos.shape[0]
    start = span[lax.axis_index("serve")] * PAGE
    first = start + BLOCK * lax.broadcasted_iota(jnp.int32, (blocks, HD), 0)
    far = first.astype(jnp.float32) * frequencies[...]
    near = lax.broadcasted_iota(jnp.int32, (BLOCK, HD), 0).astype(jnp.float32) * frequencies[...]
    far_cos[...] = jnp.cos(far)
    far_sin[...] = jnp.sin(far)
    near_cos[...] = jnp.cos(near)
    near_sin[...] = jnp.sin(near)


def finish_kernel(first, at, line_at, count, chip_count, model_dim, *refs):
    keep, received, limit, far_cos, far_sin, near_cos, near_sin = refs[:7]
    pair_squares, carriers = refs[7], refs[8 : 7 + chip_count]
    arrived = refs[7 + chip_count : -4] or carriers
    out, staged, sems = refs[-3:]
    on_diagonal = lax.broadcasted_iota(jnp.int32, (LANES, LANES), 0) == lax.broadcasted_iota(
        jnp.int32, (LANES, LANES), 1
    )
    sign = jnp.where(lax.broadcasted_iota(jnp.int32, (1, HD), 1) < HD // 2, -1.0, 1.0)
    copies = []
    for index in range(count):
        start = (first + at + index) * TILE
        rows, inside = pl.ds(start, TILE), pl.ds(index * TILE, TILE)
        of_chunk = pl.ds((at + index) * TILE, TILE)
        values = keep[of_chunk, :].astype(jnp.float32) + received[of_chunk, :].astype(jnp.float32)
        for part in arrived:
            values += part[inside, :].astype(jnp.float32)
        columns = []
        for line in range((line_at + index) * TILE // LANES, (line_at + index + 1) * TILE // LANES):
            totals = pair_squares[line : line + 1, :]
            for ref in carriers:
                totals += unpacked(ref, line)
            columns.append(jnp.sum(jnp.where(on_diagonal, totals, 0.0), axis=1, keepdims=True))
        scales = 1.0 / jnp.sqrt(jnp.concatenate(columns, axis=0) / model_dim + norm_eps)
        alive = start + lax.broadcasted_iota(jnp.int32, (TILE, LANES), 0) < limit[0:1, :]
        cosines, sines = [], []
        for block in range(start // BLOCK, (start + TILE) // BLOCK):
            block_cos = far_cos[block : block + 1, :]
            block_sin = far_sin[block : block + 1, :]
            cosines.append(block_cos * near_cos[...] - block_sin * near_sin[...])
            sines.append((sign * block_sin) * near_cos[...] + (sign * block_cos) * near_sin[...])
        cosine = jnp.concatenate(cosines, axis=0)
        sine = jnp.concatenate(sines, axis=0)
        for low in range(0, out.shape[1], 2 * HD):
            key = values[:, low : low + HD] * scales
            turned = key * cosine + pltpu.roll(key, HD // 2, 1) * sine
            staged[inside, low : low + HD] = jnp.where(alive, turned, 0.0).astype(out.dtype)
            value = values[:, low + HD : low + 2 * HD] * scales
            staged[inside, low + HD : low + 2 * HD] = jnp.where(alive, value, 0.0).astype(out.dtype)
            head = pl.ds(low, 2 * HD)
            copies.append(pltpu.make_async_copy(staged.at[inside, head], out.at[rows, head], sems.at[len(copies)]))
            copies[-1].start()
    for copy in copies:
        copy.wait()


def shards(tokens, norm_gain, kv_weight, live_blocks, span_offset):
    tensor_count = lax.axis_size("tensor")
    chip_count = tensor_count // 2
    me = lax.axis_index("tensor")
    slot_rows, depth = tokens.shape
    columns = kv_weight.shape[1] // tensor_count
    tiles = slot_rows // TILE
    model_dim = depth * tensor_count

    swap = [(i, i ^ 1) for i in range(tensor_count)]

    def shift(step):
        return [(i, (i + 2 * step) % tensor_count) for i in range(tensor_count)]

    def product(tokens, gain, kv_weight, step, first, count, staged=False, carrier=True, more=0):
        vmem = pl.BlockSpec(memory_space=pltpu.VMEM)
        rows = count * TILE
        out_shape = [jax.ShapeDtypeStruct((rows, columns), jnp.bfloat16)] * 2
        if carrier:
            out_shape[1] = jax.ShapeDtypeStruct((rows + 2 * SUBLANES, columns), jnp.bfloat16)
            out_shape.append(jax.ShapeDtypeStruct((rows // LANES + more * TILE // LANES, LANES), jnp.float32))
        if staged:
            out_shape.append(jax.ShapeDtypeStruct((depth, 2 * columns), jnp.bfloat16))
        scratch = [
            pltpu.VMEM((rows, depth), jnp.bfloat16),
            pltpu.VMEM((depth,), jnp.bfloat16),
            pltpu.SemaphoreType.DMA((CUTS,)),
            pltpu.SemaphoreType.DMA((count,)),
            pltpu.SemaphoreType.DMA,
        ]
        return pl.pallas_call(
            functools.partial(product_kernel, step, chip_count, first, staged, carrier, more),
            in_specs=[pl.BlockSpec(memory_space=pltpu.HBM) if staged else vmem] * 3,
            out_shape=out_shape,
            out_specs=[vmem] * len(out_shape),
            scratch_shapes=scratch if staged else [],
            compiler_params=FIRST if staged else PARAMS,
            cost_estimate=HEAVY if staged else COST,
        )(tokens, gain, kv_weight)

    def tables(live_blocks, span_offset):
        frequencies = rope_base ** (-(np.arange(HD // 2, dtype=np.float32) * 2.0) / HD)
        frequencies = np.concatenate([frequencies, frequencies])[None, :].astype(np.float32)
        shapes = [(slot_rows // BLOCK, HD)] * 2 + [(BLOCK, HD)] * 2
        made = pl.pallas_call(
            table_kernel,
            in_specs=[pl.BlockSpec(memory_space=pltpu.SMEM)] * 2 + [pl.BlockSpec(memory_space=pltpu.VMEM)],
            out_shape=[jax.ShapeDtypeStruct((8, LANES), jnp.int32)]
            + [jax.ShapeDtypeStruct(shape, jnp.float32) for shape in shapes],
            out_specs=[pl.BlockSpec(memory_space=pltpu.VMEM)] * 5,
            compiler_params=PARAMS,
            cost_estimate=COST,
        )(live_blocks, span_offset, jnp.asarray(frequencies))
        return list(made)

    def finish(first, at, line_at, count, keep, received, table, squares, carriers, arrived, result):
        vmem = pl.BlockSpec(memory_space=pltpu.VMEM)
        operands = [keep, received] + table + [squares] + carriers + (arrived if arrived is not carriers else [])
        aliases = {len(operands): 0}
        if result is None:
            result, aliases = jnp.zeros((1,), jnp.bfloat16), {}
        return pl.pallas_call(
            functools.partial(finish_kernel, first, at, line_at, count, chip_count, model_dim),
            in_specs=[vmem] * len(operands) + [pl.BlockSpec(memory_space=pl.ANY)],
            out_shape=jax.ShapeDtypeStruct((slot_rows, columns), jnp.bfloat16),
            out_specs=pl.BlockSpec(memory_space=pltpu.HBM),
            scratch_shapes=[pltpu.VMEM((count * TILE, columns), jnp.bfloat16), pltpu.SemaphoreType.DMA((count * columns // (2 * HD),))],
            input_output_aliases=aliases,
            compiler_params=PARAMS,
            cost_estimate=LATER,
        )(*operands, result)

    others = range(1, chip_count)
    firsts = [sum(CHUNKS[:index]) for index in range(len(CHUNKS))]
    chunk_count = len(CHUNKS)

    chunks = list(zip(firsts, CHUNKS))

    def add_halves(made, counts):
        sizes = [count * TILE for count in counts]
        added = []
        for keep, send, *squares in made:
            lines = squares[0].shape[0] if squares else 0
            out_shape = [jax.ShapeDtypeStruct((size, columns), keep.dtype) for size in sizes]
            if lines:
                out_shape[0] = jax.ShapeDtypeStruct((sizes[0] + 2 * SUBLANES, columns), keep.dtype)
                out_shape.insert(0, jax.ShapeDtypeStruct(squares[0].shape, squares[0].dtype))
            added.append(
                pl.pallas_call(
                    functools.partial(add_kernel, lines),
                    out_shape=out_shape,
                    compiler_params=PARAMS,
                    cost_estimate=COST,
                )(keep, lax.ppermute(send, "tensor", swap), *squares)
            )
        parts = [list(same) for same in zip(*added)]
        return (parts[1:], parts[0][0]) if lines else (parts, None)

    def cross(sums):
        return [lax.ppermute(part, "tensor", shift(step)) for step, part in zip(others, sums)]

    hold = lax.optimization_barrier
    made = [product(tokens, norm_gain, kv_weight, step, *chunks[0], staged=True) for step in others]
    weights = {step: parts[-1] for step, parts in zip(others, made)}
    made = [parts[:-1] for parts in made]
    made, gain, span_offset, live_blocks = hold((made, norm_gain, span_offset, live_blocks))
    table = tables(live_blocks, span_offset)
    sums = add_halves(made, chunks[0][1:])
    sums, gain, table = hold((sums, gain, table))
    tokens, gain, own_weight = pl.pallas_call(
        bring_kernel,
        in_specs=[pl.BlockSpec(memory_space=pltpu.HBM)] * 3,
        out_shape=[
            jax.ShapeDtypeStruct(shape, jnp.bfloat16) for shape in (tokens.shape, gain.shape, (depth, 2 * columns))
        ],
        out_specs=[pl.BlockSpec(memory_space=pltpu.VMEM)] * 3,
        scratch_shapes=[pltpu.SemaphoreType.DMA((3,))],
        compiler_params=BRING,
        cost_estimate=COST,
    )(tokens, gain, kv_weight)

    arrivals = [([cross(part) for part in sums[0]], sums[1])]
    for index in range(1, chunk_count):
        more = sum(CHUNKS[2:]) if index == 1 else 0
        made = [product(tokens, gain, weights[step], step, *chunks[index], carrier=index == 1, more=more) for step in others]
        count = chunks[index][1]
        sums = add_halves(made, (count - 1, 1) if count > 2 else (count,))
        if index == 2:
            sums, late = hold((sums, gain))
        arrivals.append(([cross(part) for part in sums[0]], sums[1]))
    own = [product(tokens, gain, own_weight, 0, *chunk, carrier=False) for chunk in chunks[:-1]]
    own.append(product(tokens, late, own_weight, 0, *chunks[-1], carrier=False))

    result = None
    for (first, count), (keep, send), (arrived, squares) in zip(chunks, own, arrivals):
        received = lax.ppermute(send, "tensor", swap)
        if squares is not None:
            carriers, pair_squares, line_at = arrived[0], squares, 0
        at = 0
        for part in arrived:
            size = part[0].shape[0] // TILE
            result = finish(first, at, line_at, size, keep, received, table, pair_squares, carriers, part, result)
            at += size
            line_at += size
    return result


def solution(mesh):
    in_specs = (
        P(("groups", "serve"), "tensor"),
        P("tensor"),
        P("tensor", None),
        P("groups"),
        P("groups"),
    )
    out_specs = P(("groups", "serve"), "tensor")
    return jax.shard_map(shards, mesh=mesh, in_specs=in_specs, out_specs=out_specs, check_vma=False)
```
